256 devices in a mesh: dp: 8 (over z_lo, x), seq: 32 (over y, z_hi, core).
Axes of the slice: x: 4, y: 4, z: 8 (z_hi: 4, z_lo: 2; z = z_hi * 2 + z_lo), core: 2. Of those that a mesh axis runs over, the one named last changes fastest.
Arguments:
- q_coarse: bfloat16 [8, 256, 1024], P('dp'), may hold values from -6 to 6
- k_coarse: bfloat16 [8, 256, 1024], P('dp'), may hold values from -6 to 6
- v_coarse: bfloat16 [8, 256, 1024], P('dp'), may hold values from -18 to 18
- cot_coarse: bfloat16 [8, 256, 1024], P('dp'), may hold values from -6 to 6
- coarse_ids: int32 [8, 256], P('dp'), may hold values from 0 to 5, never falling along the last dimension, each value on 1 to 64 neighbouring positions
- q_fine: bfloat16 [8, 3072, 1024], P('dp', 'seq'), may hold values from -6 to 6
- k_fine: bfloat16 [8, 3072, 1024], P('dp', 'seq'), may hold values from -6 to 6
- v_fine: bfloat16 [8, 3072, 1024], P('dp', 'seq'), may hold values from -18 to 18
- cot_fine: bfloat16 [8, 3072, 1024], P('dp', 'seq'), may hold values from -6 to 6
- fine_ids: int32 [8, 3072], P('dp', 'seq'), may hold values from 0 to 2, never falling along the last dimension, each value on 1 to 1536 neighbouring positions
- log_scale: float32 [8], replicated, may hold values from 3 to 3.7
Outputs:
- out_coarse: bfloat16 [8, 256, 1024], P('dp')
- dq_coarse: bfloat16 [8, 256, 1024], P('dp')
- dk_coarse: bfloat16 [8, 256, 1024], P('dp')
- dv_coarse: bfloat16 [8, 256, 1024], P('dp')
- out_fine: bfloat16 [8, 3072, 1024], P('dp', 'seq')
- dq_fine: bfloat16 [8, 3072, 1024], P('dp', 'seq')
- dk_fine: bfloat16 [8, 3072, 1024], P('dp', 'seq')
- dv_fine: bfloat16 [8, 3072, 1024], P('dp', 'seq')
- grad_scale: float32 [8], replicated
The draws below stay inside these ranges and needn't reach their ends.
Inputs may be any that keep to these rules, and one draw needn't show every extreme that they name: `coarse_ids`: along each image the coarse scale index never falls; every index is used; the largest scale holds exactly 64 tokens (more than one scale may) and no scale holds more. `fine_ids`: along each image the fine scale index never falls; every index is used; the largest scale holds exactly 1536 tokens (more than one scale may) and no scale holds more.
All inputs are finite; a program needn't handle non-finite values.
Results may differ from the reference program's by a relative error of at most 0.022.
Values may be sent and summed in bfloat16 or wider, within the bound.
No kernel may reach another device: no remote copies, remote signals or barrier semaphores. Data moves between devices by JAX's collectives and lax.ppermute only.
A program may use at most 128 MiB of HBM per device.

```python
import math
import jax
import jax.numpy as jnp
import numpy as np
from jax import lax

H = 8
HD = 128
HW = 1024
C_TOK = 256
CSC = 6
FSC = 3
F_TOK = 3072
IMAGES = 8


def level_of(rng, shape, split, smallest, top_value):
    loudness, own = 1.0, jax.random.fold_in(rng, 6)
    for dim, blocks in split:
        steps = jnp.exp(jax.random.uniform(jax.random.fold_in(own, dim), (blocks,), jnp.float32, smallest / len(split), top_value / len(split)))
        loudness = loudness * jnp.repeat(steps, shape[dim] // blocks).reshape([-1 if axis == dim else 1 for axis in range(len(shape))])
    return loudness


def split_up(number_of, total, bound, slope):
    loads = [(1 << 20) // math.isqrt(grade ** slope) + 1 for grade in range(2, number_of + 1)]
    spare, counts = total - bound - (number_of - 1), [1] * (number_of - 1)
    while spare > 0:
        free = [i for i in range(number_of - 1) if counts[i] < bound]
        mass, budget = sum([loads[i] for i in free]), spare
        for i in free:
            more = min(bound - counts[i], max(1, budget * loads[i] // mass), spare)
            counts[i] = counts[i] + more
            spare = spare - more
    return np.array([bound] + counts)


def ragged(key, number_of, total, reach, lean):
    if number_of == 2:
        one = jax.random.randint(key, (), max(1, total - reach), min(reach, total - 1) + 1)
        return jnp.stack([one, total - one])
    lengths = jnp.asarray(split_up(number_of, total, reach, lean), jnp.int32)
    couples = (number_of - 1) // 2
    giver, sink = lengths[1:1 + 2 * couples:2], lengths[2:2 + 2 * couples:2]
    room = jnp.minimum(giver - 1, reach - sink)
    passed = jax.random.randint(jax.random.fold_in(key, 1), (couples,), 0, 1 << 20) % (room + 1)
    lengths = lengths.at[1:1 + 2 * couples:2].set(giver - passed).at[2:2 + 2 * couples:2].set(sink + passed)
    return lengths[jax.random.permutation(jax.random.fold_in(key, 2), number_of)]


def gaussian(rng, dims, spread, bound, cuts=(), kind=jnp.bfloat16):
    factor_of = level_of(rng, dims, cuts, -0.22, 0.18) if cuts else 1.0
    array = jax.random.normal(rng, dims, jnp.float32) * spread * factor_of
    return jnp.minimum(jnp.maximum(array, -bound), bound).astype(kind)


def setup_inputs(seed: int = 0) -> dict:
    splits = jax.random.split(jax.random.key(seed), 12)
    q_coarse = gaussian(splits[0], (IMAGES, C_TOK, HW), 1.0, 6.0, ((0, 8),))
    k_coarse = gaussian(splits[1], (IMAGES, C_TOK, HW), 1.0, 6.0, ((0, 8),))
    v_coarse = gaussian(splits[2], (IMAGES, C_TOK, HW), 3.0, 18.0, ((0, 8),))
    cot_coarse = gaussian(splits[3], (IMAGES, C_TOK, HW), 1.0, 6.0, ((0, 8),))
    coarse_ids = jax.vmap(lambda own: jnp.searchsorted(jnp.cumsum(ragged(own, CSC, C_TOK, C_TOK // 4, 0)), jnp.arange(C_TOK), side="right"))(jax.random.split(splits[4], IMAGES)).reshape((IMAGES, C_TOK)).astype(jnp.int32)
    q_fine = gaussian(splits[5], (IMAGES, F_TOK, HW), 1.0, 6.0, ((0, 8), (1, 32)))
    k_fine = gaussian(splits[6], (IMAGES, F_TOK, HW), 1.0, 6.0, ((0, 8), (1, 32)))
    v_fine = gaussian(splits[7], (IMAGES, F_TOK, HW), 3.0, 18.0, ((0, 8), (1, 32)))
    cot_fine = gaussian(splits[8], (IMAGES, F_TOK, HW), 1.0, 6.0, ((0, 8), (1, 32)))
    fine_ids = jax.vmap(lambda own: jnp.searchsorted(jnp.cumsum(ragged(own, FSC, F_TOK, F_TOK // 2, 0)), jnp.arange(F_TOK), side="right"))(jax.random.split(splits[9], IMAGES)).reshape((IMAGES, F_TOK)).astype(jnp.int32)
    log_scale = jnp.clip(jax.random.uniform(splits[10], (H,), jnp.float32, 3.0, 3.7), 3.0, 3.7)
    return {"q_coarse": q_coarse, "k_coarse": k_coarse, "v_coarse": v_coarse, "cot_coarse": cot_coarse, "coarse_ids": coarse_ids, "q_fine": q_fine, "k_fine": k_fine, "v_fine": v_fine, "cot_fine": cot_fine, "fine_ids": fine_ids, "log_scale": log_scale}


norm_eps = 1e-06

def unit_heads(matrix):
    by_head = matrix.astype(jnp.float32).reshape(matrix.shape[0], H, HD)
    inv_norm = lax.rsqrt(lax.optimization_barrier(jnp.sum(by_head * by_head, axis=-1, keepdims=True)) + norm_eps)
    return (by_head * inv_norm, inv_norm)

def unit_back(unit_dir, inv_norm, grad_unit):
    along_dir = lax.optimization_barrier(jnp.sum(unit_dir * grad_unit, axis=-1, keepdims=True))
    return (inv_norm * (grad_unit - unit_dir * along_dir)).reshape(unit_dir.shape[0], H * HD)

def one_head(sharpness, query_unit, key_unit, values, cotangent, level):
    score = sharpness * jnp.dot(query_unit, key_unit.T, preferred_element_type=jnp.float32)
    visible = level[None, :] <= level[:, None]
    prob = jnp.where(visible, jnp.exp(score - sharpness), 0.0)
    dprob = jnp.dot(cotangent, values.T, preferred_element_type=jnp.float32)
    weighted = prob * dprob
    denominator = lax.optimization_barrier(jnp.sum(prob, axis=1))
    mean_dprob = lax.optimization_barrier(jnp.sum(weighted, axis=1)) / denominator
    prob_low = prob.astype(jnp.bfloat16)
    numerator = jnp.dot(prob_low, values, preferred_element_type=jnp.float32)
    along_keys = jnp.dot(prob_low, key_unit, preferred_element_type=jnp.float32)
    weighted_keys = jnp.dot(weighted.astype(jnp.bfloat16), key_unit, preferred_element_type=jnp.float32)
    outputs = numerator / denominator[:, None]
    grad_query = sharpness * (weighted_keys - mean_dprob[:, None] * along_keys) / denominator[:, None]
    norm_prob = prob / denominator[:, None]
    dscore = norm_prob * (dprob - mean_dprob[:, None])
    grad_key = sharpness * jnp.dot(dscore.astype(jnp.bfloat16).T, query_unit, preferred_element_type=jnp.float32)
    grad_value = jnp.dot(norm_prob.astype(jnp.bfloat16).T, cotangent, preferred_element_type=jnp.float32)
    scale_term = jnp.sum(dscore * score)
    return (outputs, grad_query, grad_key, grad_value, scale_term)

def one_image(sharpness, query_rows, key_rows, value_rows, cot_rows, level):
    count = query_rows.shape[0]
    query_dir, query_inv = unit_heads(query_rows)
    key_dir, key_inv = unit_heads(key_rows)
    query_unit = jnp.swapaxes(query_dir.astype(jnp.bfloat16), 0, 1)
    key_unit = jnp.swapaxes(key_dir.astype(jnp.bfloat16), 0, 1)
    values = jnp.swapaxes(value_rows.reshape(count, H, HD), 0, 1)
    cotangent = jnp.swapaxes(cot_rows.reshape(count, H, HD), 0, 1)

    def per_head(inputs):
        head_sharp, head_query, head_key, head_value, head_cot = inputs
        return one_head(head_sharp, head_query, head_key, head_value, head_cot, level)
    outputs, grad_query, grad_key, grad_value, scale_terms = lax.map(per_head, (sharpness, query_unit, key_unit, values, cotangent))
    out_rows = jnp.swapaxes(outputs, 0, 1).reshape(count, H * HD).astype(jnp.bfloat16)
    dq_rows = unit_back(query_dir, query_inv, jnp.swapaxes(grad_query, 0, 1)).astype(jnp.bfloat16)
    dk_rows = unit_back(key_dir, key_inv, jnp.swapaxes(grad_key, 0, 1)).astype(jnp.bfloat16)
    dv_rows = jnp.swapaxes(grad_value, 0, 1).reshape(count, H * HD).astype(jnp.bfloat16)
    return (out_rows, dq_rows, dk_rows, dv_rows, scale_terms)

def reference(q_coarse, k_coarse, v_coarse, cot_coarse, coarse_ids, q_fine, k_fine, v_fine, cot_fine, fine_ids, log_scale):
    sharpness = jnp.exp(log_scale)

    def per_image(inputs):
        query_c, key_c, value_c, cot_c, ids_c, query_f, key_f, value_f, cot_f, ids_f = inputs
        level = jnp.concatenate([ids_c.astype(jnp.int32), (ids_f + C_TOK).astype(jnp.int32)])
        return one_image(sharpness, jnp.concatenate([query_c, query_f]), jnp.concatenate([key_c, key_f]), jnp.concatenate([value_c, value_f]), jnp.concatenate([cot_c, cot_f]), level)
    out_rows, dq_rows, dk_rows, dv_rows, scale_terms = lax.map(per_image, (q_coarse, k_coarse, v_coarse, cot_coarse, coarse_ids, q_fine, k_fine, v_fine, cot_fine, fine_ids))
    grad_scale = lax.optimization_barrier(jnp.sum(scale_terms, axis=0)) / jnp.sqrt(jnp.float32(IMAGES * (C_TOK + F_TOK)))
    return (out_rows[:, :C_TOK], dq_rows[:, :C_TOK], dk_rows[:, :C_TOK], dv_rows[:, :C_TOK], out_rows[:, C_TOK:], dq_rows[:, C_TOK:], dk_rows[:, C_TOK:], dv_rows[:, C_TOK:], grad_scale)
```

```python
import math

import jax
import jax.numpy as jnp
from jax import lax
from jax.experimental import pallas as pl
from jax.experimental.pallas import tpu as pltpu
from jax.sharding import PartitionSpec as P

norm_eps = 1e-06
log2_e = 1.4426950408889634
k_tile = 256
note_rows = 16

planes = 4


def dot_nt(left, right):
    return lax.dot_general(
        left, right, (((1,), (1,)), ((), ())), preferred_element_type=jnp.float32
    )


def dot_nn(left, right):
    return jnp.dot(left, right, preferred_element_type=jnp.float32)


def unit_rows(rows):
    wide = rows.astype(jnp.float32)
    inv_norm = lax.rsqrt(jnp.sum(wide * wide, axis=-1, keepdims=True) + norm_eps)
    return wide * inv_norm, inv_norm


def project(key_rows, grad):
    key_dir, key_inv = unit_rows(key_rows)
    along = jnp.sum(key_dir * grad, axis=-1, keepdims=True)
    return key_inv * (grad - key_dir * along)


def fold_rows(terms):
    rows, width = terms.shape
    return jnp.sum(terms.reshape(rows // 8, 8, width), axis=0)


def seq_place():
    here = lax.axis_index("seq")
    plane = lax.shift_right_logical(here, 3)
    head = lax.bitwise_and(here, 7)
    group = lax.bitwise_and(plane - lax.shift_right_logical(head, 1), 3)
    return plane, head, group


def params(mebibytes):
    return pltpu.CompilerParams(vmem_limit_bytes=mebibytes * 1024 * 1024)


def pack_kernel(ids_ref, k_ref, v_ref, q_ref, cot_ref, all_ref):
    heads, _, width = all_ref.shape
    rows = k_ref.shape[0]
    ids = ids_ref[...]
    row = lax.broadcasted_iota(jnp.int32, (note_rows, width), 0)
    lane = lax.broadcasted_iota(jnp.int32, (note_rows, width), 1)
    note = jnp.zeros((note_rows, width), jnp.float32)
    for level in range(2):
        count = jnp.sum(jnp.where(ids <= level, 1.0, 0.0), axis=-1, keepdims=True)
        note = jnp.where((row == level) & (lane == 0), count, note)
    note = note.astype(jnp.bfloat16)
    first_query = 2 * rows + note_rows
    for head in range(heads):
        lanes = slice(head * width, (head + 1) * width)
        all_ref[head, 0:rows] = k_ref[:, lanes]
        all_ref[head, rows : 2 * rows] = v_ref[:, lanes]
        all_ref[head, 2 * rows : first_query] = note
        all_ref[head, first_query : first_query + rows] = q_ref[:, lanes]
        all_ref[head, first_query + rows :] = cot_ref[:, lanes]


def run_pack(heads, ids, keys, values, queries, cots):
    rows, features = keys.shape
    shape = (heads, 4 * rows + note_rows, features // heads)
    return pl.pallas_call(
        pack_kernel,
        out_shape=jax.ShapeDtypeStruct(shape, jnp.bfloat16),
        compiler_params=params(56),
        name="pack_heads",
    )(ids, keys, values, queries, cots)


def fine_kernel(
    log_ref,
    own_ref,
    kv1_ref,
    kv2_ref,
    kv3_ref,
    kc_ref,
    vc_ref,
    coarse_scale_ref,
    od_ref,
    dkv0_ref,
    dkv1_ref,
    dkv2_ref,
    dkv3_ref,
    scale_ref,
    key_scr,
    val_scr,
    query_scr,
    cot_scr,
    limit_scr,
    sum_scr,
    mean_scr,
    grad_scr,
    query_turn,
    cot_turn,
    prob_scr,
    turn_scr,
):
    plane, head, group = seq_place()
    members, _, width = own_ref.shape
    rows = od_ref.shape[1] // 2
    coarse = kc_ref.shape[0]
    queries = members * rows
    fine = planes * queries
    total = coarse + fine
    block = 2 * rows
    blocks = members // 2
    first_query = 2 * rows + note_rows
    half = queries // 2

    def block_start(owner, part):
        return (lax.bitwise_and(owner + part, 3) * members + 2 * part) * rows

    notes = jnp.zeros((note_rows, width), jnp.float32)
    for step, ref in enumerate((own_ref, kv1_ref, kv2_ref, kv3_ref)):
        owner = lax.bitwise_and(group - step, 3)
        notes = notes + jnp.sum(ref[:, 2 * rows : first_query].astype(jnp.float32), axis=0)
        for part in range(blocks):
            pick = slice(2 * part, 2 * part + 2)
            spot = pl.ds(pl.multiple_of(coarse + block_start(owner, part), 64), block)
            key_scr[spot, :] = unit_rows(ref[pick, 0:rows].reshape(block, width))[0].astype(
                jnp.bfloat16
            )
            val_scr[spot, 0:width] = ref[pick, rows : 2 * rows].reshape(block, width)
    val_scr[:, width:] = jnp.ones((total, width), jnp.bfloat16)
    key_scr[0:coarse, :] = kc_ref[...]
    val_scr[0:coarse, 0:width] = vc_ref[...]
    ends = [jnp.sum(notes[level : level + 1]).astype(jnp.int32) for level in range(2)]

    def limit_of(place):
        return jnp.where(place < ends[0], ends[0], jnp.where(place < ends[1], ends[1], fine))

    def rows_of(part):
        spot = lax.bitwise_and(group + part, 3) * block
        return pl.ds(pl.multiple_of(spot, 64), block)

    def own_query(part):
        pick = own_ref[2 * part : 2 * part + 2, first_query : first_query + rows]
        return unit_rows(pick.reshape(block, width))

    for part in range(blocks):
        pick = slice(2 * part, 2 * part + 2)
        spot = rows_of(part)
        query_scr[spot, :] = own_query(part)[0].astype(jnp.bfloat16)
        cot_scr[spot, :] = own_ref[pick, first_query + rows :].reshape(block, width)
        place = block_start(group, part) + lax.broadcasted_iota(jnp.int32, (block, width), 0)
        limit_scr[spot, :] = limit_of(place) + coarse

    sharp = jnp.exp(jnp.full((1, width), log_ref[head], jnp.float32))[:, 0:1]
    slope = sharp * log2_e
    sum_scr[...] = jnp.zeros_like(sum_scr)
    grad_scr[...] = jnp.zeros_like(grad_scr)

    def twice(column):
        return jnp.concatenate([column, column], axis=1)

    def keys_of(chunk):
        return pl.ds(pl.multiple_of(chunk * k_tile, k_tile), k_tile)

    def probs(chunk, first):
        cosine = dot_nt(query_scr[first:, :], key_scr[keys_of(chunk), :])
        prob = jnp.exp2(cosine * slope - slope)
        place = chunk * k_tile + lax.broadcasted_iota(jnp.int32, (1, k_tile), 1)
        prob = jnp.where(place < twice(limit_scr[first:, :]), prob, 0.0).astype(jnp.bfloat16)
        prob_scr[chunk, first:, :] = prob
        sum_scr[first:, :] += dot_nn(prob, val_scr[keys_of(chunk), :])

    def grads(chunk, first):
        prob = prob_scr[chunk, first:, :]
        dprob = dot_nt(cot_scr[first:, :], val_scr[keys_of(chunk), 0:width])
        dscore = prob.astype(jnp.float32) * (dprob - twice(mean_scr[first:, :]))
        dscore = dscore.astype(jnp.bfloat16)
        grad_scr[first:, :] += dot_nn(dscore, key_scr[keys_of(chunk), :])
        dk = dot_nn(query_turn[:, first:], dscore)
        dv = dot_nn(cot_turn[:, first:], prob)
        turn_scr[keys_of(chunk), 0:width] = jnp.transpose(dk).astype(jnp.bfloat16)
        turn_scr[keys_of(chunk), width:] = jnp.transpose(dv).astype(jnp.bfloat16)

    def all_chunks(work):
        last = (members + 2 * lax.bitwise_and(1 - group, 3)) * rows + block - 1
        shared = (limit_of(last) + coarse + k_tile - 1) // k_tile

        def both(chunk, carry):
            work(chunk, 0)
            return carry

        def upper(chunk, carry):
            work(chunk, half)
            return carry

        lax.fori_loop(0, shared, both, 0)
        lax.fori_loop(shared, total // k_tile, upper, 0)

    all_chunks(probs)

    r_den = 1.0 / sum_scr[:, width:]
    outs = sum_scr[:, :width] * r_den
    cot = cot_scr[...].astype(jnp.float32)
    mean_scr[...] = jnp.broadcast_to(
        jnp.sum(outs * cot, axis=-1, keepdims=True), mean_scr.shape
    )
    sum_scr[:, :width] = outs
    query_turn[...] = jnp.transpose(
        query_scr[...].astype(jnp.float32) * (r_den * sharp)
    ).astype(jnp.bfloat16)
    cot_turn[...] = jnp.transpose(cot * r_den).astype(jnp.bfloat16)

    all_chunks(grads)

    leading = jnp.where(plane == 0, 1.0, 0.0)
    scale = coarse_scale_ref[pl.ds(pl.multiple_of(head * 8, 8), 8), :] * leading
    for part in range(blocks):
        pick = slice(2 * part, 2 * part + 2)
        spot = rows_of(part)
        q_dir, q_inv = own_query(part)
        grad = grad_scr[spot, :] * (sharp / sum_scr[spot, width:])
        along = jnp.sum(q_dir * grad, axis=-1, keepdims=True)
        scale = scale + fold_rows(query_scr[spot, :].astype(jnp.float32) * grad)
        dq = (q_inv * (grad - q_dir * along)).astype(jnp.bfloat16)
        od_ref[pick, 0:rows] = sum_scr[spot, :width].astype(jnp.bfloat16).reshape(2, rows, width)
        od_ref[pick, rows:] = dq.reshape(2, rows, width)
    scale_ref[...] = scale

    small = coarse // planes
    for step, ref in enumerate((dkv0_ref, dkv1_ref, dkv2_ref, dkv3_ref)):
        owner = lax.bitwise_and(group + step, 3)
        target = lax.bitwise_and(plane + step, 3)
        for part in range(blocks):
            spot = pl.ds(pl.multiple_of(coarse + block_start(owner, part), 64), block)
            ref[part * block : (part + 1) * block, :] = turn_scr[spot, :]
        ref[queries:, :] = turn_scr[pl.ds(pl.multiple_of(target * small, 64), small), :]


def run_fine(log_scale, own_rows, kv_parts, key_coarse, val_coarse, coarse_scale):
    members, tall, width = own_rows.shape
    rows = (tall - note_rows) // 4
    coarse = key_coarse.shape[0]
    queries = members * rows
    total = coarse + planes * queries
    vmem = pl.BlockSpec(memory_space=pltpu.VMEM)
    low = jnp.bfloat16
    wide = jnp.float32
    return pl.pallas_call(
        fine_kernel,
        out_shape=(jax.ShapeDtypeStruct((members, 2 * rows, width), low),)
        + (jax.ShapeDtypeStruct((total // planes, 2 * width), low),) * 4
        + (jax.ShapeDtypeStruct((8, width), wide),),
        in_specs=[pl.BlockSpec(memory_space=pltpu.SMEM)] + [vmem] * 7,
        out_specs=(vmem,) * 6,
        scratch_shapes=[
            pltpu.VMEM((total, width), low),
            pltpu.VMEM((total, 2 * width), low),
            pltpu.VMEM((queries, width), low),
            pltpu.VMEM((queries, width), low),
            pltpu.VMEM((queries, width), jnp.int32),
            pltpu.VMEM((queries, 2 * width), wide),
            pltpu.VMEM((queries, width), wide),
            pltpu.VMEM((queries, width), wide),
            pltpu.VMEM((width, queries), low),
            pltpu.VMEM((width, queries), low),
            pltpu.VMEM((total // k_tile, queries, k_tile), low),
            pltpu.VMEM((total, 2 * width), low),
        ],
        compiler_params=params(28),
        cost_estimate=pl.CostEstimate(
            flops=12 * queries * total * width,
            bytes_accessed=8 * total * width,
            transcendentals=queries * total,
        ),
        name="fine_attention",
    )(log_scale, own_rows, *kv_parts, key_coarse, val_coarse, coarse_scale)


def coarse_kernel(
    log_ref,
    row_level_ref,
    col_level_ref,
    q_ref,
    k_ref,
    v_ref,
    cot_ref,
    out_ref,
    dq_ref,
    dk_ref,
    dv_ref,
    scale_ref,
    key_low_ref,
    value_ref,
):
    _, own, _ = seq_place()
    count, features = q_ref.shape
    heads = log_ref.shape[0]
    width = features // heads
    visible = col_level_ref[...] <= row_level_ref[...]
    for head in range(heads):
        lanes = slice(head * width, (head + 1) * width)
        sharp = jnp.exp(jnp.full((1, width), log_ref[head], jnp.float32))[:, 0:1]
        slope = sharp * log2_e
        q_dir, q_inv = unit_rows(q_ref[:, lanes])
        q_low = q_dir.astype(jnp.bfloat16)
        key_low = unit_rows(k_ref[:, lanes])[0].astype(jnp.bfloat16)
        values = v_ref[:, lanes]
        cot = cot_ref[:, lanes]
        prob = jnp.exp2(dot_nt(q_low, key_low) * slope - slope)
        prob = jnp.where(visible, prob, 0.0)
        r_den = 1.0 / jnp.sum(prob, axis=-1, keepdims=True)
        norm_prob = prob * r_den
        dprob = dot_nt(cot, values)
        mean = jnp.sum(norm_prob * dprob, axis=-1, keepdims=True)
        dscore = (norm_prob * (dprob - mean)).astype(jnp.bfloat16)
        norm_low = norm_prob.astype(jnp.bfloat16)
        out_ref[:, lanes] = dot_nn(norm_low, values).astype(jnp.bfloat16)
        grad = sharp * dot_nn(dscore, key_low)
        along = jnp.sum(q_dir * grad, axis=-1, keepdims=True)
        dq_ref[:, lanes] = (q_inv * (grad - q_dir * along)).astype(jnp.bfloat16)
        scale_ref[head * 8 : head * 8 + 8, :] = fold_rows(q_low.astype(jnp.float32) * grad)
        q_turned = jnp.transpose(q_dir).astype(jnp.bfloat16)
        cot_turned = jnp.transpose(cot.astype(jnp.float32)).astype(jnp.bfloat16)
        dk_ref[:, lanes] = sharp * jnp.transpose(dot_nn(q_turned, dscore))
        dv_ref[:, lanes] = jnp.transpose(dot_nn(cot_turned, norm_low))

        @pl.when(own == head)
        def _():
            key_low_ref[...] = key_low
            value_ref[...] = values


def run_coarse(log_scale, levels, queries, keys, values, cots):
    count, features = queries.shape
    heads = log_scale.shape[0]
    width = features // heads
    vmem = pl.BlockSpec(memory_space=pltpu.VMEM)
    wide = jax.ShapeDtypeStruct((count, features), jnp.float32)
    low = jax.ShapeDtypeStruct((count, features), jnp.bfloat16)
    return pl.pallas_call(
        coarse_kernel,
        out_shape=(low, low, wide, wide, jax.ShapeDtypeStruct((heads * 8, width), jnp.float32))
        + (jax.ShapeDtypeStruct((count, width), jnp.bfloat16),) * 2,
        in_specs=[pl.BlockSpec(memory_space=pltpu.SMEM)] + [vmem] * 6,
        compiler_params=params(16),
        cost_estimate=pl.CostEstimate(
            flops=12 * count * count * features,
            bytes_accessed=24 * count * features,
            transcendentals=heads * count * count,
        ),
        name="coarse_attention",
    )(log_scale, levels[:, None], levels[None, :], queries, keys, values, cots)


def sum_kernel(term0_ref, term1_ref, term2_ref, term3_ref, own_ref, scale_in_ref, dkv_ref, small_ref):
    members, pair, width = dkv_ref.shape
    rows = pair // 2
    fine = members * rows
    summed = term0_ref[...].astype(jnp.float32)
    for ref in (term1_ref, term2_ref, term3_ref):
        summed = summed + ref[...].astype(jnp.float32)
    grad = project(own_ref[:, 0:rows].reshape(fine, width), summed[:fine, :width])
    dkv_ref[:, 0:rows] = grad.astype(jnp.bfloat16).reshape(members, rows, width)
    dkv_ref[:, rows:] = summed[:fine, width:].astype(jnp.bfloat16).reshape(members, rows, width)
    small = summed.shape[0] - fine
    small_ref[0:small, :] = summed[fine:].astype(jnp.bfloat16)
    left = jnp.sum(scale_in_ref[...], axis=0, keepdims=True)
    left = jnp.sum(left, axis=-1, keepdims=True)
    row = lax.broadcasted_iota(jnp.int32, (note_rows, 2 * width), 0)
    note = jnp.zeros((note_rows, 2 * width), jnp.float32)
    for part in range(3):
        piece = left.astype(jnp.bfloat16).astype(jnp.float32)
        note = jnp.where(row == part, piece, note)
        left = left - piece
    small_ref[small:, :] = note.astype(jnp.bfloat16)


def run_sum(terms, own_rows, scales):
    count, both = terms[0].shape
    members, tall, width = own_rows.shape
    pair = (tall - note_rows) // 2
    small = count - members * pair // 2
    return pl.pallas_call(
        sum_kernel,
        out_shape=(
            jax.ShapeDtypeStruct((members, pair, width), jnp.bfloat16),
            jax.ShapeDtypeStruct((small + note_rows, both), jnp.bfloat16),
        ),
        compiler_params=params(12),
        name="sum_key_terms",
    )(*terms, own_rows, scales)


def join_kernel(terms_ref, dk_own_ref, dv_own_ref, k_ref, dk_ref, dv_ref, scale_ref):
    _, heads, tall, both = terms_ref.shape
    width = both // 2
    small = tall - note_rows
    for head in range(heads):
        lanes = slice(head * width, (head + 1) * width)
        terms = terms_ref[:, head].astype(jnp.float32)
        scale_ref[head : head + 1, :] = jnp.sum(
            jnp.sum(terms[:, small:, :width], axis=0), axis=0, keepdims=True
        )
        terms = terms[:, :small].reshape(planes * small, both)
        grad = terms[:, :width] + dk_own_ref[:, lanes]
        dk_ref[:, lanes] = project(k_ref[:, lanes], grad).astype(jnp.bfloat16)
        dv_ref[:, lanes] = (terms[:, width:] + dv_own_ref[:, lanes]).astype(jnp.bfloat16)


def run_join(terms, dk_own, dv_own, keys):
    _, heads, _, both = terms.shape
    count, features = keys.shape
    low = jax.ShapeDtypeStruct((count, features), jnp.bfloat16)
    return pl.pallas_call(
        join_kernel,
        out_shape=(low, low, jax.ShapeDtypeStruct((heads, both // 2), jnp.float32)),
        compiler_params=params(14),
        name="join_coarse",
    )(terms, dk_own, dv_own, keys)


def unpack_kernel(od_ref, dkv_ref, out_ref, dq_ref, dk_ref, dv_ref):
    heads, pair, width = od_ref.shape
    rows = pair // 2
    for head in range(heads):
        lanes = slice(head * width, (head + 1) * width)
        out_ref[:, lanes] = od_ref[head, 0:rows]
        dq_ref[:, lanes] = od_ref[head, rows:]
        dk_ref[:, lanes] = dkv_ref[head, 0:rows]
        dv_ref[:, lanes] = dkv_ref[head, rows:]


def run_unpack(od_back, dkv_back):
    heads, pair, width = od_back.shape
    flat = jax.ShapeDtypeStruct((pair // 2, heads * width), jnp.bfloat16)
    return pl.pallas_call(
        unpack_kernel,
        out_shape=(flat,) * 4,
        compiler_params=params(4),
        name="unpack_heads",
    )(od_back, dkv_back)


def body(
    q_coarse,
    k_coarse,
    v_coarse,
    cot_coarse,
    coarse_ids,
    q_fine,
    k_fine,
    v_fine,
    cot_fine,
    fine_ids,
    log_scale,
):
    heads = log_scale.shape[0]
    coarse = q_coarse.shape[1]
    rows = q_fine.shape[1]
    seq = lax.axis_size("seq")
    images = lax.axis_size("dp")
    groups = [
        [((g + h // 2) % planes) * heads + h for h in range(heads)] for g in range(planes)
    ]

    def exchange(parts):
        return lax.all_to_all(parts, "seq", 0, 0, axis_index_groups=groups, tiled=True)

    def to_plane(array, step):
        return lax.ppermute(
            array, "seq", [(i, (i + step * heads) % seq) for i in range(seq)]
        )

    own_rows = exchange(run_pack(heads, fine_ids, k_fine[0], v_fine[0], q_fine[0], cot_fine[0]))
    kv_own = own_rows[:, : 2 * rows + note_rows]
    kv_rows = [to_plane(kv_own, step) for step in range(1, planes)]

    out_c, dq_c, dk_own, dv_own, scale_c, key_c, val_c = run_coarse(
        log_scale, coarse_ids[0], q_coarse[0], k_coarse[0], v_coarse[0], cot_coarse[0]
    )
    od, *dkv, scale = run_fine(log_scale, own_rows, kv_rows, key_c, val_c, scale_c)

    terms = [dkv[0]] + [to_plane(dkv[step], step) for step in range(1, planes)]
    scales = lax.all_gather(scale, "dp", axis=0, tiled=True)
    od_back = exchange(od)
    dkv_parts, small_terms = run_sum(terms, own_rows, scales)
    dkv_back = exchange(dkv_parts)
    of_image = lax.all_gather(small_terms, "seq", axis=0)
    of_image = of_image.reshape((planes, heads) + small_terms.shape)
    dk_c, dv_c, scale_rows = run_join(of_image, dk_own, dv_own, k_coarse[0])
    fine_out, fine_dq, fine_dk, fine_dv = run_unpack(od_back, dkv_back)
    grad_scale = scale_rows[:, 0] / math.sqrt(images * (coarse + seq * rows))
    return (
        out_c[None],
        dq_c[None],
        dk_c[None],
        dv_c[None],
        fine_out[None],
        fine_dq[None],
        fine_dk[None],
        fine_dv[None],
        grad_scale,
    )


def solution(mesh):
    whole = P("dp", None, None)
    split = P("dp", "seq", None)
    return jax.shard_map(
        body,
        mesh=mesh,
        in_specs=(whole,) * 4 + (P("dp", None),) + (split,) * 4 + (P("dp", "seq"), P()),
        out_specs=(whole,) * 4 + (split,) * 4 + (P(),),
        check_vma=False,
    )
```

```python
import math

import jax
import jax.numpy as jnp
from jax import lax
from jax.experimental import pallas as pl
from jax.experimental.pallas import tpu as pltpu
from jax.sharding import PartitionSpec as P

norm_eps = 1e-06
log2_e = 1.4426950408889634
k_tile = 256
note_rows = 16

planes = 4


def dot_nt(left, right):
    return lax.dot_general(
        left, right, (((1,), (1,)), ((), ())), preferred_element_type=jnp.float32
    )


def dot_nn(left, right):
    return jnp.dot(left, right, preferred_element_type=jnp.float32)


def unit_rows(rows):
    wide = rows.astype(jnp.float32)
    inv_norm = lax.rsqrt(jnp.sum(wide * wide, axis=-1, keepdims=True) + norm_eps)
    return wide * inv_norm, inv_norm


def project(key_rows, grad):
    key_dir, key_inv = unit_rows(key_rows)
    along = jnp.sum(key_dir * grad, axis=-1, keepdims=True)
    return key_inv * (grad - key_dir * along)


def fold_rows(terms):
    rows, width = terms.shape
    return jnp.sum(terms.reshape(rows // 8, 8, width), axis=0)


def in_pieces(value, width):
    row = lax.broadcasted_iota(jnp.int32, (note_rows, width), 0)
    note = jnp.zeros((note_rows, width), jnp.float32)
    for part in range(3):
        piece = value.astype(jnp.bfloat16).astype(jnp.float32)
        note = jnp.where(row == part, piece, note)
        value = value - piece
    return note.astype(jnp.bfloat16)


def sum_all(terms):
    return jnp.sum(jnp.sum(terms, axis=0, keepdims=True), axis=-1, keepdims=True)


def seq_place():
    here = lax.axis_index("seq")
    plane = lax.bitwise_and(lax.shift_right_logical(here, 1), 3)
    head = 2 * lax.shift_right_logical(here, 3) + lax.bitwise_and(here, 1)
    return plane, head


def key_slot(plane):
    return lax.bitwise_and(plane, 1)


def query_slot(plane):
    return lax.shift_right_logical(plane, 1)


def params(mebibytes):
    return pltpu.CompilerParams(vmem_limit_bytes=mebibytes * 1024 * 1024)


def pack_kernel(ids_ref, k_ref, v_ref, q_ref, cot_ref, all_ref):
    heads, _, width = all_ref.shape
    rows = k_ref.shape[0]
    ids = ids_ref[...]
    row = lax.broadcasted_iota(jnp.int32, (note_rows, width), 0)
    lane = lax.broadcasted_iota(jnp.int32, (note_rows, width), 1)
    note = jnp.zeros((note_rows, width), jnp.float32)
    for level in range(2):
        count = jnp.sum(jnp.where(ids <= level, 1.0, 0.0), axis=-1, keepdims=True)
        note = jnp.where((row == level) & (lane == 0), count, note)
    note = note.astype(jnp.bfloat16)
    first_query = 2 * rows + note_rows
    for head in range(heads):
        lanes = slice(head * width, (head + 1) * width)
        all_ref[head, 0:rows] = k_ref[:, lanes]
        all_ref[head, rows : 2 * rows] = v_ref[:, lanes]
        all_ref[head, 2 * rows : first_query] = note
        all_ref[head, first_query : first_query + rows] = q_ref[:, lanes]
        all_ref[head, first_query + rows :] = cot_ref[:, lanes]


def run_pack(heads, ids, keys, values, queries, cots):
    rows, features = keys.shape
    shape = (heads, 4 * rows + note_rows, features // heads)
    return pl.pallas_call(
        pack_kernel,
        out_shape=jax.ShapeDtypeStruct(shape, jnp.bfloat16),
        compiler_params=params(56),
        name="pack_heads",
    )(ids, keys, values, queries, cots)


def twice(column):
    return jnp.concatenate([column, column], axis=1)


def wide_as(column, size):
    return column if size == column.shape[1] else twice(column)


def place_of(run, slot, block):
    return pl.multiple_of((2 * run + slot) * block, 64)


def key_spot(first, size):
    return pl.ds(first if isinstance(first, int) else pl.multiple_of(first, 128), size)


def all_chunks(work, some_keys, shared, chunks):
    work(0, some_keys, 0)

    def both(chunk, carry):
        work(some_keys + chunk * k_tile, k_tile, 0)
        return carry

    def upper(chunk, carry):
        work(some_keys + chunk * k_tile, k_tile, 1)
        return carry

    lax.fori_loop(0, shared, both, 0)
    lax.fori_loop(shared, chunks, upper, 0)


def forward_kernel(
    log_ref,
    own_ref,
    kv_ref,
    qc_ref,
    kc_ref,
    vc_ref,
    prob_ref,
    key_ref,
    val_ref,
    query_ref,
    cot_ref,
    num_ref,
    stat_ref,
    shared_ref,
    wide_scr,
    limit_scr,
    sum_scr,
):
    plane, head = seq_place()
    members, tall, width = own_ref.shape
    rows = (tall - note_rows) // 4
    block = 2 * rows
    runs = members // 2
    queries = query_ref.shape[0]
    some_keys = kc_ref.shape[0] // 2
    fine = key_ref.shape[0] - some_keys
    first_query = 2 * rows + note_rows

    def count(notes):
        total = jnp.sum(notes.astype(jnp.float32), axis=0)
        return [jnp.sum(total[level : level + 1]).astype(jnp.int32) for level in range(2)]

    own_counts = count(own_ref[:, 2 * rows : first_query])
    key_counts = [a + b for a, b in zip(own_counts, count(kv_ref[:, 2 * rows :]))]
    query_counts = [a + b for a, b in zip(own_counts, count(qc_ref[:, :note_rows]))]

    def limit_of(place):
        return jnp.where(
            place < query_counts[0],
            key_counts[0],
            jnp.where(place < query_counts[1], key_counts[1], fine),
        )

    own_slot = key_slot(plane)
    for ref, slot in ((own_ref, own_slot), (kv_ref, 1 - own_slot)):
        for run in range(runs):
            pick = slice(2 * run, 2 * run + 2)
            spot = pl.ds(pl.multiple_of(some_keys + place_of(run, slot, block), 64), block)
            key_ref[spot, :] = unit_rows(ref[pick, 0:rows].reshape(block, width))[0].astype(
                jnp.bfloat16
            )
            values = ref[pick, rows : 2 * rows].reshape(block, width)
            val_ref[spot, :] = values
            wide_scr[spot, 0:width] = values
    half = pl.ds(pl.multiple_of(query_slot(plane) * some_keys, some_keys), some_keys)
    key_ref[0:some_keys, :] = kc_ref[half, :]
    val_ref[0:some_keys, :] = vc_ref[half, :]
    wide_scr[0:some_keys, 0:width] = vc_ref[half, :]
    wide_scr[:, width:] = jnp.ones((some_keys + fine, width), jnp.bfloat16)

    own_slot = query_slot(plane)
    for ref, slot, start in ((own_ref, own_slot, first_query), (qc_ref, 1 - own_slot, note_rows)):
        for run in range(runs):
            pick = slice(2 * run, 2 * run + 2)
            spot = pl.ds(place_of(run, slot, block), block)
            query_ref[spot, :] = unit_rows(
                ref[pick, start : start + rows].reshape(block, width)
            )[0].astype(jnp.bfloat16)
            cot_ref[spot, :] = ref[pick, start + rows : start + 2 * rows].reshape(block, width)
    limit_scr[...] = some_keys + limit_of(
        lax.broadcasted_iota(jnp.int32, (queries, width), 0)
    )

    sharp = jnp.exp(jnp.full((1, width), log_ref[head], jnp.float32))[:, 0:1]
    slope = sharp * log2_e
    sum_scr[...] = jnp.zeros_like(sum_scr)

    def probs(start, size, part):
        first = part * queries // 2
        spot = key_spot(start, size)
        cosine = dot_nt(query_ref[first:, :], key_ref[spot, :])
        prob = jnp.exp2(cosine * slope - slope)
        place = start + lax.broadcasted_iota(jnp.int32, (1, size), 1)
        seen = place < wide_as(limit_scr[first:, :], size)
        prob = jnp.where(seen, prob, 0.0).astype(jnp.bfloat16)
        prob_ref[first:, spot] = prob
        sum_scr[first:, :] += dot_nn(prob, wide_scr[spot, :])

    shared = (limit_of(queries // 2 - 1) + k_tile - 1) // k_tile
    shared_ref[0] = shared
    all_chunks(probs, some_keys, shared, fine // k_tile)

    num = sum_scr[:, :width]
    num_ref[...] = num
    weighted = jnp.sum(num * cot_ref[...].astype(jnp.float32), axis=-1, keepdims=True)
    row = lax.broadcasted_iota(jnp.int32, (width, width), 0)
    lane = lax.broadcasted_iota(jnp.int32, (width, width), 1)
    parts = queries // width
    for part in range(parts):
        spot = slice(part * width, (part + 1) * width)
        for index, value in ((part, sum_scr[spot, width:]), (parts + part, weighted[spot])):
            stat_ref[index : index + 1, :] = jnp.sum(
                jnp.where(row == lane, value, 0.0), axis=0, keepdims=True
            )


def backward_kernel(
    log_ref,
    shared_ref,
    own_ref,
    qc_ref,
    stat_ref,
    other_stat_ref,
    prob_ref,
    key_ref,
    val_ref,
    query_ref,
    cot_ref,
    num_ref,
    coarse_scale_ref,
    od_ref,
    od_send_ref,
    dkv_ref,
    dkv_send_ref,
    small_ref,
    den_scr,
    mean_scr,
    grad_scr,
    query_turn,
    cot_turn,
    turn_scr,
):
    plane, head = seq_place()
    members, tall, width = own_ref.shape
    rows = (tall - note_rows) // 4
    block = 2 * rows
    runs = members // 2
    queries = query_ref.shape[0]
    first_query = 2 * rows + note_rows
    some_keys = small_ref.shape[0] - note_rows
    fine = key_ref.shape[0] - some_keys
    sharp = jnp.exp(jnp.full((1, width), log_ref[head], jnp.float32))[:, 0:1]

    row = lax.broadcasted_iota(jnp.int32, (width, width), 0)
    lane = lax.broadcasted_iota(jnp.int32, (width, width), 1)
    parts = queries // width

    def column(index):
        values = stat_ref[index : index + 1, :] + other_stat_ref[index : index + 1, :]
        return jnp.sum(jnp.where(row == lane, values, 0.0), axis=1, keepdims=True)

    for part in range(parts):
        spot = slice(part * width, (part + 1) * width)
        r_den = 1.0 / column(part)
        den_scr[spot, :] = jnp.broadcast_to(r_den, (width, width))
        mean_scr[spot, :] = jnp.broadcast_to(column(parts + part) * r_den, (width, width))

    grad_scr[...] = jnp.zeros_like(grad_scr)
    query_turn[...] = jnp.transpose(
        query_ref[...].astype(jnp.float32) * (den_scr[...] * sharp)
    ).astype(jnp.bfloat16)
    cot_turn[...] = jnp.transpose(cot_ref[...].astype(jnp.float32) * den_scr[...]).astype(
        jnp.bfloat16
    )

    def grads(start, size, part):
        first = part * queries // 2
        spot = key_spot(start, size)
        prob = prob_ref[first:, spot]
        dprob = dot_nt(cot_ref[first:, :], val_ref[spot, :])
        dscore = prob.astype(jnp.float32) * (dprob - wide_as(mean_scr[first:, :], size))
        dscore = dscore.astype(jnp.bfloat16)
        grad_scr[first:, :] += dot_nn(dscore, key_ref[spot, :])
        dk = dot_nn(query_turn[:, first:], dscore)
        dv = dot_nn(cot_turn[:, first:], prob)
        turn_scr[spot, 0:width] = jnp.transpose(dk).astype(jnp.bfloat16)
        turn_scr[spot, width:] = jnp.transpose(dv).astype(jnp.bfloat16)

    all_chunks(grads, some_keys, shared_ref[0], fine // k_tile)

    own_slot = query_slot(plane)
    scale = coarse_scale_ref[pl.ds(pl.multiple_of(head * 8, 8), 8), :]
    scale = scale * jnp.where(plane == 0, 1.0, 0.0)
    for ref, slot, start, target in (
        (own_ref, own_slot, first_query, od_ref),
        (qc_ref, 1 - own_slot, note_rows, od_send_ref),
    ):
        for run in range(runs):
            spot = pl.ds(place_of(run, slot, block), block)
            pick = ref[2 * run : 2 * run + 2, start : start + rows]
            q_dir, q_inv = unit_rows(pick.reshape(block, width))
            r_den = den_scr[spot, :]
            grad = grad_scr[spot, :] * (r_den * sharp)
            along = jnp.sum(q_dir * grad, axis=-1, keepdims=True)
            scale = scale + fold_rows(query_ref[spot, :].astype(jnp.float32) * grad)
            to = slice(run * block, (run + 1) * block)
            target[to, 0:width] = (num_ref[spot, :] * r_den).astype(jnp.bfloat16)
            target[to, width:] = (q_inv * (grad - q_dir * along)).astype(jnp.bfloat16)

    own_slot = key_slot(plane)
    for slot, target in ((own_slot, dkv_ref), (1 - own_slot, dkv_send_ref)):
        for run in range(runs):
            spot = pl.ds(pl.multiple_of(some_keys + place_of(run, slot, block), 64), block)
            target[run * block : (run + 1) * block, :] = turn_scr[spot, :]
    small_ref[0:some_keys, :] = turn_scr[0:some_keys, :]
    small_ref[some_keys:, :] = in_pieces(sum_all(scale), 2 * width)


def run_fine(log_scale, own_rows, kv_rows, qc_rows, key_coarse, val_coarse, coarse_scale, swap):
    members, tall, width = own_rows.shape
    rows = (tall - note_rows) // 4
    some_keys = key_coarse.shape[0] // 2
    queries = 2 * members * rows
    total = some_keys + queries
    vmem = pl.BlockSpec(memory_space=pltpu.VMEM)
    smem = pl.BlockSpec(memory_space=pltpu.SMEM)

    def low(*shape):
        return jax.ShapeDtypeStruct(shape, jnp.bfloat16)

    def wide(*shape):
        return jax.ShapeDtypeStruct(shape, jnp.float32)

    prob, keys, values, query, cot, num, stat, shared = pl.pallas_call(
        forward_kernel,
        out_shape=(
            low(queries, total),
            low(total, width),
            low(total, width),
            low(queries, width),
            low(queries, width),
            wide(queries, width),
            wide(2 * queries // width, width),
            jax.ShapeDtypeStruct((1,), jnp.int32),
        ),
        in_specs=[smem] + [vmem] * 5,
        out_specs=(vmem,) * 7 + (smem,),
        scratch_shapes=[
            pltpu.VMEM((total, 2 * width), jnp.bfloat16),
            pltpu.VMEM((queries, width), jnp.int32),
            pltpu.VMEM((queries, 2 * width), jnp.float32),
        ],
        compiler_params=params(20),
        cost_estimate=pl.CostEstimate(
            flops=4 * queries * total * width,
            bytes_accessed=4 * queries * total,
            transcendentals=queries * total,
        ),
        name="fine_forward",
    )(log_scale, own_rows, kv_rows, qc_rows, key_coarse, val_coarse)
    other_stat = swap(stat)
    half = low(queries // 2, 2 * width)
    return pl.pallas_call(
        backward_kernel,
        out_shape=(half, half, half, half, low(some_keys + note_rows, 2 * width)),
        in_specs=[smem, smem] + [vmem] * 11,
        out_specs=(vmem,) * 5,
        scratch_shapes=[
            pltpu.VMEM((queries, width), jnp.float32),
            pltpu.VMEM((queries, width), jnp.float32),
            pltpu.VMEM((queries, width), jnp.float32),
            pltpu.VMEM((width, queries), jnp.bfloat16),
            pltpu.VMEM((width, queries), jnp.bfloat16),
            pltpu.VMEM((total, 2 * width), jnp.bfloat16),
        ],
        compiler_params=params(20),
        cost_estimate=pl.CostEstimate(
            flops=8 * queries * total * width,
            bytes_accessed=4 * queries * total,
            transcendentals=0,
        ),
        name="fine_backward",
    )(
        log_scale,
        shared,
        own_rows,
        qc_rows,
        stat,
        other_stat,
        prob,
        keys,
        values,
        query,
        cot,
        num,
        coarse_scale,
    )


def coarse_kernel(
    log_ref,
    row_level_ref,
    col_level_ref,
    q_ref,
    k_ref,
    v_ref,
    cot_ref,
    out_ref,
    dq_ref,
    dk_ref,
    dv_ref,
    scale_ref,
    key_low_ref,
    value_ref,
):
    _, own = seq_place()
    count, features = q_ref.shape
    heads = log_ref.shape[0]
    width = features // heads
    visible = col_level_ref[...] <= row_level_ref[...]
    for head in range(heads):
        lanes = slice(head * width, (head + 1) * width)
        sharp = jnp.exp(jnp.full((1, width), log_ref[head], jnp.float32))[:, 0:1]
        slope = sharp * log2_e
        q_dir, q_inv = unit_rows(q_ref[:, lanes])
        q_low = q_dir.astype(jnp.bfloat16)
        key_low = unit_rows(k_ref[:, lanes])[0].astype(jnp.bfloat16)
        values = v_ref[:, lanes]
        cot = cot_ref[:, lanes]
        prob = jnp.exp2(dot_nt(q_low, key_low) * slope - slope)
        prob = jnp.where(visible, prob, 0.0)
        r_den = 1.0 / jnp.sum(prob, axis=-1, keepdims=True)
        norm_prob = prob * r_den
        dprob = dot_nt(cot, values)
        mean = jnp.sum(norm_prob * dprob, axis=-1, keepdims=True)
        dscore = (norm_prob * (dprob - mean)).astype(jnp.bfloat16)
        norm_low = norm_prob.astype(jnp.bfloat16)
        out_ref[:, lanes] = dot_nn(norm_low, values).astype(jnp.bfloat16)
        grad = sharp * dot_nn(dscore, key_low)
        along = jnp.sum(q_dir * grad, axis=-1, keepdims=True)
        dq_ref[:, lanes] = (q_inv * (grad - q_dir * along)).astype(jnp.bfloat16)
        scale_ref[head * 8 : head * 8 + 8, :] = fold_rows(q_low.astype(jnp.float32) * grad)
        q_turned = jnp.transpose(q_dir).astype(jnp.bfloat16)
        cot_turned = jnp.transpose(cot.astype(jnp.float32)).astype(jnp.bfloat16)
        dk_ref[:, lanes] = sharp * jnp.transpose(dot_nn(q_turned, dscore))
        dv_ref[:, lanes] = jnp.transpose(dot_nn(cot_turned, norm_low))

        @pl.when(own == head)
        def _():
            key_low_ref[...] = key_low
            value_ref[...] = values


def run_coarse(log_scale, levels, queries, keys, values, cots):
    count, features = queries.shape
    heads = log_scale.shape[0]
    width = features // heads
    vmem = pl.BlockSpec(memory_space=pltpu.VMEM)
    wide = jax.ShapeDtypeStruct((count, features), jnp.float32)
    low = jax.ShapeDtypeStruct((count, features), jnp.bfloat16)
    return pl.pallas_call(
        coarse_kernel,
        out_shape=(low, low, wide, wide, jax.ShapeDtypeStruct((heads * 8, width), jnp.float32))
        + (jax.ShapeDtypeStruct((count, width), jnp.bfloat16),) * 2,
        in_specs=[pl.BlockSpec(memory_space=pltpu.SMEM)] + [vmem] * 6,
        compiler_params=params(16),
        cost_estimate=pl.CostEstimate(
            flops=12 * count * count * features,
            bytes_accessed=24 * count * features,
            transcendentals=heads * count * count,
        ),
        name="coarse_attention",
    )(log_scale, levels[:, None], levels[None, :], queries, keys, values, cots)


def small_kernel(own_ref, near_ref, across_ref, far_ref, sum_ref, scale_ref):
    plane, _ = seq_place()
    some_keys = own_ref.shape[0] - note_rows
    terms = [ref[...].astype(jnp.float32) for ref in (own_ref, near_ref, across_ref, far_ref)]
    half = query_slot(plane)
    for place, pair in ((half, terms[:2]), (1 - half, terms[2:])):
        spot = pl.ds(pl.multiple_of(place * some_keys, some_keys), some_keys)
        sum_ref[spot, :] = (pair[0][:some_keys] + pair[1][:some_keys]).astype(jnp.bfloat16)
    scale = terms[0][some_keys:] + terms[1][some_keys:] + terms[2][some_keys:] + terms[3][some_keys:]
    scale = jnp.sum(scale[:, : scale_ref.shape[2]], axis=0, keepdims=True)
    scale_ref[...] = jnp.broadcast_to(scale[None], scale_ref.shape)


def run_small(images, terms):
    tall, both = terms[0].shape
    return pl.pallas_call(
        small_kernel,
        out_shape=(
            jax.ShapeDtypeStruct((2 * (tall - note_rows), both), jnp.bfloat16),
            jax.ShapeDtypeStruct((images, 8, both // 2), jnp.float32),
        ),
        compiler_params=params(4),
        name="sum_coarse_terms",
    )(*terms)


def sum_kernel(od_ref, other_od_ref, dkv_ref, other_dkv_ref, own_ref, scale_ref, all_ref):
    members, tall, width = all_ref.shape
    rows = (tall - note_rows) // 4
    fine = members * rows

    def put(place, value):
        all_ref[:, place * rows : (place + 1) * rows] = value.astype(jnp.bfloat16).reshape(
            members, rows, width
        )

    summed = od_ref[...].astype(jnp.float32) + other_od_ref[...].astype(jnp.float32)
    put(0, summed[:, :width])
    put(1, summed[:, width:])
    summed = dkv_ref[...].astype(jnp.float32) + other_dkv_ref[...].astype(jnp.float32)
    put(2, project(own_ref[:, 0:rows].reshape(fine, width), summed[:, :width]))
    put(3, summed[:, width:])
    scale = jnp.sum(scale_ref[:, 0, 0:1], axis=0, keepdims=True)
    note = in_pieces(scale, width)
    for member in range(members):
        all_ref[member, 4 * rows :] = note


def run_sum(od, other_od, dkv, other_dkv, own_rows, scale):
    return pl.pallas_call(
        sum_kernel,
        out_shape=jax.ShapeDtypeStruct(own_rows.shape, jnp.bfloat16),
        compiler_params=params(10),
        name="sum_pairs",
    )(od, other_od, dkv, other_dkv, own_rows, scale)


def join_kernel(terms_ref, dk_own_ref, dv_own_ref, k_ref, dk_ref, dv_ref):
    heads, _, both = terms_ref.shape
    width = both // 2
    for head in range(heads):
        lanes = slice(head * width, (head + 1) * width)
        terms = terms_ref[head].astype(jnp.float32)
        grad = terms[:, :width] + dk_own_ref[:, lanes]
        dk_ref[:, lanes] = project(k_ref[:, lanes], grad).astype(jnp.bfloat16)
        dv_ref[:, lanes] = (terms[:, width:] + dv_own_ref[:, lanes]).astype(jnp.bfloat16)


def run_join(terms, dk_own, dv_own, keys):
    low = jax.ShapeDtypeStruct(keys.shape, jnp.bfloat16)
    return pl.pallas_call(
        join_kernel,
        out_shape=(low, low),
        compiler_params=params(14),
        name="join_coarse",
    )(terms, dk_own, dv_own, keys)


def unpack_kernel(all_ref, out_ref, dq_ref, dk_ref, dv_ref, scale_ref):
    heads, tall, width = all_ref.shape
    rows = (tall - note_rows) // 4
    for head in range(heads):
        lanes = slice(head * width, (head + 1) * width)
        for place, ref in enumerate((out_ref, dq_ref, dk_ref, dv_ref)):
            ref[:, lanes] = all_ref[head, place * rows : (place + 1) * rows]
    scale_ref[...] = jnp.sum(all_ref[:, 4 * rows :].astype(jnp.float32), axis=1)


def run_unpack(all_back):
    heads, tall, width = all_back.shape
    flat = jax.ShapeDtypeStruct(((tall - note_rows) // 4, heads * width), jnp.bfloat16)
    return pl.pallas_call(
        unpack_kernel,
        out_shape=(flat,) * 4 + (jax.ShapeDtypeStruct((heads, width), jnp.float32),),
        compiler_params=params(4),
        name="unpack_heads",
    )(all_back)


def body(
    q_coarse,
    k_coarse,
    v_coarse,
    cot_coarse,
    coarse_ids,
    q_fine,
    k_fine,
    v_fine,
    cot_fine,
    fine_ids,
    log_scale,
):
    heads = log_scale.shape[0]
    coarse = q_coarse.shape[1]
    rows = q_fine.shape[1]
    seq = lax.axis_size("seq")
    images = lax.axis_size("dp")
    groups = [
        [8 * (h // 2) + 2 * plane + h % 2 for h in range(heads)] for plane in range(planes)
    ]

    def exchange(parts):
        return lax.all_to_all(parts, "seq", 0, 0, axis_index_groups=groups, tiled=True)

    def to_plane(array, flip):
        return lax.ppermute(array, "seq", [(i, i ^ (2 * flip)) for i in range(seq)])

    own_rows = exchange(run_pack(heads, fine_ids, k_fine[0], v_fine[0], q_fine[0], cot_fine[0]))
    kv_rows = to_plane(own_rows[:, : 2 * rows + note_rows], 1)
    qc_rows = to_plane(own_rows[:, 2 * rows :], 3)

    out_c, dq_c, dk_own, dv_own, scale_c, key_c, val_c = run_coarse(
        log_scale, coarse_ids[0], q_coarse[0], k_coarse[0], v_coarse[0], cot_coarse[0]
    )
    od, od_send, dkv, dkv_send, small = run_fine(
        log_scale, own_rows, kv_rows, qc_rows, key_c, val_c, scale_c, lambda stat: to_plane(stat, 3)
    )

    small_sum, scale = run_small(images, [small] + [to_plane(small, flip) for flip in (1, 2, 3)])
    of_image = lax.all_gather(small_sum, "seq", axis=0, axis_index_groups=groups)

    other_dkv = to_plane(dkv_send, 1)
    other_od = to_plane(od_send, 3)
    scale = lax.all_to_all(scale, "dp", 0, 0, tiled=True)
    all_back = exchange(run_sum(od, other_od, dkv, other_dkv, own_rows, scale))
    fine_out, fine_dq, fine_dk, fine_dv, scale = run_unpack(all_back)
    dk_c, dv_c = run_join(of_image, dk_own, dv_own, k_coarse[0])
    grad_scale = scale[:, 0] / math.sqrt(images * (coarse + seq * rows))
    return (
        out_c[None],
        dq_c[None],
        dk_c[None],
        dv_c[None],
        fine_out[None],
        fine_dq[None],
        fine_dk[None],
        fine_dv[None],
        grad_scale,
    )


def solution(mesh):
    whole = P("dp", None, None)
    split = P("dp", "seq", None)
    return jax.shard_map(
        body,
        mesh=mesh,
        in_specs=(whole,) * 4 + (P("dp", None),) + (split,) * 4 + (P("dp", "seq"), P()),
        out_specs=(whole,) * 4 + (split,) * 4 + (P(),),
        check_vma=False,
    )
```

```python
import math
from functools import partial

import jax
import jax.numpy as jnp
from jax import lax
from jax.experimental import pallas as pl
from jax.experimental.pallas import tpu as pltpu
from jax.sharding import PartitionSpec as P

norm_eps = 1e-06
log2_e = 1.4426950408889634
k_tile = 256
note_rows = 16

planes = 4


def dot_nt(left, right):
    return lax.dot_general(
        left, right, (((1,), (1,)), ((), ())), preferred_element_type=jnp.float32
    )


def dot_nn(left, right):
    return jnp.dot(left, right, preferred_element_type=jnp.float32)


def unit_rows(rows):
    wide = rows.astype(jnp.float32)
    inv_norm = lax.rsqrt(jnp.sum(wide * wide, axis=-1, keepdims=True) + norm_eps)
    return wide * inv_norm, inv_norm


def project(key_rows, grad):
    key_dir, key_inv = unit_rows(key_rows)
    along = jnp.sum(key_dir * grad, axis=-1, keepdims=True)
    return key_inv * (grad - key_dir * along)


def fold_rows(terms):
    rows, width = terms.shape
    return jnp.sum(terms.reshape(rows // 8, 8, width), axis=0)


def in_pieces(value, width):
    row = lax.broadcasted_iota(jnp.int32, (note_rows, width), 0)
    note = jnp.zeros((note_rows, width), jnp.float32)
    for part in range(3):
        piece = value.astype(jnp.bfloat16).astype(jnp.float32)
        note = jnp.where(row == part, piece, note)
        value = value - piece
    return note.astype(jnp.bfloat16)


def sum_all(terms):
    return jnp.sum(jnp.sum(terms, axis=0, keepdims=True), axis=-1, keepdims=True)


def seq_place():
    here = lax.axis_index("seq")
    plane = lax.bitwise_and(lax.shift_right_logical(here, 1), 3)
    head = 2 * lax.shift_right_logical(here, 3) + lax.bitwise_and(here, 1)
    return plane, head


def key_slot(plane):
    return lax.bitwise_and(plane, 1)


def query_slot(plane):
    return lax.shift_right_logical(plane, 1)


def params(mebibytes):
    return pltpu.CompilerParams(vmem_limit_bytes=mebibytes * 1024 * 1024)


def pack_kernel(ids_ref, k_ref, v_ref, q_ref, cot_ref, all_ref):
    heads, _, width = all_ref.shape
    rows = k_ref.shape[0]
    ids = ids_ref[...]
    row = lax.broadcasted_iota(jnp.int32, (note_rows, width), 0)
    lane = lax.broadcasted_iota(jnp.int32, (note_rows, width), 1)
    note = jnp.zeros((note_rows, width), jnp.float32)
    for level in range(2):
        count = jnp.sum(jnp.where(ids <= level, 1.0, 0.0), axis=-1, keepdims=True)
        note = jnp.where((row == level) & (lane == 0), count, note)
    note = note.astype(jnp.bfloat16)
    first_query = 2 * rows + note_rows
    for head in range(heads):
        lanes = slice(head * width, (head + 1) * width)
        all_ref[head, 0:rows] = k_ref[:, lanes]
        all_ref[head, rows : 2 * rows] = v_ref[:, lanes]
        all_ref[head, 2 * rows : first_query] = note
        all_ref[head, first_query : first_query + rows] = q_ref[:, lanes]
        all_ref[head, first_query + rows :] = cot_ref[:, lanes]


def run_pack(heads, ids, keys, values, queries, cots):
    rows, features = keys.shape
    shape = (heads, 4 * rows + note_rows, features // heads)
    return pl.pallas_call(
        pack_kernel,
        out_shape=jax.ShapeDtypeStruct(shape, jnp.bfloat16),
        compiler_params=params(56),
        name="pack_heads",
    )(ids, keys, values, queries, cots)


def twice(column):
    return jnp.concatenate([column, column], axis=1)


def wide_as(column, size):
    return column if size == column.shape[1] else twice(column)


def place_of(run, slot, block):
    return pl.multiple_of((2 * run + slot) * block, 64)


def key_spot(first, size):
    return pl.ds(first if isinstance(first, int) else pl.multiple_of(first, 128), size)


def all_chunks(work, some_keys, shared, chunks):
    work(0, some_keys, 0)

    def both(chunk, carry):
        work(some_keys + chunk * k_tile, k_tile, 0)
        return carry

    def upper(chunk, carry):
        work(some_keys + chunk * k_tile, k_tile, 1)
        return carry

    lax.fori_loop(0, shared, both, 0)
    lax.fori_loop(shared, chunks, upper, 0)


def forward_kernel(
    log_ref,
    own_ref,
    kv_ref,
    qc_ref,
    kc_ref,
    vc_ref,
    prob_ref,
    key_ref,
    val_ref,
    query_ref,
    cot_ref,
    num_ref,
    stat_ref,
    shared_ref,
    wide_scr,
    limit_scr,
    sum_scr,
):
    plane, head = seq_place()
    members, tall, width = own_ref.shape
    rows = (tall - note_rows) // 4
    block = 2 * rows
    runs = members // 2
    queries = query_ref.shape[0]
    some_keys = kc_ref.shape[0] // 2
    fine = key_ref.shape[0] - some_keys
    first_query = 2 * rows + note_rows

    def count(notes):
        total = jnp.sum(notes.astype(jnp.float32), axis=0)
        return [jnp.sum(total[level : level + 1]).astype(jnp.int32) for level in range(2)]

    own_counts = count(own_ref[:, 2 * rows : first_query])
    key_counts = [a + b for a, b in zip(own_counts, count(kv_ref[:, 2 * rows :]))]
    query_counts = [a + b for a, b in zip(own_counts, count(qc_ref[:, :note_rows]))]

    def limit_of(place):
        return jnp.where(
            place < query_counts[0],
            key_counts[0],
            jnp.where(place < query_counts[1], key_counts[1], fine),
        )

    own_slot = key_slot(plane)
    for ref, slot in ((own_ref, own_slot), (kv_ref, 1 - own_slot)):
        for run in range(runs):
            pick = slice(2 * run, 2 * run + 2)
            spot = pl.ds(pl.multiple_of(some_keys + place_of(run, slot, block), 64), block)
            key_ref[spot, :] = unit_rows(ref[pick, 0:rows].reshape(block, width))[0].astype(
                jnp.bfloat16
            )
            values = ref[pick, rows : 2 * rows].reshape(block, width)
            val_ref[spot, :] = values
            wide_scr[spot, 0:width] = values
    half = pl.ds(pl.multiple_of(query_slot(plane) * some_keys, some_keys), some_keys)
    key_ref[0:some_keys, :] = kc_ref[half, :]
    val_ref[0:some_keys, :] = vc_ref[half, :]
    wide_scr[0:some_keys, 0:width] = vc_ref[half, :]
    wide_scr[:, width:] = jnp.ones((some_keys + fine, width), jnp.bfloat16)

    own_slot = query_slot(plane)
    for ref, slot, start in ((own_ref, own_slot, first_query), (qc_ref, 1 - own_slot, note_rows)):
        for run in range(runs):
            pick = slice(2 * run, 2 * run + 2)
            spot = pl.ds(place_of(run, slot, block), block)
            query_ref[spot, :] = unit_rows(
                ref[pick, start : start + rows].reshape(block, width)
            )[0].astype(jnp.bfloat16)
            cot_ref[spot, :] = ref[pick, start + rows : start + 2 * rows].reshape(block, width)
    limit_scr[...] = some_keys + limit_of(
        lax.broadcasted_iota(jnp.int32, (queries, width), 0)
    )

    sharp = jnp.exp(jnp.full((1, width), log_ref[head], jnp.float32))[:, 0:1]
    slope = sharp * log2_e
    sum_scr[...] = jnp.zeros_like(sum_scr)

    def probs(start, size, part):
        first = part * queries // 2
        spot = key_spot(start, size)
        cosine = dot_nt(query_ref[first:, :], key_ref[spot, :])
        prob = jnp.exp2(cosine * slope - slope)
        place = start + lax.broadcasted_iota(jnp.int32, (1, size), 1)
        seen = place < wide_as(limit_scr[first:, :], size)
        prob = jnp.where(seen, prob, 0.0).astype(jnp.bfloat16)
        prob_ref[first:, spot] = prob
        sum_scr[first:, :] += dot_nn(prob, wide_scr[spot, :])

    shared = (limit_of(queries // 2 - 1) + k_tile - 1) // k_tile
    shared_ref[0] = shared
    all_chunks(probs, some_keys, shared, fine // k_tile)

    num = sum_scr[:, :width]
    num_ref[...] = num
    weighted = jnp.sum(num * cot_ref[...].astype(jnp.float32), axis=-1, keepdims=True)
    row = lax.broadcasted_iota(jnp.int32, (width, width), 0)
    lane = lax.broadcasted_iota(jnp.int32, (width, width), 1)
    parts = queries // width
    for part in range(parts):
        spot = slice(part * width, (part + 1) * width)
        for index, value in ((part, sum_scr[spot, width:]), (parts + part, weighted[spot])):
            stat_ref[index : index + 1, :] = jnp.sum(
                jnp.where(row == lane, value, 0.0), axis=0, keepdims=True
            )


def backward_kernel(
    log_ref,
    shared_ref,
    own_ref,
    qc_ref,
    stat_ref,
    other_stat_ref,
    prob_ref,
    key_ref,
    val_ref,
    query_ref,
    cot_ref,
    num_ref,
    coarse_scale_ref,
    od_ref,
    od_send_ref,
    dkv_ref,
    dkv_send_ref,
    small_ref,
    den_scr,
    mean_scr,
    grad_scr,
    query_turn,
    cot_turn,
    turn_scr,
):
    plane, head = seq_place()
    members, tall, width = own_ref.shape
    rows = (tall - note_rows) // 4
    block = 2 * rows
    runs = members // 2
    queries = query_ref.shape[0]
    first_query = 2 * rows + note_rows
    some_keys = small_ref.shape[0] - note_rows
    fine = key_ref.shape[0] - some_keys
    sharp = jnp.exp(jnp.full((1, width), log_ref[head], jnp.float32))[:, 0:1]

    row = lax.broadcasted_iota(jnp.int32, (width, width), 0)
    lane = lax.broadcasted_iota(jnp.int32, (width, width), 1)
    parts = queries // width

    def column(index):
        values = stat_ref[index : index + 1, :] + other_stat_ref[index : index + 1, :]
        return jnp.sum(jnp.where(row == lane, values, 0.0), axis=1, keepdims=True)

    for part in range(parts):
        spot = slice(part * width, (part + 1) * width)
        r_den = 1.0 / column(part)
        den_scr[spot, :] = jnp.broadcast_to(r_den, (width, width))
        mean_scr[spot, :] = jnp.broadcast_to(column(parts + part) * r_den, (width, width))

    grad_scr[...] = jnp.zeros_like(grad_scr)
    query_turn[...] = jnp.transpose(
        query_ref[...].astype(jnp.float32) * (den_scr[...] * sharp)
    ).astype(jnp.bfloat16)
    cot_turn[...] = jnp.transpose(cot_ref[...].astype(jnp.float32) * den_scr[...]).astype(
        jnp.bfloat16
    )

    def grads(start, size, part):
        first = part * queries // 2
        spot = key_spot(start, size)
        prob = prob_ref[first:, spot]
        dprob = dot_nt(cot_ref[first:, :], val_ref[spot, :])
        dscore = prob.astype(jnp.float32) * (dprob - wide_as(mean_scr[first:, :], size))
        dscore = dscore.astype(jnp.bfloat16)
        grad_scr[first:, :] += dot_nn(dscore, key_ref[spot, :])
        dk = dot_nn(query_turn[:, first:], dscore)
        dv = dot_nn(cot_turn[:, first:], prob)
        turn_scr[spot, 0:width] = jnp.transpose(dk).astype(jnp.bfloat16)
        turn_scr[spot, width:] = jnp.transpose(dv).astype(jnp.bfloat16)

    all_chunks(grads, some_keys, shared_ref[0], fine // k_tile)

    own_slot = query_slot(plane)
    scale = coarse_scale_ref[pl.ds(pl.multiple_of(head * 8, 8), 8), :]
    scale = scale * jnp.where(plane == 0, 1.0, 0.0)
    for ref, slot, start, target in (
        (own_ref, own_slot, first_query, od_ref),
        (qc_ref, 1 - own_slot, note_rows, od_send_ref),
    ):
        for run in range(runs):
            spot = pl.ds(place_of(run, slot, block), block)
            pick = ref[2 * run : 2 * run + 2, start : start + rows]
            q_dir, q_inv = unit_rows(pick.reshape(block, width))
            r_den = den_scr[spot, :]
            grad = grad_scr[spot, :] * (r_den * sharp)
            along = jnp.sum(q_dir * grad, axis=-1, keepdims=True)
            scale = scale + fold_rows(query_ref[spot, :].astype(jnp.float32) * grad)
            to = slice(run * block, (run + 1) * block)
            target[to, 0:width] = (num_ref[spot, :] * r_den).astype(jnp.bfloat16)
            target[to, width:] = (q_inv * (grad - q_dir * along)).astype(jnp.bfloat16)

    own_slot = key_slot(plane)
    for slot, target in ((own_slot, dkv_ref), (1 - own_slot, dkv_send_ref)):
        for run in range(runs):
            spot = pl.ds(pl.multiple_of(some_keys + place_of(run, slot, block), 64), block)
            target[run * block : (run + 1) * block, :] = turn_scr[spot, :]
    small_ref[0:some_keys, :] = turn_scr[0:some_keys, :]
    small_ref[some_keys:, :] = in_pieces(sum_all(scale), 2 * width)


def run_fine(log_scale, own_rows, kv_rows, qc_rows, key_coarse, val_coarse, coarse_scale, swap):
    members, tall, width = own_rows.shape
    rows = (tall - note_rows) // 4
    some_keys = key_coarse.shape[0] // 2
    queries = 2 * members * rows
    total = some_keys + queries
    vmem = pl.BlockSpec(memory_space=pltpu.VMEM)
    smem = pl.BlockSpec(memory_space=pltpu.SMEM)

    def low(*shape):
        return jax.ShapeDtypeStruct(shape, jnp.bfloat16)

    def wide(*shape):
        return jax.ShapeDtypeStruct(shape, jnp.float32)

    prob, keys, values, query, cot, num, stat, shared = pl.pallas_call(
        forward_kernel,
        out_shape=(
            low(queries, total),
            low(total, width),
            low(total, width),
            low(queries, width),
            low(queries, width),
            wide(queries, width),
            wide(2 * queries // width, width),
            jax.ShapeDtypeStruct((1,), jnp.int32),
        ),
        in_specs=[smem] + [vmem] * 5,
        out_specs=(vmem,) * 7 + (smem,),
        scratch_shapes=[
            pltpu.VMEM((total, 2 * width), jnp.bfloat16),
            pltpu.VMEM((queries, width), jnp.int32),
            pltpu.VMEM((queries, 2 * width), jnp.float32),
        ],
        compiler_params=params(16),
        cost_estimate=pl.CostEstimate(
            flops=4 * queries * total * width,
            bytes_accessed=4 * queries * total,
            transcendentals=queries * total,
        ),
        name="fine_forward",
    )(log_scale, own_rows, kv_rows, qc_rows, key_coarse, val_coarse)
    other_stat = swap(stat)
    half = low(queries // 2, 2 * width)
    return pl.pallas_call(
        backward_kernel,
        out_shape=(half, half, half, half, low(some_keys + note_rows, 2 * width)),
        in_specs=[smem, smem] + [vmem] * 11,
        out_specs=(vmem,) * 5,
        scratch_shapes=[
            pltpu.VMEM((queries, width), jnp.float32),
            pltpu.VMEM((queries, width), jnp.float32),
            pltpu.VMEM((queries, width), jnp.float32),
            pltpu.VMEM((width, queries), jnp.bfloat16),
            pltpu.VMEM((width, queries), jnp.bfloat16),
            pltpu.VMEM((total, 2 * width), jnp.bfloat16),
        ],
        compiler_params=params(16),
        cost_estimate=pl.CostEstimate(
            flops=8 * queries * total * width,
            bytes_accessed=4 * queries * total,
            transcendentals=0,
        ),
        name="fine_backward",
    )(
        log_scale,
        shared,
        own_rows,
        qc_rows,
        stat,
        other_stat,
        prob,
        keys,
        values,
        query,
        cot,
        num,
        coarse_scale,
    )


def coarse_kernel(
    log_ref,
    row_level_ref,
    col_level_ref,
    q_ref,
    k_ref,
    v_ref,
    cot_ref,
    out_ref,
    dq_ref,
    dk_ref,
    dv_ref,
    scale_ref,
    key_low_ref,
    value_ref,
):
    _, own = seq_place()
    count, features = q_ref.shape
    heads = log_ref.shape[0]
    width = features // heads
    visible = col_level_ref[...] <= row_level_ref[...]
    for head in range(heads):
        lanes = slice(head * width, (head + 1) * width)
        sharp = jnp.exp(jnp.full((1, width), log_ref[head], jnp.float32))[:, 0:1]
        slope = sharp * log2_e
        q_dir, q_inv = unit_rows(q_ref[:, lanes])
        q_low = q_dir.astype(jnp.bfloat16)
        key_low = unit_rows(k_ref[:, lanes])[0].astype(jnp.bfloat16)
        values = v_ref[:, lanes]
        cot = cot_ref[:, lanes]
        prob = jnp.exp2(dot_nt(q_low, key_low) * slope - slope)
        prob = jnp.where(visible, prob, 0.0)
        r_den = 1.0 / jnp.sum(prob, axis=-1, keepdims=True)
        norm_prob = prob * r_den
        dprob = dot_nt(cot, values)
        mean = jnp.sum(norm_prob * dprob, axis=-1, keepdims=True)
        dscore = (norm_prob * (dprob - mean)).astype(jnp.bfloat16)
        norm_low = norm_prob.astype(jnp.bfloat16)
        out_ref[:, lanes] = dot_nn(norm_low, values).astype(jnp.bfloat16)
        grad = sharp * dot_nn(dscore, key_low)
        along = jnp.sum(q_dir * grad, axis=-1, keepdims=True)
        dq_ref[:, lanes] = (q_inv * (grad - q_dir * along)).astype(jnp.bfloat16)
        scale_ref[head * 8 : head * 8 + 8, :] = fold_rows(q_low.astype(jnp.float32) * grad)
        q_turned = jnp.transpose(q_dir).astype(jnp.bfloat16)
        cot_turned = jnp.transpose(cot.astype(jnp.float32)).astype(jnp.bfloat16)
        dk_ref[:, lanes] = sharp * jnp.transpose(dot_nn(q_turned, dscore))
        dv_ref[:, lanes] = jnp.transpose(dot_nn(cot_turned, norm_low))

        @pl.when(own == head)
        def _():
            key_low_ref[...] = key_low
            value_ref[...] = values


def run_coarse(log_scale, levels, queries, keys, values, cots):
    count, features = queries.shape
    heads = log_scale.shape[0]
    width = features // heads
    vmem = pl.BlockSpec(memory_space=pltpu.VMEM)
    wide = jax.ShapeDtypeStruct((count, features), jnp.float32)
    low = jax.ShapeDtypeStruct((count, features), jnp.bfloat16)
    return pl.pallas_call(
        coarse_kernel,
        out_shape=(low, low, wide, wide, jax.ShapeDtypeStruct((heads * 8, width), jnp.float32))
        + (jax.ShapeDtypeStruct((count, width), jnp.bfloat16),) * 2,
        in_specs=[pl.BlockSpec(memory_space=pltpu.SMEM)] + [vmem] * 6,
        compiler_params=params(14),
        cost_estimate=pl.CostEstimate(
            flops=12 * count * count * features,
            bytes_accessed=24 * count * features,
            transcendentals=heads * count * count,
        ),
        name="coarse_attention",
    )(log_scale, levels[:, None], levels[None, :], queries, keys, values, cots)


def small_kernel(own_ref, near_ref, across_ref, far_ref, sum_ref, scale_ref):
    plane, _ = seq_place()
    some_keys = own_ref.shape[0] - note_rows
    terms = [ref[...].astype(jnp.float32) for ref in (own_ref, near_ref, across_ref, far_ref)]
    half = query_slot(plane)
    for place, pair in ((half, terms[:2]), (1 - half, terms[2:])):
        spot = pl.ds(pl.multiple_of(place * some_keys, some_keys), some_keys)
        sum_ref[spot, :] = (pair[0][:some_keys] + pair[1][:some_keys]).astype(jnp.bfloat16)
    scale = terms[0][some_keys:] + terms[1][some_keys:] + terms[2][some_keys:] + terms[3][some_keys:]
    scale = jnp.sum(scale[:, : scale_ref.shape[1]], axis=0, keepdims=True)
    scale_ref[...] = jnp.broadcast_to(scale, scale_ref.shape)


def run_small(terms):
    tall, both = terms[0].shape
    return pl.pallas_call(
        small_kernel,
        out_shape=(
            jax.ShapeDtypeStruct((2 * (tall - note_rows), both), jnp.bfloat16),
            jax.ShapeDtypeStruct((8, both // 2), jnp.float32),
        ),
        compiler_params=params(2),
        name="sum_coarse_terms",
    )(*terms)


def sum_kernel(
    od_ref, other_od_ref, dkv_ref, other_dkv_ref, own_ref, scale_ref, other_scale_ref, all_ref
):
    members, tall, width = all_ref.shape
    rows = (tall - note_rows) // 4
    fine = members * rows

    def put(place, value):
        all_ref[:, place * rows : (place + 1) * rows] = value.astype(jnp.bfloat16).reshape(
            members, rows, width
        )

    summed = od_ref[...].astype(jnp.float32) + other_od_ref[...].astype(jnp.float32)
    put(0, summed[:, :width])
    put(1, summed[:, width:])
    summed = dkv_ref[...].astype(jnp.float32) + other_dkv_ref[...].astype(jnp.float32)
    put(2, project(own_ref[:, 0:rows].reshape(fine, width), summed[:, :width]))
    put(3, summed[:, width:])
    note = in_pieces(scale_ref[0:1, 0:1] + other_scale_ref[0:1, 0:1], width)
    for member in range(members):
        all_ref[member, 4 * rows :] = note


def run_sum(od, other_od, dkv, other_dkv, own_rows, scale, other_scale):
    return pl.pallas_call(
        sum_kernel,
        out_shape=jax.ShapeDtypeStruct(own_rows.shape, jnp.bfloat16),
        compiler_params=params(6),
        name="sum_pairs",
    )(od, other_od, dkv, other_dkv, own_rows, scale, other_scale)


def join_kernel(terms_ref, dk_own_ref, dv_own_ref, k_ref, dk_ref, dv_ref, last_ref):
    heads, _, both = terms_ref.shape
    width = both // 2
    for head in range(heads):
        lanes = slice(head * width, (head + 1) * width)
        terms = terms_ref[head].astype(jnp.float32)
        grad = terms[:, :width] + dk_own_ref[:, lanes]
        dk_ref[:, lanes] = project(k_ref[:, lanes], grad).astype(jnp.bfloat16)
        dv_ref[:, lanes] = (terms[:, width:] + dv_own_ref[:, lanes]).astype(jnp.bfloat16)
    last_ref[...] = jnp.zeros_like(last_ref)


def run_join(terms, dk_own, dv_own, keys):
    low = jax.ShapeDtypeStruct(keys.shape, jnp.bfloat16)
    return pl.pallas_call(
        join_kernel,
        out_shape=(low, low, jax.ShapeDtypeStruct((8, 128), jnp.float32)),
        compiler_params=params(8),
        name="join_coarse",
    )(terms, dk_own, dv_own, keys)


def unpack_kernel(factor, all_ref, _, out_ref, dq_ref, dk_ref, dv_ref, scale_ref):
    heads, tall, width = all_ref.shape
    rows = (tall - note_rows) // 4
    for head in range(heads):
        lanes = slice(head * width, (head + 1) * width)
        for place, ref in enumerate((out_ref, dq_ref, dk_ref, dv_ref)):
            ref[:, lanes] = all_ref[head, place * rows : (place + 1) * rows]
        note = all_ref[head, 4 * rows :].astype(jnp.float32)
        scale_ref[head] = jnp.sum(note[:, 0:1]) * factor


def run_unpack(factor, all_back, after):
    heads, tall, width = all_back.shape
    flat = jax.ShapeDtypeStruct(((tall - note_rows) // 4, heads * width), jnp.bfloat16)
    vmem = pl.BlockSpec(memory_space=pltpu.VMEM)
    return pl.pallas_call(
        partial(unpack_kernel, factor),
        out_shape=(flat,) * 4 + (jax.ShapeDtypeStruct((heads,), jnp.float32),),
        in_specs=[vmem, vmem],
        out_specs=(vmem,) * 4 + (pl.BlockSpec(memory_space=pltpu.SMEM),),
        compiler_params=params(3),
        name="unpack_heads",
    )(all_back, after)


def body(
    q_coarse,
    k_coarse,
    v_coarse,
    cot_coarse,
    coarse_ids,
    q_fine,
    k_fine,
    v_fine,
    cot_fine,
    fine_ids,
    log_scale,
):
    heads = log_scale.shape[0]
    coarse = q_coarse.shape[1]
    rows = q_fine.shape[1]
    seq = lax.axis_size("seq")
    images = lax.axis_size("dp")
    groups = [
        [8 * (h // 2) + 2 * plane + h % 2 for h in range(heads)] for plane in range(planes)
    ]

    def exchange(parts):
        return lax.all_to_all(parts, "seq", 0, 0, axis_index_groups=groups, tiled=True)

    def to_plane(array, flip):
        return lax.ppermute(array, "seq", [(i, i ^ (2 * flip)) for i in range(seq)])

    def to_image(array, flip):
        return lax.ppermute(array, "dp", [(i, i ^ flip) for i in range(images)])

    own_rows = exchange(run_pack(heads, fine_ids, k_fine[0], v_fine[0], q_fine[0], cot_fine[0]))
    kv_rows = to_plane(own_rows[:, : 2 * rows + note_rows], 1)
    qc_rows = to_plane(own_rows[:, 2 * rows :], 3)

    out_c, dq_c, dk_own, dv_own, scale_c, key_c, val_c = run_coarse(
        log_scale, coarse_ids[0], q_coarse[0], k_coarse[0], v_coarse[0], cot_coarse[0]
    )
    od, od_send, dkv, dkv_send, small = run_fine(
        log_scale, own_rows, kv_rows, qc_rows, key_c, val_c, scale_c, lambda stat: to_plane(stat, 3)
    )

    small_sum, scale = run_small([small] + [to_plane(small, flip) for flip in (1, 2, 3)])
    of_image = lax.all_gather(small_sum, "seq", axis=0, axis_index_groups=groups)

    other_dkv = to_plane(dkv_send, 1)
    other_od = to_plane(od_send, 3)
    for flip in (1, 2):
        scale = scale + to_image(scale, flip)
    all_parts = run_sum(od, other_od, dkv, other_dkv, own_rows, scale, to_image(scale, 4))
    all_back = exchange(all_parts)
    dk_c, dv_c, after = run_join(of_image, dk_own, dv_own, k_coarse[0])
    factor = 1.0 / math.sqrt(images * (coarse + seq * rows))
    fine_out, fine_dq, fine_dk, fine_dv, grad_scale = run_unpack(factor, all_back, after)
    return (
        out_c[None],
        dq_c[None],
        dk_c[None],
        dv_c[None],
        fine_out[None],
        fine_dq[None],
        fine_dk[None],
        fine_dv[None],
        grad_scale,
    )


def solution(mesh):
    whole = P("dp", None, None)
    split = P("dp", "seq", None)
    return jax.shard_map(
        body,
        mesh=mesh,
        in_specs=(whole,) * 4 + (P("dp", None),) + (split,) * 4 + (P("dp", "seq"), P()),
        out_specs=(whole,) * 4 + (split,) * 4 + (P(),),
        check_vma=False,
    )
```

```python
import math
from functools import partial

import jax
import jax.numpy as jnp
from jax import lax
from jax.experimental import pallas as pl
from jax.experimental.pallas import tpu as pltpu
from jax.sharding import PartitionSpec as P

norm_eps = 1e-06
log2_e = 1.4426950408889634
k_tile = 256
note_rows = 16

planes = 4


def dot_nt(left, right):
    return lax.dot_general(
        left, right, (((1,), (1,)), ((), ())), preferred_element_type=jnp.float32
    )


def dot_nn(left, right):
    return jnp.dot(left, right, preferred_element_type=jnp.float32)


def unit_rows(rows):
    wide = rows.astype(jnp.float32)
    inv_norm = lax.rsqrt(jnp.sum(wide * wide, axis=-1, keepdims=True) + norm_eps)
    return wide * inv_norm, inv_norm


def project(key_rows, grad):
    key_dir, key_inv = unit_rows(key_rows)
    along = jnp.sum(key_dir * grad, axis=-1, keepdims=True)
    return key_inv * (grad - key_dir * along)


def fold_rows(terms):
    rows, width = terms.shape
    return jnp.sum(terms.reshape(rows // 8, 8, width), axis=0)


def in_pieces(value, width):
    row = lax.broadcasted_iota(jnp.int32, (note_rows, width), 0)
    note = jnp.zeros((note_rows, width), jnp.float32)
    for part in range(3):
        piece = value.astype(jnp.bfloat16).astype(jnp.float32)
        note = jnp.where(row == part, piece, note)
        value = value - piece
    return note.astype(jnp.bfloat16)


def sum_all(terms):
    return jnp.sum(jnp.sum(terms, axis=0, keepdims=True), axis=-1, keepdims=True)


def seq_place():
    here = lax.axis_index("seq")
    plane = lax.bitwise_and(lax.shift_right_logical(here, 1), 3)
    head = 2 * lax.shift_right_logical(here, 3) + lax.bitwise_and(here, 1)
    return plane, head


def key_slot(plane):
    return lax.bitwise_and(plane, 1)


def query_slot(plane):
    return lax.shift_right_logical(plane, 1)


def params(mebibytes):
    return pltpu.CompilerParams(vmem_limit_bytes=mebibytes * 1024 * 1024)


def pack_kernel(ids_ref, k_ref, v_ref, q_ref, cot_ref, all_ref):
    heads, _, width = all_ref.shape
    rows = k_ref.shape[0]
    ids = ids_ref[...]
    row = lax.broadcasted_iota(jnp.int32, (note_rows, width), 0)
    lane = lax.broadcasted_iota(jnp.int32, (note_rows, width), 1)
    note = jnp.zeros((note_rows, width), jnp.float32)
    for level in range(2):
        count = jnp.sum(jnp.where(ids <= level, 1.0, 0.0), axis=-1, keepdims=True)
        note = jnp.where((row == level) & (lane == 0), count, note)
    note = note.astype(jnp.bfloat16)
    first_query = 2 * rows + note_rows
    for head in range(heads):
        lanes = slice(head * width, (head + 1) * width)
        all_ref[head, 0:rows] = k_ref[:, lanes]
        all_ref[head, rows : 2 * rows] = v_ref[:, lanes]
        all_ref[head, 2 * rows : first_query] = note
        all_ref[head, first_query : first_query + rows] = q_ref[:, lanes]
        all_ref[head, first_query + rows :] = cot_ref[:, lanes]


def run_pack(heads, ids, keys, values, queries, cots):
    rows, features = keys.shape
    shape = (heads, 4 * rows + note_rows, features // heads)
    return pl.pallas_call(
        pack_kernel,
        out_shape=jax.ShapeDtypeStruct(shape, jnp.bfloat16),
        compiler_params=params(56),
        name="pack_heads",
    )(ids, keys, values, queries, cots)


def twice(column):
    return jnp.concatenate([column, column], axis=1)


def wide_as(column, size):
    return column if size == column.shape[1] else twice(column)


def place_of(run, slot, block):
    return pl.multiple_of((2 * run + slot) * block, 64)


def key_spot(first, size):
    return pl.ds(first if isinstance(first, int) else pl.multiple_of(first, 128), size)


def all_chunks(work, some_keys, shared, chunks):
    work(0, some_keys, 0)

    def both(chunk, carry):
        work(some_keys + chunk * k_tile, k_tile, 0)
        return carry

    def upper(chunk, carry):
        work(some_keys + chunk * k_tile, k_tile, 1)
        return carry

    lax.fori_loop(0, shared, both, 0)
    lax.fori_loop(shared, chunks, upper, 0)


def forward_kernel(
    log_ref,
    own_ref,
    kv_ref,
    qc_ref,
    kc_ref,
    vc_ref,
    prob_ref,
    key_ref,
    val_ref,
    query_ref,
    cot_ref,
    num_ref,
    stat_ref,
    shared_ref,
    wide_scr,
    limit_scr,
    sum_scr,
):
    plane, head = seq_place()
    members, tall, width = own_ref.shape
    rows = (tall - note_rows) // 4
    block = 2 * rows
    runs = members // 2
    queries = query_ref.shape[0]
    some_keys = kc_ref.shape[0] // 2
    fine = key_ref.shape[0] - some_keys
    first_query = 2 * rows + note_rows

    def count(notes):
        total = jnp.sum(notes.astype(jnp.float32), axis=0)
        return [jnp.sum(total[level : level + 1]).astype(jnp.int32) for level in range(2)]

    own_counts = count(own_ref[:, 2 * rows : first_query])
    key_counts = [a + b for a, b in zip(own_counts, count(kv_ref[:, 2 * rows :]))]
    query_counts = [a + b for a, b in zip(own_counts, count(qc_ref[:, :note_rows]))]

    def limit_of(place):
        return jnp.where(
            place < query_counts[0],
            key_counts[0],
            jnp.where(place < query_counts[1], key_counts[1], fine),
        )

    own_slot = key_slot(plane)
    for ref, slot in ((own_ref, own_slot), (kv_ref, 1 - own_slot)):
        for run in range(runs):
            pick = slice(2 * run, 2 * run + 2)
            spot = pl.ds(pl.multiple_of(some_keys + place_of(run, slot, block), 64), block)
            key_ref[spot, :] = unit_rows(ref[pick, 0:rows].reshape(block, width))[0].astype(
                jnp.bfloat16
            )
            values = ref[pick, rows : 2 * rows].reshape(block, width)
            val_ref[spot, :] = values
            wide_scr[spot, 0:width] = values
    half = pl.ds(pl.multiple_of(query_slot(plane) * some_keys, some_keys), some_keys)
    key_ref[0:some_keys, :] = kc_ref[half, :]
    val_ref[0:some_keys, :] = vc_ref[half, :]
    wide_scr[0:some_keys, 0:width] = vc_ref[half, :]
    wide_scr[:, width:] = jnp.ones((some_keys + fine, width), jnp.bfloat16)

    own_slot = query_slot(plane)
    for ref, slot, start in ((own_ref, own_slot, first_query), (qc_ref, 1 - own_slot, note_rows)):
        for run in range(runs):
            pick = slice(2 * run, 2 * run + 2)
            spot = pl.ds(place_of(run, slot, block), block)
            query_ref[spot, :] = unit_rows(
                ref[pick, start : start + rows].reshape(block, width)
            )[0].astype(jnp.bfloat16)
            cot_ref[spot, :] = ref[pick, start + rows : start + 2 * rows].reshape(block, width)
    limit_scr[...] = some_keys + limit_of(
        lax.broadcasted_iota(jnp.int32, (queries, width), 0)
    )

    sharp = jnp.exp(jnp.full((1, width), log_ref[head], jnp.float32))[:, 0:1]
    slope = sharp * log2_e
    sum_scr[...] = jnp.zeros_like(sum_scr)

    def probs(start, size, part):
        first = part * queries // 2
        spot = key_spot(start, size)
        cosine = dot_nt(query_ref[first:, :], key_ref[spot, :])
        prob = jnp.exp2(cosine * slope - slope)
        place = start + lax.broadcasted_iota(jnp.int32, (1, size), 1)
        seen = place < wide_as(limit_scr[first:, :], size)
        prob = jnp.where(seen, prob, 0.0).astype(jnp.bfloat16)
        prob_ref[first:, spot] = prob
        sum_scr[first:, :] += dot_nn(prob, wide_scr[spot, :])

    shared = (limit_of(queries // 2 - 1) + k_tile - 1) // k_tile
    shared_ref[0] = shared
    all_chunks(probs, some_keys, shared, fine // k_tile)

    num = sum_scr[:, :width]
    num_ref[...] = num
    weighted = jnp.sum(num * cot_ref[...].astype(jnp.float32), axis=-1, keepdims=True)
    row = lax.broadcasted_iota(jnp.int32, (width, width), 0)
    lane = lax.broadcasted_iota(jnp.int32, (width, width), 1)
    parts = queries // width
    for part in range(parts):
        spot = slice(part * width, (part + 1) * width)
        for index, value in ((part, sum_scr[spot, width:]), (parts + part, weighted[spot])):
            stat_ref[index : index + 1, :] = jnp.sum(
                jnp.where(row == lane, value, 0.0), axis=0, keepdims=True
            )


def backward_kernel(
    log_ref,
    shared_ref,
    own_ref,
    qc_ref,
    stat_ref,
    other_stat_ref,
    prob_ref,
    key_ref,
    val_ref,
    query_ref,
    cot_ref,
    num_ref,
    coarse_scale_ref,
    od_ref,
    od_send_ref,
    dkv_ref,
    dkv_send_ref,
    small_ref,
    den_scr,
    mean_scr,
    grad_scr,
    query_turn,
    cot_turn,
    turn_scr,
    od_scr,
    sems,
):
    plane, head = seq_place()
    members, tall, width = own_ref.shape
    rows = (tall - note_rows) // 4
    block = 2 * rows
    runs = members // 2
    queries = query_ref.shape[0]
    first_query = 2 * rows + note_rows
    some_keys = small_ref.shape[0] - note_rows
    fine = key_ref.shape[0] - some_keys
    sharp = jnp.exp(jnp.full((1, width), log_ref[head], jnp.float32))[:, 0:1]

    row = lax.broadcasted_iota(jnp.int32, (width, width), 0)
    lane = lax.broadcasted_iota(jnp.int32, (width, width), 1)
    parts = queries // width

    def column(index):
        values = stat_ref[index : index + 1, :] + other_stat_ref[index : index + 1, :]
        return jnp.sum(jnp.where(row == lane, values, 0.0), axis=1, keepdims=True)

    for part in range(parts):
        spot = slice(part * width, (part + 1) * width)
        r_den = 1.0 / column(part)
        den_scr[spot, :] = jnp.broadcast_to(r_den, (width, width))
        mean_scr[spot, :] = jnp.broadcast_to(column(parts + part) * r_den, (width, width))

    grad_scr[...] = jnp.zeros_like(grad_scr)
    query_turn[...] = jnp.transpose(
        query_ref[...].astype(jnp.float32) * (den_scr[...] * sharp)
    ).astype(jnp.bfloat16)
    cot_turn[...] = jnp.transpose(cot_ref[...].astype(jnp.float32) * den_scr[...]).astype(
        jnp.bfloat16
    )

    def grads(start, size, part):
        first = part * queries // 2
        spot = key_spot(start, size)
        prob = prob_ref[first:, spot]
        dprob = dot_nt(cot_ref[first:, :], val_ref[spot, :])
        dscore = prob.astype(jnp.float32) * (dprob - wide_as(mean_scr[first:, :], size))
        dscore = dscore.astype(jnp.bfloat16)
        grad_scr[first:, :] += dot_nn(dscore, key_ref[spot, :])
        dk = dot_nn(query_turn[:, first:], dscore)
        dv = dot_nn(cot_turn[:, first:], prob)
        turn_scr[spot, 0:width] = jnp.transpose(dk).astype(jnp.bfloat16)
        turn_scr[spot, width:] = jnp.transpose(dv).astype(jnp.bfloat16)

    all_chunks(grads, some_keys, shared_ref[0], fine // k_tile)

    copies = []

    def send(source, target):
        copies.append(pltpu.make_async_copy(source, target, sems.at[len(copies)]))
        copies[-1].start()

    own_slot = key_slot(plane)
    for slot, target in ((1 - own_slot, dkv_send_ref), (own_slot, dkv_ref)):
        for run in range(runs):
            spot = pl.ds(pl.multiple_of(some_keys + place_of(run, slot, block), 64), block)
            send(turn_scr.at[spot, :], target.at[run * block : (run + 1) * block, :])

    own_slot = query_slot(plane)
    scale = coarse_scale_ref[pl.ds(pl.multiple_of(head * 8, 8), 8), :]
    scale = scale * jnp.where(plane == 0, 1.0, 0.0)
    for index, (ref, slot, start, target) in enumerate(
        (
            (qc_ref, 1 - own_slot, note_rows, od_send_ref),
            (own_ref, own_slot, first_query, od_ref),
        )
    ):
        for run in range(runs):
            spot = pl.ds(place_of(run, slot, block), block)
            pick = ref[2 * run : 2 * run + 2, start : start + rows]
            q_dir, q_inv = unit_rows(pick.reshape(block, width))
            r_den = den_scr[spot, :]
            grad = grad_scr[spot, :] * (r_den * sharp)
            along = jnp.sum(q_dir * grad, axis=-1, keepdims=True)
            scale = scale + fold_rows(query_ref[spot, :].astype(jnp.float32) * grad)
            to = slice(run * block, (run + 1) * block)
            od_scr[index, to, 0:width] = (num_ref[spot, :] * r_den).astype(jnp.bfloat16)
            od_scr[index, to, width:] = (q_inv * (grad - q_dir * along)).astype(jnp.bfloat16)
        send(od_scr.at[index], target)
    small_ref[0:some_keys, :] = turn_scr[0:some_keys, :]
    small_ref[some_keys:, :] = in_pieces(sum_all(scale), 2 * width)
    for copy in copies:
        copy.wait()


def run_fine(log_scale, own_rows, kv_rows, qc_rows, key_coarse, val_coarse, coarse_scale, swap):
    members, tall, width = own_rows.shape
    rows = (tall - note_rows) // 4
    some_keys = key_coarse.shape[0] // 2
    queries = 2 * members * rows
    total = some_keys + queries
    vmem = pl.BlockSpec(memory_space=pltpu.VMEM)
    smem = pl.BlockSpec(memory_space=pltpu.SMEM)

    def low(*shape):
        return jax.ShapeDtypeStruct(shape, jnp.bfloat16)

    def wide(*shape):
        return jax.ShapeDtypeStruct(shape, jnp.float32)

    prob, keys, values, query, cot, num, stat, shared = pl.pallas_call(
        forward_kernel,
        out_shape=(
            low(queries, total),
            low(total, width),
            low(total, width),
            low(queries, width),
            low(queries, width),
            wide(queries, width),
            wide(2 * queries // width, width),
            jax.ShapeDtypeStruct((1,), jnp.int32),
        ),
        in_specs=[smem] + [vmem] * 5,
        out_specs=(vmem,) * 7 + (smem,),
        scratch_shapes=[
            pltpu.VMEM((total, 2 * width), jnp.bfloat16),
            pltpu.VMEM((queries, width), jnp.int32),
            pltpu.VMEM((queries, 2 * width), jnp.float32),
        ],
        compiler_params=params(16),
        cost_estimate=pl.CostEstimate(
            flops=4 * queries * total * width,
            bytes_accessed=4 * queries * total,
            transcendentals=queries * total,
        ),
        name="fine_forward",
    )(log_scale, own_rows, kv_rows, qc_rows, key_coarse, val_coarse)
    other_stat = swap(stat)
    half = low(queries // 2, 2 * width)
    return pl.pallas_call(
        backward_kernel,
        out_shape=(half, half, half, half, low(some_keys + note_rows, 2 * width)),
        in_specs=[smem, smem] + [vmem] * 11,
        out_specs=(pl.BlockSpec(memory_space=pltpu.HBM),) * 4 + (vmem,),
        scratch_shapes=[
            pltpu.VMEM((queries, width), jnp.float32),
            pltpu.VMEM((queries, width), jnp.float32),
            pltpu.VMEM((queries, width), jnp.float32),
            pltpu.VMEM((width, queries), jnp.bfloat16),
            pltpu.VMEM((width, queries), jnp.bfloat16),
            pltpu.VMEM((total, 2 * width), jnp.bfloat16),
            pltpu.VMEM((2, queries // 2, 2 * width), jnp.bfloat16),
            pltpu.SemaphoreType.DMA((members + 2,)),
        ],
        compiler_params=params(16),
        cost_estimate=pl.CostEstimate(
            flops=8 * queries * total * width,
            bytes_accessed=4 * queries * total,
            transcendentals=0,
        ),
        name="fine_backward",
    )(
        log_scale,
        shared,
        own_rows,
        qc_rows,
        stat,
        other_stat,
        prob,
        keys,
        values,
        query,
        cot,
        num,
        coarse_scale,
    )


def coarse_kernel(
    log_ref,
    row_level_ref,
    col_level_ref,
    q_ref,
    k_ref,
    v_ref,
    cot_ref,
    out_ref,
    dq_ref,
    dk_ref,
    dv_ref,
    scale_ref,
    key_low_ref,
    value_ref,
):
    _, own = seq_place()
    count, features = q_ref.shape
    heads = log_ref.shape[0]
    width = features // heads
    visible = col_level_ref[...] <= row_level_ref[...]
    for head in range(heads):
        lanes = slice(head * width, (head + 1) * width)
        sharp = jnp.exp(jnp.full((1, width), log_ref[head], jnp.float32))[:, 0:1]
        slope = sharp * log2_e
        q_dir, q_inv = unit_rows(q_ref[:, lanes])
        q_low = q_dir.astype(jnp.bfloat16)
        key_low = unit_rows(k_ref[:, lanes])[0].astype(jnp.bfloat16)
        values = v_ref[:, lanes]
        cot = cot_ref[:, lanes]
        prob = jnp.exp2(dot_nt(q_low, key_low) * slope - slope)
        prob = jnp.where(visible, prob, 0.0)
        r_den = 1.0 / jnp.sum(prob, axis=-1, keepdims=True)
        norm_prob = prob * r_den
        dprob = dot_nt(cot, values)
        mean = jnp.sum(norm_prob * dprob, axis=-1, keepdims=True)
        dscore = (norm_prob * (dprob - mean)).astype(jnp.bfloat16)
        norm_low = norm_prob.astype(jnp.bfloat16)
        out_ref[:, lanes] = dot_nn(norm_low, values).astype(jnp.bfloat16)
        grad = sharp * dot_nn(dscore, key_low)
        along = jnp.sum(q_dir * grad, axis=-1, keepdims=True)
        dq_ref[:, lanes] = (q_inv * (grad - q_dir * along)).astype(jnp.bfloat16)
        scale_ref[head * 8 : head * 8 + 8, :] = fold_rows(q_low.astype(jnp.float32) * grad)
        q_turned = jnp.transpose(q_dir).astype(jnp.bfloat16)
        cot_turned = jnp.transpose(cot.astype(jnp.float32)).astype(jnp.bfloat16)
        dk_ref[:, lanes] = sharp * jnp.transpose(dot_nn(q_turned, dscore))
        dv_ref[:, lanes] = jnp.transpose(dot_nn(cot_turned, norm_low))

        @pl.when(own == head)
        def _():
            key_low_ref[...] = key_low
            value_ref[...] = values


def run_coarse(log_scale, levels, queries, keys, values, cots):
    count, features = queries.shape
    heads = log_scale.shape[0]
    width = features // heads
    vmem = pl.BlockSpec(memory_space=pltpu.VMEM)
    wide = jax.ShapeDtypeStruct((count, features), jnp.float32)
    low = jax.ShapeDtypeStruct((count, features), jnp.bfloat16)
    return pl.pallas_call(
        coarse_kernel,
        out_shape=(low, low, wide, wide, jax.ShapeDtypeStruct((heads * 8, width), jnp.float32))
        + (jax.ShapeDtypeStruct((count, width), jnp.bfloat16),) * 2,
        in_specs=[pl.BlockSpec(memory_space=pltpu.SMEM)] + [vmem] * 6,
        compiler_params=params(14),
        cost_estimate=pl.CostEstimate(
            flops=12 * count * count * features,
            bytes_accessed=24 * count * features,
            transcendentals=heads * count * count,
        ),
        name="coarse_attention",
    )(log_scale, levels[:, None], levels[None, :], queries, keys, values, cots)


def small_kernel(own_ref, near_ref, across_ref, far_ref, sum_ref, scale_ref):
    plane, _ = seq_place()
    some_keys = own_ref.shape[0] - note_rows
    terms = [ref[...].astype(jnp.float32) for ref in (own_ref, near_ref, across_ref, far_ref)]
    half = query_slot(plane)
    for place, pair in ((half, terms[:2]), (1 - half, terms[2:])):
        spot = pl.ds(pl.multiple_of(place * some_keys, some_keys), some_keys)
        sum_ref[spot, :] = (pair[0][:some_keys] + pair[1][:some_keys]).astype(jnp.bfloat16)
    scale = terms[0][some_keys:] + terms[1][some_keys:] + terms[2][some_keys:] + terms[3][some_keys:]
    scale = jnp.sum(scale[:, : scale_ref.shape[1]], axis=0, keepdims=True)
    scale_ref[...] = jnp.broadcast_to(scale, scale_ref.shape)


def run_small(terms):
    tall, both = terms[0].shape
    return pl.pallas_call(
        small_kernel,
        out_shape=(
            jax.ShapeDtypeStruct((2 * (tall - note_rows), both), jnp.bfloat16),
            jax.ShapeDtypeStruct((8, both // 2), jnp.float32),
        ),
        compiler_params=params(2),
        name="sum_coarse_terms",
    )(*terms)


def sum_kernel(
    od_hbm,
    other_od_ref,
    dkv_hbm,
    other_dkv_ref,
    own_ref,
    scale_ref,
    other_scale_ref,
    all_ref,
    od_ref,
    dkv_ref,
    sems,
):
    copies = [
        pltpu.make_async_copy(od_hbm, od_ref, sems.at[0]),
        pltpu.make_async_copy(dkv_hbm, dkv_ref, sems.at[1]),
    ]
    for copy in copies:
        copy.start()
    members, tall, width = all_ref.shape
    rows = (tall - note_rows) // 4
    fine = members * rows

    def put(place, value):
        all_ref[:, place * rows : (place + 1) * rows] = value.astype(jnp.bfloat16).reshape(
            members, rows, width
        )

    copies[0].wait()
    summed = od_ref[...].astype(jnp.float32) + other_od_ref[...].astype(jnp.float32)
    put(0, summed[:, :width])
    put(1, summed[:, width:])
    copies[1].wait()
    summed = dkv_ref[...].astype(jnp.float32) + other_dkv_ref[...].astype(jnp.float32)
    put(2, project(own_ref[:, 0:rows].reshape(fine, width), summed[:, :width]))
    put(3, summed[:, width:])
    note = in_pieces(scale_ref[0:1, 0:1] + other_scale_ref[0:1, 0:1], width)
    for member in range(members):
        all_ref[member, 4 * rows :] = note


def run_sum(od, other_od, dkv, other_dkv, own_rows, scale, other_scale):
    vmem = pl.BlockSpec(memory_space=pltpu.VMEM)
    hbm = pl.BlockSpec(memory_space=pltpu.HBM)
    return pl.pallas_call(
        sum_kernel,
        out_shape=jax.ShapeDtypeStruct(own_rows.shape, jnp.bfloat16),
        in_specs=[hbm, vmem, hbm, vmem, vmem, vmem, vmem],
        out_specs=vmem,
        scratch_shapes=[
            pltpu.VMEM(od.shape, jnp.bfloat16),
            pltpu.VMEM(dkv.shape, jnp.bfloat16),
            pltpu.SemaphoreType.DMA((2,)),
        ],
        compiler_params=params(6),
        name="sum_pairs",
    )(od, other_od, dkv, other_dkv, own_rows, scale, other_scale)


def join_kernel(terms_ref, dk_own_ref, dv_own_ref, k_ref, dk_ref, dv_ref, last_ref):
    heads, _, both = terms_ref.shape
    width = both // 2
    for head in range(heads):
        lanes = slice(head * width, (head + 1) * width)
        terms = terms_ref[head].astype(jnp.float32)
        grad = terms[:, :width] + dk_own_ref[:, lanes]
        dk_ref[:, lanes] = project(k_ref[:, lanes], grad).astype(jnp.bfloat16)
        dv_ref[:, lanes] = (terms[:, width:] + dv_own_ref[:, lanes]).astype(jnp.bfloat16)
    last_ref[...] = jnp.zeros_like(last_ref)


def run_join(terms, dk_own, dv_own, keys):
    low = jax.ShapeDtypeStruct(keys.shape, jnp.bfloat16)
    return pl.pallas_call(
        join_kernel,
        out_shape=(low, low, jax.ShapeDtypeStruct((8, 128), jnp.float32)),
        compiler_params=params(8),
        name="join_coarse",
    )(terms, dk_own, dv_own, keys)


def unpack_kernel(factor, all_ref, _, out_ref, dq_ref, dk_ref, dv_ref, scale_ref):
    heads, tall, width = all_ref.shape
    rows = (tall - note_rows) // 4
    for head in range(heads):
        lanes = slice(head * width, (head + 1) * width)
        for place, ref in enumerate((out_ref, dq_ref, dk_ref, dv_ref)):
            ref[:, lanes] = all_ref[head, place * rows : (place + 1) * rows]
        note = all_ref[head, 4 * rows :].astype(jnp.float32)
        scale_ref[head] = jnp.sum(note[:, 0:1]) * factor


def run_unpack(factor, all_back, after):
    heads, tall, width = all_back.shape
    flat = jax.ShapeDtypeStruct(((tall - note_rows) // 4, heads * width), jnp.bfloat16)
    vmem = pl.BlockSpec(memory_space=pltpu.VMEM)
    return pl.pallas_call(
        partial(unpack_kernel, factor),
        out_shape=(flat,) * 4 + (jax.ShapeDtypeStruct((heads,), jnp.float32),),
        in_specs=[vmem, vmem],
        out_specs=(vmem,) * 4 + (pl.BlockSpec(memory_space=pltpu.SMEM),),
        compiler_params=params(3),
        name="unpack_heads",
    )(all_back, after)


def body(
    q_coarse,
    k_coarse,
    v_coarse,
    cot_coarse,
    coarse_ids,
    q_fine,
    k_fine,
    v_fine,
    cot_fine,
    fine_ids,
    log_scale,
):
    heads = log_scale.shape[0]
    coarse = q_coarse.shape[1]
    rows = q_fine.shape[1]
    seq = lax.axis_size("seq")
    images = lax.axis_size("dp")
    groups = [
        [8 * (h // 2) + 2 * plane + h % 2 for h in range(heads)] for plane in range(planes)
    ]

    def exchange(parts):
        return lax.all_to_all(parts, "seq", 0, 0, axis_index_groups=groups, tiled=True)

    def to_plane(array, flip):
        return lax.ppermute(array, "seq", [(i, i ^ (2 * flip)) for i in range(seq)])

    def to_image(array, flip):
        return lax.ppermute(array, "dp", [(i, i ^ flip) for i in range(images)])

    own_rows = exchange(run_pack(heads, fine_ids, k_fine[0], v_fine[0], q_fine[0], cot_fine[0]))
    kv_rows = to_plane(own_rows[:, : 2 * rows + note_rows], 1)
    qc_rows = to_plane(own_rows[:, 2 * rows :], 3)

    out_c, dq_c, dk_own, dv_own, scale_c, key_c, val_c = run_coarse(
        log_scale, coarse_ids[0], q_coarse[0], k_coarse[0], v_coarse[0], cot_coarse[0]
    )
    od, od_send, dkv, dkv_send, small = run_fine(
        log_scale, own_rows, kv_rows, qc_rows, key_c, val_c, scale_c, lambda stat: to_plane(stat, 3)
    )

    small_sum, scale = run_small([small] + [to_plane(small, flip) for flip in (1, 2, 3)])
    of_image = lax.all_gather(small_sum, "seq", axis=0, axis_index_groups=groups)

    other_dkv = to_plane(dkv_send, 1)
    other_od = to_plane(od_send, 3)
    scale = scale + to_image(scale, 1) + to_image(scale, 2) + to_image(scale, 3)
    all_parts = run_sum(od, other_od, dkv, other_dkv, own_rows, scale, to_image(scale, 4))
    all_back = exchange(all_parts)
    dk_c, dv_c, after = run_join(of_image, dk_own, dv_own, k_coarse[0])
    factor = 1.0 / math.sqrt(images * (coarse + seq * rows))
    fine_out, fine_dq, fine_dk, fine_dv, grad_scale = run_unpack(factor, all_back, after)
    return (
        out_c[None],
        dq_c[None],
        dk_c[None],
        dv_c[None],
        fine_out[None],
        fine_dq[None],
        fine_dk[None],
        fine_dv[None],
        grad_scale,
    )


def solution(mesh):
    whole = P("dp", None, None)
    split = P("dp", "seq", None)
    return jax.shard_map(
        body,
        mesh=mesh,
        in_specs=(whole,) * 4 + (P("dp", None),) + (split,) * 4 + (P("dp", "seq"), P()),
        out_specs=(whole,) * 4 + (split,) * 4 + (P(),),
        check_vma=False,
    )
```

```python
import math
from functools import partial

import jax
import jax.numpy as jnp
from jax import lax
from jax.experimental import pallas as pl
from jax.experimental.pallas import tpu as pltpu
from jax.sharding import PartitionSpec as P

norm_eps = 1e-06
log2_e = 1.4426950408889634
k_tile = 256
note_rows = 16

planes = 4


def dot_nt(left, right):
    return lax.dot_general(
        left, right, (((1,), (1,)), ((), ())), preferred_element_type=jnp.float32
    )


def dot_nn(left, right):
    return jnp.dot(left, right, preferred_element_type=jnp.float32)


def unit_rows(rows):
    wide = rows.astype(jnp.float32)
    inv_norm = lax.rsqrt(jnp.sum(wide * wide, axis=-1, keepdims=True) + norm_eps)
    return wide * inv_norm, inv_norm


def project(key_rows, grad):
    key_dir, key_inv = unit_rows(key_rows)
    along = jnp.sum(key_dir * grad, axis=-1, keepdims=True)
    return key_inv * (grad - key_dir * along)


def fold_rows(terms):
    rows, width = terms.shape
    return jnp.sum(terms.reshape(rows // 8, 8, width), axis=0)


def in_pieces(value, width):
    row = lax.broadcasted_iota(jnp.int32, (note_rows, width), 0)
    note = jnp.zeros((note_rows, width), jnp.float32)
    for part in range(3):
        piece = value.astype(jnp.bfloat16).astype(jnp.float32)
        note = jnp.where(row == part, piece, note)
        value = value - piece
    return note.astype(jnp.bfloat16)


def sum_all(terms):
    return jnp.sum(jnp.sum(terms, axis=0, keepdims=True), axis=-1, keepdims=True)


def seq_place():
    here = lax.axis_index("seq")
    plane = lax.bitwise_and(lax.shift_right_logical(here, 1), 3)
    head = 2 * lax.shift_right_logical(here, 3) + lax.bitwise_and(here, 1)
    return plane, head


def key_slot(plane):
    return lax.bitwise_and(plane, 1)


def query_slot(plane):
    return lax.shift_right_logical(plane, 1)


late_chain = pl.CostEstimate(flops=60_000_000_000, bytes_accessed=0, transcendentals=0)


def params(mebibytes):
    return pltpu.CompilerParams(vmem_limit_bytes=mebibytes * 1024 * 1024)


def pack_kernel(ids_ref, k_ref, v_ref, q_ref, cot_ref, all_ref):
    heads, _, width = all_ref.shape
    rows = k_ref.shape[0]
    ids = ids_ref[...]
    row = lax.broadcasted_iota(jnp.int32, (note_rows, width), 0)
    lane = lax.broadcasted_iota(jnp.int32, (note_rows, width), 1)
    note = jnp.zeros((note_rows, width), jnp.float32)
    for level in range(2):
        count = jnp.sum(jnp.where(ids <= level, 1.0, 0.0), axis=-1, keepdims=True)
        note = jnp.where((row == level) & (lane == 0), count, note)
    note = note.astype(jnp.bfloat16)
    first_query = 2 * rows + note_rows
    for head in range(heads):
        lanes = slice(head * width, (head + 1) * width)
        all_ref[head, 0:rows] = k_ref[:, lanes]
        all_ref[head, rows : 2 * rows] = v_ref[:, lanes]
        all_ref[head, 2 * rows : first_query] = note
        all_ref[head, first_query : first_query + rows] = q_ref[:, lanes]
        all_ref[head, first_query + rows :] = cot_ref[:, lanes]


def run_pack(heads, ids, keys, values, queries, cots):
    rows, features = keys.shape
    shape = (heads, 4 * rows + note_rows, features // heads)
    return pl.pallas_call(
        pack_kernel,
        out_shape=jax.ShapeDtypeStruct(shape, jnp.bfloat16),
        compiler_params=params(56),
        name="pack_heads",
    )(ids, keys, values, queries, cots)


def twice(column):
    return jnp.concatenate([column, column], axis=1)


def wide_as(column, size):
    return column if size == column.shape[1] else twice(column)


def place_of(run, slot, block):
    return pl.multiple_of((2 * run + slot) * block, 64)


def key_spot(first, size):
    return pl.ds(first if isinstance(first, int) else pl.multiple_of(first, 128), size)


def all_chunks(work, some_keys, shared, chunks):
    work(0, some_keys, 0)

    def both(chunk, carry):
        work(some_keys + chunk * k_tile, k_tile, 0)
        return carry

    def upper(chunk, carry):
        work(some_keys + chunk * k_tile, k_tile, 1)
        return carry

    lax.fori_loop(0, shared, both, 0)
    lax.fori_loop(shared, chunks, upper, 0)


def forward_kernel(
    log_ref,
    own_ref,
    kv_ref,
    qc_ref,
    kc_ref,
    vc_ref,
    prob_ref,
    key_ref,
    val_ref,
    query_ref,
    cot_ref,
    num_ref,
    stat_ref,
    shared_ref,
    wide_scr,
    limit_scr,
    sum_scr,
):
    plane, head = seq_place()
    members, tall, width = own_ref.shape
    rows = (tall - note_rows) // 4
    block = 2 * rows
    runs = members // 2
    queries = query_ref.shape[0]
    some_keys = kc_ref.shape[0] // 2
    fine = key_ref.shape[0] - some_keys
    first_query = 2 * rows + note_rows

    def count(notes):
        total = jnp.sum(notes.astype(jnp.float32), axis=0)
        return [jnp.sum(total[level : level + 1]).astype(jnp.int32) for level in range(2)]

    own_counts = count(own_ref[:, 2 * rows : first_query])
    key_counts = [a + b for a, b in zip(own_counts, count(kv_ref[:, 2 * rows :]))]
    query_counts = [a + b for a, b in zip(own_counts, count(qc_ref[:, :note_rows]))]

    def limit_of(place):
        return jnp.where(
            place < query_counts[0],
            key_counts[0],
            jnp.where(place < query_counts[1], key_counts[1], fine),
        )

    own_slot = key_slot(plane)
    for ref, slot in ((own_ref, own_slot), (kv_ref, 1 - own_slot)):
        for run in range(runs):
            pick = slice(2 * run, 2 * run + 2)
            spot = pl.ds(pl.multiple_of(some_keys + place_of(run, slot, block), 64), block)
            key_ref[spot, :] = unit_rows(ref[pick, 0:rows].reshape(block, width))[0].astype(
                jnp.bfloat16
            )
            values = ref[pick, rows : 2 * rows].reshape(block, width)
            val_ref[spot, :] = values
            wide_scr[spot, 0:width] = values
    half = pl.ds(pl.multiple_of(query_slot(plane) * some_keys, some_keys), some_keys)
    key_ref[0:some_keys, :] = kc_ref[half, :]
    val_ref[0:some_keys, :] = vc_ref[half, :]
    wide_scr[0:some_keys, 0:width] = vc_ref[half, :]
    wide_scr[:, width:] = jnp.ones((some_keys + fine, width), jnp.bfloat16)

    own_slot = query_slot(plane)
    for ref, slot, start in ((own_ref, own_slot, first_query), (qc_ref, 1 - own_slot, note_rows)):
        for run in range(runs):
            pick = slice(2 * run, 2 * run + 2)
            spot = pl.ds(place_of(run, slot, block), block)
            query_ref[spot, :] = unit_rows(
                ref[pick, start : start + rows].reshape(block, width)
            )[0].astype(jnp.bfloat16)
            cot_ref[spot, :] = ref[pick, start + rows : start + 2 * rows].reshape(block, width)
    limit_scr[...] = some_keys + limit_of(
        lax.broadcasted_iota(jnp.int32, (queries, width), 0)
    )

    sharp = jnp.exp(jnp.full((1, width), log_ref[head], jnp.float32))[:, 0:1]
    slope = sharp * log2_e
    sum_scr[...] = jnp.zeros_like(sum_scr)

    def probs(start, size, part):
        first = part * queries // 2
        spot = key_spot(start, size)
        cosine = dot_nt(query_ref[first:, :], key_ref[spot, :])
        prob = jnp.exp2(cosine * slope - slope)
        place = start + lax.broadcasted_iota(jnp.int32, (1, size), 1)
        seen = place < wide_as(limit_scr[first:, :], size)
        prob = jnp.where(seen, prob, 0.0).astype(jnp.bfloat16)
        prob_ref[first:, spot] = prob
        sum_scr[first:, :] += dot_nn(prob, wide_scr[spot, :])

    shared = (limit_of(queries // 2 - 1) + k_tile - 1) // k_tile
    shared_ref[0] = shared
    all_chunks(probs, some_keys, shared, fine // k_tile)

    num = sum_scr[:, :width]
    num_ref[...] = num
    weighted = jnp.sum(num * cot_ref[...].astype(jnp.float32), axis=-1, keepdims=True)
    row = lax.broadcasted_iota(jnp.int32, (width, width), 0)
    lane = lax.broadcasted_iota(jnp.int32, (width, width), 1)
    parts = queries // width
    for part in range(parts):
        spot = slice(part * width, (part + 1) * width)
        for index, value in ((part, sum_scr[spot, width:]), (parts + part, weighted[spot])):
            stat_ref[index : index + 1, :] = jnp.sum(
                jnp.where(row == lane, value, 0.0), axis=0, keepdims=True
            )


def backward_kernel(
    log_ref,
    shared_ref,
    own_ref,
    qc_ref,
    stat_ref,
    other_stat_ref,
    prob_ref,
    key_ref,
    val_ref,
    query_ref,
    cot_ref,
    num_ref,
    coarse_scale_ref,
    od_ref,
    od_send_ref,
    dkv_ref,
    dkv_send_ref,
    small_ref,
    den_scr,
    mean_scr,
    grad_scr,
    query_turn,
    cot_turn,
    turn_scr,
):
    plane, head = seq_place()
    members, tall, width = own_ref.shape
    rows = (tall - note_rows) // 4
    block = 2 * rows
    runs = members // 2
    queries = query_ref.shape[0]
    first_query = 2 * rows + note_rows
    some_keys = small_ref.shape[0] - note_rows
    fine = key_ref.shape[0] - some_keys
    sharp = jnp.exp(jnp.full((1, width), log_ref[head], jnp.float32))[:, 0:1]

    row = lax.broadcasted_iota(jnp.int32, (width, width), 0)
    lane = lax.broadcasted_iota(jnp.int32, (width, width), 1)
    parts = queries // width

    def column(index):
        values = stat_ref[index : index + 1, :] + other_stat_ref[index : index + 1, :]
        return jnp.sum(jnp.where(row == lane, values, 0.0), axis=1, keepdims=True)

    for part in range(parts):
        spot = slice(part * width, (part + 1) * width)
        r_den = 1.0 / column(part)
        den_scr[spot, :] = jnp.broadcast_to(r_den, (width, width))
        mean_scr[spot, :] = jnp.broadcast_to(column(parts + part) * r_den, (width, width))

    grad_scr[...] = jnp.zeros_like(grad_scr)
    query_turn[...] = jnp.transpose(
        query_ref[...].astype(jnp.float32) * (den_scr[...] * sharp)
    ).astype(jnp.bfloat16)
    cot_turn[...] = jnp.transpose(cot_ref[...].astype(jnp.float32) * den_scr[...]).astype(
        jnp.bfloat16
    )

    def grads(start, size, part):
        first = part * queries // 2
        spot = key_spot(start, size)
        prob = prob_ref[first:, spot]
        dprob = dot_nt(cot_ref[first:, :], val_ref[spot, :])
        dscore = prob.astype(jnp.float32) * (dprob - wide_as(mean_scr[first:, :], size))
        dscore = dscore.astype(jnp.bfloat16)
        grad_scr[first:, :] += dot_nn(dscore, key_ref[spot, :])
        dk = dot_nn(query_turn[:, first:], dscore)
        dv = dot_nn(cot_turn[:, first:], prob)
        turn_scr[spot, 0:width] = jnp.transpose(dk).astype(jnp.bfloat16)
        turn_scr[spot, width:] = jnp.transpose(dv).astype(jnp.bfloat16)

    all_chunks(grads, some_keys, shared_ref[0], fine // k_tile)

    own_slot = query_slot(plane)
    scale = coarse_scale_ref[pl.ds(pl.multiple_of(head * 8, 8), 8), :]
    scale = scale * jnp.where(plane == 0, 1.0, 0.0)
    for ref, slot, start, target in (
        (own_ref, own_slot, first_query, od_ref),
        (qc_ref, 1 - own_slot, note_rows, od_send_ref),
    ):
        for run in range(runs):
            spot = pl.ds(place_of(run, slot, block), block)
            pick = ref[2 * run : 2 * run + 2, start : start + rows]
            q_dir, q_inv = unit_rows(pick.reshape(block, width))
            r_den = den_scr[spot, :]
            grad = grad_scr[spot, :] * (r_den * sharp)
            along = jnp.sum(q_dir * grad, axis=-1, keepdims=True)
            scale = scale + fold_rows(query_ref[spot, :].astype(jnp.float32) * grad)
            to = slice(run * block, (run + 1) * block)
            target[to, 0:width] = (num_ref[spot, :] * r_den).astype(jnp.bfloat16)
            target[to, width:] = (q_inv * (grad - q_dir * along)).astype(jnp.bfloat16)

    own_slot = key_slot(plane)
    for slot, target in ((own_slot, dkv_ref), (1 - own_slot, dkv_send_ref)):
        for run in range(runs):
            spot = pl.ds(pl.multiple_of(some_keys + place_of(run, slot, block), 64), block)
            target[run * block : (run + 1) * block, :] = turn_scr[spot, :]
    small_ref[0:some_keys, :] = turn_scr[0:some_keys, :]
    small_ref[some_keys:, :] = in_pieces(sum_all(scale), 2 * width)


def run_fine(log_scale, own_rows, kv_rows, qc_rows, key_coarse, val_coarse, coarse_scale, swap):
    members, tall, width = own_rows.shape
    rows = (tall - note_rows) // 4
    some_keys = key_coarse.shape[0] // 2
    queries = 2 * members * rows
    total = some_keys + queries
    vmem = pl.BlockSpec(memory_space=pltpu.VMEM)
    smem = pl.BlockSpec(memory_space=pltpu.SMEM)

    def low(*shape):
        return jax.ShapeDtypeStruct(shape, jnp.bfloat16)

    def wide(*shape):
        return jax.ShapeDtypeStruct(shape, jnp.float32)

    prob, keys, values, query, cot, num, stat, shared = pl.pallas_call(
        forward_kernel,
        out_shape=(
            low(queries, total),
            low(total, width),
            low(total, width),
            low(queries, width),
            low(queries, width),
            wide(queries, width),
            wide(2 * queries // width, width),
            jax.ShapeDtypeStruct((1,), jnp.int32),
        ),
        in_specs=[smem] + [vmem] * 5,
        out_specs=(vmem,) * 7 + (smem,),
        scratch_shapes=[
            pltpu.VMEM((total, 2 * width), jnp.bfloat16),
            pltpu.VMEM((queries, width), jnp.int32),
            pltpu.VMEM((queries, 2 * width), jnp.float32),
        ],
        compiler_params=params(16),
        cost_estimate=pl.CostEstimate(
            flops=4 * queries * total * width,
            bytes_accessed=4 * queries * total,
            transcendentals=queries * total,
        ),
        name="fine_forward",
    )(log_scale, own_rows, kv_rows, qc_rows, key_coarse, val_coarse)
    other_stat = swap(stat)
    half = low(queries // 2, 2 * width)
    return pl.pallas_call(
        backward_kernel,
        out_shape=(half, half, half, half, low(some_keys + note_rows, 2 * width)),
        in_specs=[smem, smem] + [vmem] * 11,
        out_specs=(vmem,) * 5,
        scratch_shapes=[
            pltpu.VMEM((queries, width), jnp.float32),
            pltpu.VMEM((queries, width), jnp.float32),
            pltpu.VMEM((queries, width), jnp.float32),
            pltpu.VMEM((width, queries), jnp.bfloat16),
            pltpu.VMEM((width, queries), jnp.bfloat16),
            pltpu.VMEM((total, 2 * width), jnp.bfloat16),
        ],
        compiler_params=params(16),
        cost_estimate=pl.CostEstimate(
            flops=8 * queries * total * width,
            bytes_accessed=4 * queries * total,
            transcendentals=0,
        ),
        name="fine_backward",
    )(
        log_scale,
        shared,
        own_rows,
        qc_rows,
        stat,
        other_stat,
        prob,
        keys,
        values,
        query,
        cot,
        num,
        coarse_scale,
    )


def coarse_kernel(
    log_ref,
    row_level_ref,
    col_level_ref,
    q_ref,
    k_ref,
    v_ref,
    cot_ref,
    out_ref,
    dq_ref,
    dk_ref,
    dv_ref,
    scale_ref,
    key_low_ref,
    value_ref,
):
    _, own = seq_place()
    count, features = q_ref.shape
    heads = log_ref.shape[0]
    width = features // heads
    visible = col_level_ref[...] <= row_level_ref[...]
    for head in range(heads):
        lanes = slice(head * width, (head + 1) * width)
        sharp = jnp.exp(jnp.full((1, width), log_ref[head], jnp.float32))[:, 0:1]
        slope = sharp * log2_e
        q_dir, q_inv = unit_rows(q_ref[:, lanes])
        q_low = q_dir.astype(jnp.bfloat16)
        key_low = unit_rows(k_ref[:, lanes])[0].astype(jnp.bfloat16)
        values = v_ref[:, lanes]
        cot = cot_ref[:, lanes]
        prob = jnp.exp2(dot_nt(q_low, key_low) * slope - slope)
        prob = jnp.where(visible, prob, 0.0)
        r_den = 1.0 / jnp.sum(prob, axis=-1, keepdims=True)
        norm_prob = prob * r_den
        dprob = dot_nt(cot, values)
        mean = jnp.sum(norm_prob * dprob, axis=-1, keepdims=True)
        dscore = (norm_prob * (dprob - mean)).astype(jnp.bfloat16)
        norm_low = norm_prob.astype(jnp.bfloat16)
        out_ref[:, lanes] = dot_nn(norm_low, values).astype(jnp.bfloat16)
        grad = sharp * dot_nn(dscore, key_low)
        along = jnp.sum(q_dir * grad, axis=-1, keepdims=True)
        dq_ref[:, lanes] = (q_inv * (grad - q_dir * along)).astype(jnp.bfloat16)
        scale_ref[head * 8 : head * 8 + 8, :] = fold_rows(q_low.astype(jnp.float32) * grad)
        q_turned = jnp.transpose(q_dir).astype(jnp.bfloat16)
        cot_turned = jnp.transpose(cot.astype(jnp.float32)).astype(jnp.bfloat16)
        dk_ref[:, lanes] = sharp * jnp.transpose(dot_nn(q_turned, dscore))
        dv_ref[:, lanes] = jnp.transpose(dot_nn(cot_turned, norm_low))

        @pl.when(own == head)
        def _():
            key_low_ref[...] = key_low
            value_ref[...] = values


def run_coarse(log_scale, levels, queries, keys, values, cots):
    count, features = queries.shape
    heads = log_scale.shape[0]
    width = features // heads
    vmem = pl.BlockSpec(memory_space=pltpu.VMEM)
    wide = jax.ShapeDtypeStruct((count, features), jnp.float32)
    low = jax.ShapeDtypeStruct((count, features), jnp.bfloat16)
    return pl.pallas_call(
        coarse_kernel,
        out_shape=(low, low, wide, wide, jax.ShapeDtypeStruct((heads * 8, width), jnp.float32))
        + (jax.ShapeDtypeStruct((count, width), jnp.bfloat16),) * 2,
        in_specs=[pl.BlockSpec(memory_space=pltpu.SMEM)] + [vmem] * 6,
        compiler_params=params(14),
        cost_estimate=pl.CostEstimate(
            flops=12 * count * count * features,
            bytes_accessed=24 * count * features,
            transcendentals=heads * count * count,
        ),
        name="coarse_attention",
    )(log_scale, levels[:, None], levels[None, :], queries, keys, values, cots)


def small_kernel(own_ref, near_ref, across_ref, far_ref, sum_ref, scale_ref):
    plane, _ = seq_place()
    some_keys = own_ref.shape[0] - note_rows
    terms = [ref[...].astype(jnp.float32) for ref in (own_ref, near_ref, across_ref, far_ref)]
    half = query_slot(plane)
    for place, pair in ((half, terms[:2]), (1 - half, terms[2:])):
        spot = pl.ds(pl.multiple_of(place * some_keys, some_keys), some_keys)
        sum_ref[spot, :] = (pair[0][:some_keys] + pair[1][:some_keys]).astype(jnp.bfloat16)
    scale = terms[0][some_keys:] + terms[1][some_keys:] + terms[2][some_keys:] + terms[3][some_keys:]
    scale = jnp.sum(scale[:, : scale_ref.shape[1]], axis=0, keepdims=True)
    scale_ref[...] = jnp.broadcast_to(scale, scale_ref.shape)


def run_small(terms):
    tall, both = terms[0].shape
    return pl.pallas_call(
        small_kernel,
        out_shape=(
            jax.ShapeDtypeStruct((2 * (tall - note_rows), both), jnp.bfloat16),
            jax.ShapeDtypeStruct((8, both // 2), jnp.float32),
        ),
        compiler_params=params(2),
        name="sum_coarse_terms",
    )(*terms)


def sum_kernel(
    od_ref, other_od_ref, dkv_ref, other_dkv_ref, own_ref, scale_ref, other_scale_ref, all_ref
):
    members, tall, width = all_ref.shape
    rows = (tall - note_rows) // 4
    fine = members * rows

    def put(place, value):
        all_ref[:, place * rows : (place + 1) * rows] = value.astype(jnp.bfloat16).reshape(
            members, rows, width
        )

    summed = od_ref[...].astype(jnp.float32) + other_od_ref[...].astype(jnp.float32)
    put(0, summed[:, :width])
    put(1, summed[:, width:])
    summed = dkv_ref[...].astype(jnp.float32) + other_dkv_ref[...].astype(jnp.float32)
    put(2, project(own_ref[:, 0:rows].reshape(fine, width), summed[:, :width]))
    put(3, summed[:, width:])
    note = in_pieces(scale_ref[0:1, 0:1] + other_scale_ref[0:1, 0:1], width)
    for member in range(members):
        all_ref[member, 4 * rows :] = note


def run_sum(od, other_od, dkv, other_dkv, own_rows, scale, other_scale):
    return pl.pallas_call(
        sum_kernel,
        out_shape=jax.ShapeDtypeStruct(own_rows.shape, jnp.bfloat16),
        compiler_params=params(6),
        cost_estimate=late_chain,
        name="sum_pairs",
    )(od, other_od, dkv, other_dkv, own_rows, scale, other_scale)


def join_kernel(terms_ref, dk_own_ref, dv_own_ref, k_ref, dk_ref, dv_ref, last_ref):
    heads, _, both = terms_ref.shape
    width = both // 2
    for head in range(heads):
        lanes = slice(head * width, (head + 1) * width)
        terms = terms_ref[head].astype(jnp.float32)
        grad = terms[:, :width] + dk_own_ref[:, lanes]
        dk_ref[:, lanes] = project(k_ref[:, lanes], grad).astype(jnp.bfloat16)
        dv_ref[:, lanes] = (terms[:, width:] + dv_own_ref[:, lanes]).astype(jnp.bfloat16)
    last_ref[...] = jnp.zeros_like(last_ref)


def run_join(terms, dk_own, dv_own, keys):
    low = jax.ShapeDtypeStruct(keys.shape, jnp.bfloat16)
    return pl.pallas_call(
        join_kernel,
        out_shape=(low, low, jax.ShapeDtypeStruct((8, 128), jnp.float32)),
        compiler_params=params(8),
        name="join_coarse",
    )(terms, dk_own, dv_own, keys)


def unpack_kernel(factor, all_ref, _, out_ref, dq_ref, dk_ref, dv_ref, scale_ref):
    heads, tall, width = all_ref.shape
    rows = (tall - note_rows) // 4
    for head in range(heads):
        lanes = slice(head * width, (head + 1) * width)
        for place, ref in enumerate((out_ref, dq_ref, dk_ref, dv_ref)):
            ref[:, lanes] = all_ref[head, place * rows : (place + 1) * rows]
        note = all_ref[head, 4 * rows :].astype(jnp.float32)
        scale_ref[head] = jnp.sum(note[:, 0:1]) * factor


def run_unpack(factor, all_back, after):
    heads, tall, width = all_back.shape
    flat = jax.ShapeDtypeStruct(((tall - note_rows) // 4, heads * width), jnp.bfloat16)
    vmem = pl.BlockSpec(memory_space=pltpu.VMEM)
    return pl.pallas_call(
        partial(unpack_kernel, factor),
        out_shape=(flat,) * 4 + (jax.ShapeDtypeStruct((heads,), jnp.float32),),
        in_specs=[vmem, vmem],
        out_specs=(vmem,) * 4 + (pl.BlockSpec(memory_space=pltpu.SMEM),),
        compiler_params=params(3),
        cost_estimate=late_chain,
        name="unpack_heads",
    )(all_back, after)


def body(
    q_coarse,
    k_coarse,
    v_coarse,
    cot_coarse,
    coarse_ids,
    q_fine,
    k_fine,
    v_fine,
    cot_fine,
    fine_ids,
    log_scale,
):
    heads = log_scale.shape[0]
    coarse = q_coarse.shape[1]
    rows = q_fine.shape[1]
    seq = lax.axis_size("seq")
    images = lax.axis_size("dp")
    groups = [
        [8 * (h // 2) + 2 * plane + h % 2 for h in range(heads)] for plane in range(planes)
    ]

    def exchange(parts):
        return lax.all_to_all(parts, "seq", 0, 0, axis_index_groups=groups, tiled=True)

    def to_plane(array, flip):
        return lax.ppermute(array, "seq", [(i, i ^ (2 * flip)) for i in range(seq)])

    def to_image(array, flip):
        return lax.ppermute(array, "dp", [(i, i ^ flip) for i in range(images)])

    own_rows = exchange(run_pack(heads, fine_ids, k_fine[0], v_fine[0], q_fine[0], cot_fine[0]))
    kv_rows = to_plane(own_rows[:, : 2 * rows + note_rows], 1)
    qc_rows = to_plane(own_rows[:, 2 * rows :], 3)

    out_c, dq_c, dk_own, dv_own, scale_c, key_c, val_c = run_coarse(
        log_scale, coarse_ids[0], q_coarse[0], k_coarse[0], v_coarse[0], cot_coarse[0]
    )
    od, od_send, dkv, dkv_send, small = run_fine(
        log_scale, own_rows, kv_rows, qc_rows, key_c, val_c, scale_c, lambda stat: to_plane(stat, 3)
    )

    small_sum, scale = run_small([small] + [to_plane(small, flip) for flip in (1, 2, 3)])
    of_image = lax.all_gather(small_sum, "seq", axis=0, axis_index_groups=groups)

    other_dkv = to_plane(dkv_send, 1)
    other_od = to_plane(od_send, 3)
    scale = scale + to_image(scale, 1) + to_image(scale, 2) + to_image(scale, 3)
    all_parts = run_sum(od, other_od, dkv, other_dkv, own_rows, scale, to_image(scale, 4))
    all_back = exchange(all_parts)
    dk_c, dv_c, after = run_join(of_image, dk_own, dv_own, k_coarse[0])
    factor = 1.0 / math.sqrt(images * (coarse + seq * rows))
    fine_out, fine_dq, fine_dk, fine_dv, grad_scale = run_unpack(factor, all_back, after)
    return (
        out_c[None],
        dq_c[None],
        dk_c[None],
        dv_c[None],
        fine_out[None],
        fine_dq[None],
        fine_dk[None],
        fine_dv[None],
        grad_scale,
    )


def solution(mesh):
    whole = P("dp", None, None)
    split = P("dp", "seq", None)
    return jax.shard_map(
        body,
        mesh=mesh,
        in_specs=(whole,) * 4 + (P("dp", None),) + (split,) * 4 + (P("dp", "seq"), P()),
        out_specs=(whole,) * 4 + (split,) * 4 + (P(),),
        check_vma=False,
    )
```

```python
import math
from functools import partial

import jax
import jax.numpy as jnp
from jax import lax
from jax.experimental import pallas as pl
from jax.experimental.pallas import tpu as pltpu
from jax.sharding import PartitionSpec as P

norm_eps = 1e-06
log2_e = 1.4426950408889634
k_tile = 256
note_rows = 16

planes = 4


def dot_nt(left, right):
    return lax.dot_general(
        left, right, (((1,), (1,)), ((), ())), preferred_element_type=jnp.float32
    )


def dot_nn(left, right):
    return jnp.dot(left, right, preferred_element_type=jnp.float32)


def unit_rows(rows):
    wide = rows.astype(jnp.float32)
    inv_norm = lax.rsqrt(jnp.sum(wide * wide, axis=-1, keepdims=True) + norm_eps)
    return wide * inv_norm, inv_norm


def project(key_rows, grad):
    key_dir, key_inv = unit_rows(key_rows)
    along = jnp.sum(key_dir * grad, axis=-1, keepdims=True)
    return key_inv * (grad - key_dir * along)


def fold_rows(terms):
    rows, width = terms.shape
    return jnp.sum(terms.reshape(rows // 8, 8, width), axis=0)


def in_pieces(value, width):
    row = lax.broadcasted_iota(jnp.int32, (note_rows, width), 0)
    note = jnp.zeros((note_rows, width), jnp.float32)
    for part in range(3):
        piece = value.astype(jnp.bfloat16).astype(jnp.float32)
        note = jnp.where(row == part, piece, note)
        value = value - piece
    return note.astype(jnp.bfloat16)


def sum_all(terms):
    return jnp.sum(jnp.sum(terms, axis=0, keepdims=True), axis=-1, keepdims=True)


def seq_place():
    here = lax.axis_index("seq")
    plane = lax.bitwise_and(lax.shift_right_logical(here, 1), 3)
    head = 2 * lax.shift_right_logical(here, 3) + lax.bitwise_and(here, 1)
    return plane, head


def key_slot(plane):
    return lax.bitwise_and(plane, 1)


def query_slot(plane):
    return lax.shift_right_logical(plane, 1)


def params(mebibytes):
    return pltpu.CompilerParams(vmem_limit_bytes=mebibytes * 1024 * 1024)


def pack_kernel(ids_ref, k_ref, v_ref, q_ref, cot_ref, all_ref):
    heads, _, width = all_ref.shape
    rows = k_ref.shape[0]
    ids = ids_ref[...]
    row = lax.broadcasted_iota(jnp.int32, (note_rows, width), 0)
    lane = lax.broadcasted_iota(jnp.int32, (note_rows, width), 1)
    note = jnp.zeros((note_rows, width), jnp.float32)
    for level in range(2):
        count = jnp.sum(jnp.where(ids <= level, 1.0, 0.0), axis=-1, keepdims=True)
        note = jnp.where((row == level) & (lane == 0), count, note)
    note = note.astype(jnp.bfloat16)
    first_query = 2 * rows + note_rows
    for head in range(heads):
        lanes = slice(head * width, (head + 1) * width)
        all_ref[head, 0:rows] = k_ref[:, lanes]
        all_ref[head, rows : 2 * rows] = v_ref[:, lanes]
        all_ref[head, 2 * rows : first_query] = note
        all_ref[head, first_query : first_query + rows] = q_ref[:, lanes]
        all_ref[head, first_query + rows :] = cot_ref[:, lanes]


def run_pack(heads, ids, keys, values, queries, cots):
    rows, features = keys.shape
    shape = (heads, 4 * rows + note_rows, features // heads)
    return pl.pallas_call(
        pack_kernel,
        out_shape=jax.ShapeDtypeStruct(shape, jnp.bfloat16),
        compiler_params=params(56),
        name="pack_heads",
    )(ids, keys, values, queries, cots)


def twice(column):
    return jnp.concatenate([column, column], axis=1)


def wide_as(column, size):
    return column if size == column.shape[1] else twice(column)


def place_of(run, slot, block):
    return pl.multiple_of((2 * run + slot) * block, 64)


def key_spot(first, size):
    return pl.ds(first if isinstance(first, int) else pl.multiple_of(first, 128), size)


def all_chunks(work, some_keys, shared, chunks):
    work(0, some_keys, 0, True)
    work(some_keys, some_keys, 0, False)

    def both(chunk, carry):
        work(2 * some_keys + chunk * k_tile, k_tile, 0, True)
        return carry

    def upper(chunk, carry):
        work(2 * some_keys + chunk * k_tile, k_tile, 1, True)
        return carry

    lax.fori_loop(0, shared, both, 0)
    lax.fori_loop(shared, chunks, upper, 0)


def forward_kernel(
    log_ref,
    own_ref,
    kv_ref,
    qc_ref,
    kc_ref,
    vc_ref,
    prob_ref,
    key_ref,
    val_ref,
    query_ref,
    cot_ref,
    num_ref,
    stat_ref,
    shared_ref,
    wide_scr,
    limit_scr,
    sum_scr,
):
    plane, head = seq_place()
    members, tall, width = own_ref.shape
    rows = (tall - note_rows) // 4
    block = 2 * rows
    runs = members // 2
    queries = query_ref.shape[0]
    coarse = kc_ref.shape[0]
    some_keys = coarse // 2
    fine = key_ref.shape[0] - coarse
    first_query = 2 * rows + note_rows

    def count(notes):
        total = jnp.sum(notes.astype(jnp.float32), axis=0)
        return [jnp.sum(total[level : level + 1]).astype(jnp.int32) for level in range(2)]

    own_counts = count(own_ref[:, 2 * rows : first_query])
    key_counts = [a + b for a, b in zip(own_counts, count(kv_ref[:, 2 * rows :]))]
    query_counts = [a + b for a, b in zip(own_counts, count(qc_ref[:, :note_rows]))]

    def limit_of(place):
        return jnp.where(
            place < query_counts[0],
            key_counts[0],
            jnp.where(place < query_counts[1], key_counts[1], fine),
        )

    own_slot = key_slot(plane)
    for ref, slot in ((own_ref, own_slot), (kv_ref, 1 - own_slot)):
        for run in range(runs):
            pick = slice(2 * run, 2 * run + 2)
            spot = pl.ds(pl.multiple_of(coarse + place_of(run, slot, block), 64), block)
            key_ref[spot, :] = unit_rows(ref[pick, 0:rows].reshape(block, width))[0].astype(
                jnp.bfloat16
            )
            values = ref[pick, rows : 2 * rows].reshape(block, width)
            val_ref[spot, :] = values
            wide_scr[spot, 0:width] = values
    own_half = query_slot(plane)
    for index, half in enumerate((own_half, 1 - own_half)):
        spot = slice(index * some_keys, (index + 1) * some_keys)
        half = pl.ds(pl.multiple_of(half * some_keys, some_keys), some_keys)
        key_ref[spot, :] = kc_ref[half, :]
        val_ref[spot, :] = vc_ref[half, :]
        wide_scr[spot, 0:width] = vc_ref[half, :]
    wide_scr[:, width:] = jnp.ones((coarse + fine, width), jnp.bfloat16)

    own_slot = query_slot(plane)
    for ref, slot, start in ((own_ref, own_slot, first_query), (qc_ref, 1 - own_slot, note_rows)):
        for run in range(runs):
            pick = slice(2 * run, 2 * run + 2)
            spot = pl.ds(place_of(run, slot, block), block)
            query_ref[spot, :] = unit_rows(
                ref[pick, start : start + rows].reshape(block, width)
            )[0].astype(jnp.bfloat16)
            cot_ref[spot, :] = ref[pick, start + rows : start + 2 * rows].reshape(block, width)
    limit_scr[...] = coarse + limit_of(
        lax.broadcasted_iota(jnp.int32, (queries, width), 0)
    )

    sharp = jnp.exp(jnp.full((1, width), log_ref[head], jnp.float32))[:, 0:1]
    slope = sharp * log2_e
    sum_scr[...] = jnp.zeros_like(sum_scr)

    def probs(start, size, part, counts):
        first = part * queries // 2
        spot = key_spot(start, size)
        cosine = dot_nt(query_ref[first:, :], key_ref[spot, :])
        prob = jnp.exp2(cosine * slope - slope)
        place = start + lax.broadcasted_iota(jnp.int32, (1, size), 1)
        seen = place < wide_as(limit_scr[first:, :], size)
        prob = jnp.where(seen, prob, 0.0).astype(jnp.bfloat16)
        prob_ref[first:, spot] = prob
        if counts:
            sum_scr[first:, :] += dot_nn(prob, wide_scr[spot, :])

    shared = (limit_of(queries // 2 - 1) + k_tile - 1) // k_tile
    shared_ref[0] = shared
    all_chunks(probs, some_keys, shared, fine // k_tile)

    num = sum_scr[:, :width]
    num_ref[...] = num
    weighted = jnp.sum(num * cot_ref[...].astype(jnp.float32), axis=-1, keepdims=True)
    row = lax.broadcasted_iota(jnp.int32, (width, width), 0)
    lane = lax.broadcasted_iota(jnp.int32, (width, width), 1)
    parts = queries // width
    for part in range(parts):
        spot = slice(part * width, (part + 1) * width)
        for index, value in ((part, sum_scr[spot, width:]), (parts + part, weighted[spot])):
            stat_ref[index : index + 1, :] = jnp.sum(
                jnp.where(row == lane, value, 0.0), axis=0, keepdims=True
            )


def backward_kernel(
    log_ref,
    shared_ref,
    own_ref,
    qc_ref,
    stat_ref,
    other_stat_ref,
    prob_ref,
    key_ref,
    val_ref,
    query_ref,
    cot_ref,
    num_ref,
    coarse_scale_ref,
    od_ref,
    od_send_ref,
    dkv_ref,
    dkv_send_ref,
    small_ref,
    den_scr,
    mean_scr,
    grad_scr,
    query_turn,
    cot_turn,
    turn_scr,
):
    plane, head = seq_place()
    members, tall, width = own_ref.shape
    rows = (tall - note_rows) // 4
    block = 2 * rows
    runs = members // 2
    queries = query_ref.shape[0]
    first_query = 2 * rows + note_rows
    coarse = small_ref.shape[0] - note_rows
    fine = key_ref.shape[0] - coarse
    sharp = jnp.exp(jnp.full((1, width), log_ref[head], jnp.float32))[:, 0:1]

    row = lax.broadcasted_iota(jnp.int32, (width, width), 0)
    lane = lax.broadcasted_iota(jnp.int32, (width, width), 1)
    parts = queries // width

    def column(index):
        values = stat_ref[index : index + 1, :] + other_stat_ref[index : index + 1, :]
        return jnp.sum(jnp.where(row == lane, values, 0.0), axis=1, keepdims=True)

    for part in range(parts):
        spot = slice(part * width, (part + 1) * width)
        r_den = 1.0 / column(part)
        den_scr[spot, :] = jnp.broadcast_to(r_den, (width, width))
        mean_scr[spot, :] = jnp.broadcast_to(column(parts + part) * r_den, (width, width))

    grad_scr[...] = jnp.zeros_like(grad_scr)
    query_turn[...] = jnp.transpose(
        query_ref[...].astype(jnp.float32) * (den_scr[...] * sharp)
    ).astype(jnp.bfloat16)
    cot_turn[...] = jnp.transpose(cot_ref[...].astype(jnp.float32) * den_scr[...]).astype(
        jnp.bfloat16
    )

    def grads(start, size, part, counts):
        first = part * queries // 2
        spot = key_spot(start, size)
        prob = prob_ref[first:, spot]
        dprob = dot_nt(cot_ref[first:, :], val_ref[spot, :])
        dscore = prob.astype(jnp.float32) * (dprob - wide_as(mean_scr[first:, :], size))
        dscore = dscore.astype(jnp.bfloat16)
        if counts:
            grad_scr[first:, :] += dot_nn(dscore, key_ref[spot, :])
        dk = dot_nn(query_turn[:, first:], dscore)
        dv = dot_nn(cot_turn[:, first:], prob)
        turn_scr[spot, 0:width] = jnp.transpose(dk).astype(jnp.bfloat16)
        turn_scr[spot, width:] = jnp.transpose(dv).astype(jnp.bfloat16)

    all_chunks(grads, coarse // 2, shared_ref[0], fine // k_tile)

    own_slot = query_slot(plane)
    scale = coarse_scale_ref[pl.ds(pl.multiple_of(head * 8, 8), 8), :]
    scale = scale * jnp.where(plane == 0, 1.0, 0.0)
    for ref, slot, start, target in (
        (own_ref, own_slot, first_query, od_ref),
        (qc_ref, 1 - own_slot, note_rows, od_send_ref),
    ):
        for run in range(runs):
            spot = pl.ds(place_of(run, slot, block), block)
            pick = ref[2 * run : 2 * run + 2, start : start + rows]
            q_dir, q_inv = unit_rows(pick.reshape(block, width))
            r_den = den_scr[spot, :]
            grad = grad_scr[spot, :] * (r_den * sharp)
            along = jnp.sum(q_dir * grad, axis=-1, keepdims=True)
            scale = scale + fold_rows(query_ref[spot, :].astype(jnp.float32) * grad)
            to = slice(run * block, (run + 1) * block)
            target[to, 0:width] = (num_ref[spot, :] * r_den).astype(jnp.bfloat16)
            target[to, width:] = (q_inv * (grad - q_dir * along)).astype(jnp.bfloat16)

    own_slot = key_slot(plane)
    for slot, target in ((own_slot, dkv_ref), (1 - own_slot, dkv_send_ref)):
        for run in range(runs):
            spot = pl.ds(pl.multiple_of(coarse + place_of(run, slot, block), 64), block)
            target[run * block : (run + 1) * block, :] = turn_scr[spot, :]
    small_ref[0:coarse, :] = turn_scr[0:coarse, :]
    small_ref[coarse:, :] = in_pieces(sum_all(scale), 2 * width)


def run_fine(log_scale, own_rows, kv_rows, qc_rows, key_coarse, val_coarse, coarse_scale, swap):
    members, tall, width = own_rows.shape
    rows = (tall - note_rows) // 4
    coarse = key_coarse.shape[0]
    queries = 2 * members * rows
    total = coarse + queries
    vmem = pl.BlockSpec(memory_space=pltpu.VMEM)
    smem = pl.BlockSpec(memory_space=pltpu.SMEM)

    def low(*shape):
        return jax.ShapeDtypeStruct(shape, jnp.bfloat16)

    def wide(*shape):
        return jax.ShapeDtypeStruct(shape, jnp.float32)

    prob, keys, values, query, cot, num, stat, shared = pl.pallas_call(
        forward_kernel,
        out_shape=(
            low(queries, total),
            low(total, width),
            low(total, width),
            low(queries, width),
            low(queries, width),
            wide(queries, width),
            wide(2 * queries // width, width),
            jax.ShapeDtypeStruct((1,), jnp.int32),
        ),
        in_specs=[smem] + [vmem] * 5,
        out_specs=(vmem,) * 7 + (smem,),
        scratch_shapes=[
            pltpu.VMEM((total, 2 * width), jnp.bfloat16),
            pltpu.VMEM((queries, width), jnp.int32),
            pltpu.VMEM((queries, 2 * width), jnp.float32),
        ],
        compiler_params=params(16),
        cost_estimate=pl.CostEstimate(
            flops=4 * queries * total * width,
            bytes_accessed=4 * queries * total,
            transcendentals=queries * total,
        ),
        name="fine_forward",
    )(log_scale, own_rows, kv_rows, qc_rows, key_coarse, val_coarse)
    other_stat = swap(stat)
    half = low(queries // 2, 2 * width)
    return pl.pallas_call(
        backward_kernel,
        out_shape=(half, half, half, half, low(coarse + note_rows, 2 * width)),
        in_specs=[smem, smem] + [vmem] * 11,
        out_specs=(vmem,) * 5,
        scratch_shapes=[
            pltpu.VMEM((queries, width), jnp.float32),
            pltpu.VMEM((queries, width), jnp.float32),
            pltpu.VMEM((queries, width), jnp.float32),
            pltpu.VMEM((width, queries), jnp.bfloat16),
            pltpu.VMEM((width, queries), jnp.bfloat16),
            pltpu.VMEM((total, 2 * width), jnp.bfloat16),
        ],
        compiler_params=params(16),
        cost_estimate=pl.CostEstimate(
            flops=8 * queries * total * width,
            bytes_accessed=4 * queries * total,
            transcendentals=0,
        ),
        name="fine_backward",
    )(
        log_scale,
        shared,
        own_rows,
        qc_rows,
        stat,
        other_stat,
        prob,
        keys,
        values,
        query,
        cot,
        num,
        coarse_scale,
    )


def coarse_kernel(
    log_ref,
    row_level_ref,
    col_level_ref,
    q_ref,
    k_ref,
    v_ref,
    cot_ref,
    out_ref,
    dq_ref,
    dk_ref,
    dv_ref,
    scale_ref,
    key_low_ref,
    value_ref,
):
    _, own = seq_place()
    count, features = q_ref.shape
    heads = log_ref.shape[0]
    width = features // heads
    visible = col_level_ref[...] <= row_level_ref[...]
    for head in range(heads):
        lanes = slice(head * width, (head + 1) * width)
        sharp = jnp.exp(jnp.full((1, width), log_ref[head], jnp.float32))[:, 0:1]
        slope = sharp * log2_e
        q_dir, q_inv = unit_rows(q_ref[:, lanes])
        q_low = q_dir.astype(jnp.bfloat16)
        key_low = unit_rows(k_ref[:, lanes])[0].astype(jnp.bfloat16)
        values = v_ref[:, lanes]
        cot = cot_ref[:, lanes]
        prob = jnp.exp2(dot_nt(q_low, key_low) * slope - slope)
        prob = jnp.where(visible, prob, 0.0)
        r_den = 1.0 / jnp.sum(prob, axis=-1, keepdims=True)
        norm_prob = prob * r_den
        dprob = dot_nt(cot, values)
        mean = jnp.sum(norm_prob * dprob, axis=-1, keepdims=True)
        dscore = (norm_prob * (dprob - mean)).astype(jnp.bfloat16)
        norm_low = norm_prob.astype(jnp.bfloat16)
        out_ref[:, lanes] = dot_nn(norm_low, values).astype(jnp.bfloat16)
        grad = sharp * dot_nn(dscore, key_low)
        along = jnp.sum(q_dir * grad, axis=-1, keepdims=True)
        dq_ref[:, lanes] = (q_inv * (grad - q_dir * along)).astype(jnp.bfloat16)
        scale_ref[head * 8 : head * 8 + 8, :] = fold_rows(q_low.astype(jnp.float32) * grad)
        q_turned = jnp.transpose(q_dir).astype(jnp.bfloat16)
        cot_turned = jnp.transpose(cot.astype(jnp.float32)).astype(jnp.bfloat16)
        dk_ref[:, lanes] = sharp * jnp.transpose(dot_nn(q_turned, dscore))
        dv_ref[:, lanes] = jnp.transpose(dot_nn(cot_turned, norm_low))

        @pl.when(own == head)
        def _():
            key_low_ref[...] = key_low
            value_ref[...] = values


def run_coarse(log_scale, levels, queries, keys, values, cots):
    count, features = queries.shape
    heads = log_scale.shape[0]
    width = features // heads
    vmem = pl.BlockSpec(memory_space=pltpu.VMEM)
    wide = jax.ShapeDtypeStruct((count, features), jnp.float32)
    low = jax.ShapeDtypeStruct((count, features), jnp.bfloat16)
    return pl.pallas_call(
        coarse_kernel,
        out_shape=(low, low, wide, wide, jax.ShapeDtypeStruct((heads * 8, width), jnp.float32))
        + (jax.ShapeDtypeStruct((count, width), jnp.bfloat16),) * 2,
        in_specs=[pl.BlockSpec(memory_space=pltpu.SMEM)] + [vmem] * 6,
        compiler_params=params(14),
        cost_estimate=pl.CostEstimate(
            flops=12 * count * count * features,
            bytes_accessed=24 * count * features,
            transcendentals=heads * count * count,
        ),
        name="coarse_attention",
    )(log_scale, levels[:, None], levels[None, :], queries, keys, values, cots)


def small_kernel(own_ref, near_ref, sum_ref, scale_ref):
    coarse, both = sum_ref.shape
    some_keys = coarse // 2
    summed = own_ref[...].astype(jnp.float32) + near_ref[...].astype(jnp.float32)
    own_half = query_slot(seq_place()[0])
    for index, half in enumerate((own_half, 1 - own_half)):
        spot = pl.ds(pl.multiple_of(half * some_keys, some_keys), some_keys)
        sum_ref[spot, :] = summed[index * some_keys : (index + 1) * some_keys].astype(jnp.bfloat16)
    scale = jnp.sum(summed[coarse:, : both // 2], axis=0, keepdims=True)
    scale_ref[...] = jnp.broadcast_to(scale, scale_ref.shape)


def run_small(own, near):
    tall, both = own.shape
    return pl.pallas_call(
        small_kernel,
        out_shape=(
            jax.ShapeDtypeStruct((tall - note_rows, both), jnp.bfloat16),
            jax.ShapeDtypeStruct((8, both // 2), jnp.float32),
        ),
        compiler_params=params(2),
        name="sum_coarse_terms",
    )(own, near)


def sum_kernel(
    od_ref, other_od_ref, dkv_ref, other_dkv_ref, own_ref, *scale_and_all
):
    *scale_refs, all_ref = scale_and_all
    members, tall, width = all_ref.shape
    rows = (tall - note_rows) // 4
    fine = members * rows

    def put(place, value):
        all_ref[:, place * rows : (place + 1) * rows] = value.astype(jnp.bfloat16).reshape(
            members, rows, width
        )

    summed = od_ref[...].astype(jnp.float32) + other_od_ref[...].astype(jnp.float32)
    put(0, summed[:, :width])
    put(1, summed[:, width:])
    summed = dkv_ref[...].astype(jnp.float32) + other_dkv_ref[...].astype(jnp.float32)
    put(2, project(own_ref[:, 0:rows].reshape(fine, width), summed[:, :width]))
    put(3, summed[:, width:])
    scale = scale_refs[0][0:1, 0:1]
    for ref in scale_refs[1:]:
        scale = scale + ref[0:1, 0:1]
    note = in_pieces(scale, width)
    for member in range(members):
        all_ref[member, 4 * rows :] = note


def run_sum(od, other_od, dkv, other_dkv, own_rows, scales):
    return pl.pallas_call(
        sum_kernel,
        out_shape=jax.ShapeDtypeStruct(own_rows.shape, jnp.bfloat16),
        compiler_params=params(6),
        name="sum_pairs",
    )(od, other_od, dkv, other_dkv, own_rows, *scales)


def join_kernel(terms_ref, dk_own_ref, dv_own_ref, k_ref, dk_ref, dv_ref, last_ref):
    heads, _, both = terms_ref.shape
    width = both // 2
    for head in range(heads):
        lanes = slice(head * width, (head + 1) * width)
        terms = terms_ref[head].astype(jnp.float32)
        grad = terms[:, :width] + dk_own_ref[:, lanes]
        dk_ref[:, lanes] = project(k_ref[:, lanes], grad).astype(jnp.bfloat16)
        dv_ref[:, lanes] = (terms[:, width:] + dv_own_ref[:, lanes]).astype(jnp.bfloat16)
    last_ref[...] = jnp.zeros_like(last_ref)


def run_join(terms, dk_own, dv_own, keys):
    low = jax.ShapeDtypeStruct(keys.shape, jnp.bfloat16)
    return pl.pallas_call(
        join_kernel,
        out_shape=(low, low, jax.ShapeDtypeStruct((8, 128), jnp.float32)),
        compiler_params=params(8),
        name="join_coarse",
    )(terms, dk_own, dv_own, keys)


def unpack_kernel(factor, all_ref, _, out_ref, dq_ref, dk_ref, dv_ref, scale_ref):
    heads, tall, width = all_ref.shape
    rows = (tall - note_rows) // 4
    for head in range(heads):
        lanes = slice(head * width, (head + 1) * width)
        for place, ref in enumerate((out_ref, dq_ref, dk_ref, dv_ref)):
            ref[:, lanes] = all_ref[head, place * rows : (place + 1) * rows]
        note = all_ref[head, 4 * rows :].astype(jnp.float32)
        scale_ref[head] = jnp.sum(note[:, 0:1]) * factor


def run_unpack(factor, all_back, after):
    heads, tall, width = all_back.shape
    flat = jax.ShapeDtypeStruct(((tall - note_rows) // 4, heads * width), jnp.bfloat16)
    vmem = pl.BlockSpec(memory_space=pltpu.VMEM)
    return pl.pallas_call(
        partial(unpack_kernel, factor),
        out_shape=(flat,) * 4 + (jax.ShapeDtypeStruct((heads,), jnp.float32),),
        in_specs=[vmem, vmem],
        out_specs=(vmem,) * 4 + (pl.BlockSpec(memory_space=pltpu.SMEM),),
        compiler_params=params(3),
        name="unpack_heads",
    )(all_back, after)


def body(
    q_coarse,
    k_coarse,
    v_coarse,
    cot_coarse,
    coarse_ids,
    q_fine,
    k_fine,
    v_fine,
    cot_fine,
    fine_ids,
    log_scale,
):
    heads = log_scale.shape[0]
    coarse = q_coarse.shape[1]
    rows = q_fine.shape[1]
    seq = lax.axis_size("seq")
    images = lax.axis_size("dp")
    groups = [
        [8 * (h // 2) + 2 * plane + h % 2 for h in range(heads)] for plane in range(planes)
    ]

    def exchange(parts):
        return lax.all_to_all(parts, "seq", 0, 0, axis_index_groups=groups, tiled=True)

    def to_plane(array, flip):
        return lax.ppermute(array, "seq", [(i, i ^ (2 * flip)) for i in range(seq)])

    def to_image(array, flip):
        return lax.ppermute(array, "dp", [(i, i ^ flip) for i in range(images)])

    def to_both(array, image_flip, plane_flip):
        there = [
            (i ^ image_flip) * seq + (j ^ (2 * plane_flip))
            for i in range(images)
            for j in range(seq)
        ]
        return lax.ppermute(array, ("dp", "seq"), list(enumerate(there)))

    own_rows = exchange(run_pack(heads, fine_ids, k_fine[0], v_fine[0], q_fine[0], cot_fine[0]))
    kv_rows = to_plane(own_rows[:, : 2 * rows + note_rows], 1)
    qc_rows = to_plane(own_rows[:, 2 * rows :], 3)

    out_c, dq_c, dk_own, dv_own, scale_c, key_c, val_c = run_coarse(
        log_scale, coarse_ids[0], q_coarse[0], k_coarse[0], v_coarse[0], cot_coarse[0]
    )
    od, od_send, dkv, dkv_send, small = run_fine(
        log_scale, own_rows, kv_rows, qc_rows, key_c, val_c, scale_c, lambda stat: to_plane(stat, 3)
    )

    small_sum, scale = run_small(small, to_plane(small, 1))
    of_image = lax.all_gather(small_sum, "seq", axis=0, axis_index_groups=groups)

    other_dkv = to_plane(dkv_send, 1)
    other_od = to_plane(od_send, 3)
    scale = scale + to_image(scale, 1) + to_image(scale, 2) + to_image(scale, 3)
    scales = [scale, to_plane(scale, 3), to_image(scale, 4), to_both(scale, 4, 3)]
    all_parts = run_sum(od, other_od, dkv, other_dkv, own_rows, scales)
    all_back = exchange(all_parts)
    dk_c, dv_c, after = run_join(of_image, dk_own, dv_own, k_coarse[0])
    factor = 1.0 / math.sqrt(images * (coarse + seq * rows))
    fine_out, fine_dq, fine_dk, fine_dv, grad_scale = run_unpack(factor, all_back, after)
    return (
        out_c[None],
        dq_c[None],
        dk_c[None],
        dv_c[None],
        fine_out[None],
        fine_dq[None],
        fine_dk[None],
        fine_dv[None],
        grad_scale,
    )


def solution(mesh):
    whole = P("dp", None, None)
    split = P("dp", "seq", None)
    return jax.shard_map(
        body,
        mesh=mesh,
        in_specs=(whole,) * 4 + (P("dp", None),) + (split,) * 4 + (P("dp", "seq"), P()),
        out_specs=(whole,) * 4 + (split,) * 4 + (P(),),
        check_vma=False,
    )
```

```python
import math
from functools import partial

import jax
import jax.numpy as jnp
from jax import lax
from jax.experimental import pallas as pl
from jax.experimental.pallas import tpu as pltpu
from jax.sharding import PartitionSpec as P

norm_eps = 1e-06
log2_e = 1.4426950408889634
k_tile = 256
q_rows = 384
note_rows = 16

planes = 4


def dot_nt(left, right):
    return lax.dot_general(
        left, right, (((1,), (1,)), ((), ())), preferred_element_type=jnp.float32
    )


def dot_nn(left, right):
    return jnp.dot(left, right, preferred_element_type=jnp.float32)


def unit_rows(rows):
    wide = rows.astype(jnp.float32)
    inv_norm = lax.rsqrt(jnp.sum(wide * wide, axis=-1, keepdims=True) + norm_eps)
    return wide * inv_norm, inv_norm


def project(key_rows, grad):
    key_dir, key_inv = unit_rows(key_rows)
    along = jnp.sum(key_dir * grad, axis=-1, keepdims=True)
    return key_inv * (grad - key_dir * along)


def fold_rows(terms):
    rows, width = terms.shape
    return jnp.sum(terms.reshape(rows // 8, 8, width), axis=0)


def in_pieces(value, width):
    row = lax.broadcasted_iota(jnp.int32, (note_rows, width), 0)
    note = jnp.zeros((note_rows, width), jnp.float32)
    for part in range(3):
        piece = value.astype(jnp.bfloat16).astype(jnp.float32)
        note = jnp.where(row == part, piece, note)
        value = value - piece
    return note.astype(jnp.bfloat16)


def sum_all(terms):
    return jnp.sum(jnp.sum(terms, axis=0, keepdims=True), axis=-1, keepdims=True)


def seq_place():
    here = lax.axis_index("seq")
    plane = lax.bitwise_and(lax.shift_right_logical(here, 1), 3)
    head = 2 * lax.shift_right_logical(here, 3) + lax.bitwise_and(here, 1)
    return plane, head


def key_slot(plane):
    return lax.bitwise_and(plane, 1)


def query_slot(plane):
    return lax.shift_right_logical(plane, 1)


def params(mebibytes):
    return pltpu.CompilerParams(vmem_limit_bytes=mebibytes * 1024 * 1024)


def pack_kernel(ids_ref, k_ref, v_ref, q_ref, cot_ref, all_ref):
    heads, _, width = all_ref.shape
    rows = k_ref.shape[0]
    ids = ids_ref[...]
    row = lax.broadcasted_iota(jnp.int32, (note_rows, width), 0)
    lane = lax.broadcasted_iota(jnp.int32, (note_rows, width), 1)
    note = jnp.zeros((note_rows, width), jnp.float32)
    for level in range(2):
        count = jnp.sum(jnp.where(ids <= level, 1.0, 0.0), axis=-1, keepdims=True)
        note = jnp.where((row == level) & (lane == 0), count, note)
    note = note.astype(jnp.bfloat16)
    first_query = 2 * rows + note_rows
    for head in range(heads):
        lanes = slice(head * width, (head + 1) * width)
        all_ref[head, 0:rows] = k_ref[:, lanes]
        all_ref[head, rows : 2 * rows] = v_ref[:, lanes]
        all_ref[head, 2 * rows : first_query] = note
        all_ref[head, first_query : first_query + rows] = q_ref[:, lanes]
        all_ref[head, first_query + rows :] = cot_ref[:, lanes]


def run_pack(heads, ids, keys, values, queries, cots):
    rows, features = keys.shape
    shape = (heads, 4 * rows + note_rows, features // heads)
    return pl.pallas_call(
        pack_kernel,
        out_shape=jax.ShapeDtypeStruct(shape, jnp.bfloat16),
        compiler_params=params(56),
        name="pack_heads",
    )(ids, keys, values, queries, cots)


def twice(column):
    return jnp.concatenate([column, column], axis=1)


def wide_as(column, size):
    return column if size == column.shape[1] else twice(column)


def place_of(run, slot, block):
    return pl.multiple_of((2 * run + slot) * block, 64)


def key_spot(first, size):
    return pl.ds(first if isinstance(first, int) else pl.multiple_of(first, 128), size)


def all_chunks(work, some_keys, shared, chunks):
    work(0, some_keys, 0, True)
    work(some_keys, some_keys, 0, False)

    def both(chunk, carry):
        work(2 * some_keys + chunk * k_tile, k_tile, 0, True)
        return carry

    def upper(chunk, carry):
        work(2 * some_keys + chunk * k_tile, k_tile, 1, True)
        return carry

    lax.fori_loop(0, shared, both, 0)
    lax.fori_loop(shared, chunks, upper, 0)


def forward_kernel(
    log_ref,
    own_ref,
    kv_ref,
    qc_ref,
    kc_ref,
    vc_ref,
    prob_ref,
    key_ref,
    val_ref,
    query_ref,
    cot_ref,
    num_ref,
    stat_ref,
    shared_ref,
    wide_scr,
    limit_scr,
    sum_scr,
):
    plane, head = seq_place()
    members, tall, width = own_ref.shape
    rows = (tall - note_rows) // 4
    block = 2 * rows
    runs = members // 2
    queries = query_ref.shape[0]
    coarse = kc_ref.shape[0]
    some_keys = coarse // 2
    fine = key_ref.shape[0] - coarse
    first_query = 2 * rows + note_rows

    def count(notes):
        total = jnp.sum(notes.astype(jnp.float32), axis=0)
        return [jnp.sum(total[level : level + 1]).astype(jnp.int32) for level in range(2)]

    own_counts = count(own_ref[:, 2 * rows : first_query])
    key_counts = [a + b for a, b in zip(own_counts, count(kv_ref[:, 2 * rows :]))]
    query_counts = [a + b for a, b in zip(own_counts, count(qc_ref[:, :note_rows]))]

    def limit_of(place):
        return jnp.where(
            place < query_counts[0],
            key_counts[0],
            jnp.where(place < query_counts[1], key_counts[1], fine),
        )

    own_slot = key_slot(plane)
    for ref, slot in ((own_ref, own_slot), (kv_ref, 1 - own_slot)):
        for run in range(runs):
            pick = slice(2 * run, 2 * run + 2)
            spot = pl.ds(pl.multiple_of(coarse + place_of(run, slot, block), 64), block)
            key_ref[spot, :] = unit_rows(ref[pick, 0:rows].reshape(block, width))[0].astype(
                jnp.bfloat16
            )
            values = ref[pick, rows : 2 * rows].reshape(block, width)
            val_ref[spot, :] = values
            wide_scr[spot, 0:width] = values
    own_half = query_slot(plane)
    for index, half in enumerate((own_half, 1 - own_half)):
        spot = slice(index * some_keys, (index + 1) * some_keys)
        half = pl.ds(pl.multiple_of(half * some_keys, some_keys), some_keys)
        key_ref[spot, :] = kc_ref[half, :]
        val_ref[spot, :] = vc_ref[half, :]
        wide_scr[spot, 0:width] = vc_ref[half, :]
    wide_scr[:, width:] = jnp.ones((coarse + fine, width), jnp.bfloat16)

    own_slot = query_slot(plane)
    for ref, slot, start in ((own_ref, own_slot, first_query), (qc_ref, 1 - own_slot, note_rows)):
        for run in range(runs):
            pick = slice(2 * run, 2 * run + 2)
            spot = pl.ds(place_of(run, slot, block), block)
            query_ref[spot, :] = unit_rows(
                ref[pick, start : start + rows].reshape(block, width)
            )[0].astype(jnp.bfloat16)
            cot_ref[spot, :] = ref[pick, start + rows : start + 2 * rows].reshape(block, width)
    limit_scr[...] = coarse + limit_of(
        lax.broadcasted_iota(jnp.int32, (queries, width), 0)
    )

    sharp = jnp.exp(jnp.full((1, width), log_ref[head], jnp.float32))[:, 0:1]
    slope = sharp * log2_e
    sum_scr[...] = jnp.zeros_like(sum_scr)

    def probs(start, size, part, counts):
        spot = key_spot(start, size)
        place = start + lax.broadcasted_iota(jnp.int32, (1, size), 1)
        for first in range(part * queries // 2, queries, q_rows):
            here = slice(first, first + q_rows)
            cosine = dot_nt(query_ref[here, :], key_ref[spot, :])
            prob = jnp.exp2(cosine * slope - slope)
            seen = place < wide_as(limit_scr[here, :], size)
            prob = jnp.where(seen, prob, 0.0).astype(jnp.bfloat16)
            prob_ref[here, spot] = prob
            if counts:
                sum_scr[here, :] += dot_nn(prob, wide_scr[spot, :])

    shared = (limit_of(queries // 2 - 1) + k_tile - 1) // k_tile
    shared_ref[0] = shared
    all_chunks(probs, some_keys, shared, fine // k_tile)

    num = sum_scr[:, :width]
    num_ref[...] = num
    weighted = jnp.sum(num * cot_ref[...].astype(jnp.float32), axis=-1, keepdims=True)
    row = lax.broadcasted_iota(jnp.int32, (width, width), 0)
    lane = lax.broadcasted_iota(jnp.int32, (width, width), 1)
    parts = queries // width
    for part in range(parts):
        spot = slice(part * width, (part + 1) * width)
        for index, value in ((part, sum_scr[spot, width:]), (parts + part, weighted[spot])):
            stat_ref[index : index + 1, :] = jnp.sum(
                jnp.where(row == lane, value, 0.0), axis=0, keepdims=True
            )


def backward_kernel(
    log_ref,
    shared_ref,
    own_ref,
    qc_ref,
    stat_ref,
    other_stat_ref,
    prob_ref,
    key_ref,
    val_ref,
    query_ref,
    cot_ref,
    num_ref,
    coarse_scale_ref,
    od_ref,
    od_send_ref,
    dkv_ref,
    dkv_send_ref,
    small_ref,
    den_scr,
    mean_scr,
    grad_scr,
    query_turn,
    cot_turn,
    turn_scr,
    score_scr,
):
    plane, head = seq_place()
    members, tall, width = own_ref.shape
    rows = (tall - note_rows) // 4
    block = 2 * rows
    runs = members // 2
    queries = query_ref.shape[0]
    first_query = 2 * rows + note_rows
    coarse = small_ref.shape[0] - note_rows
    fine = key_ref.shape[0] - coarse
    sharp = jnp.exp(jnp.full((1, width), log_ref[head], jnp.float32))[:, 0:1]

    row = lax.broadcasted_iota(jnp.int32, (width, width), 0)
    lane = lax.broadcasted_iota(jnp.int32, (width, width), 1)
    parts = queries // width

    def column(index):
        values = stat_ref[index : index + 1, :] + other_stat_ref[index : index + 1, :]
        return jnp.sum(jnp.where(row == lane, values, 0.0), axis=1, keepdims=True)

    for part in range(parts):
        spot = slice(part * width, (part + 1) * width)
        r_den = 1.0 / column(part)
        den_scr[spot, :] = jnp.broadcast_to(r_den, (width, width))
        mean_scr[spot, :] = jnp.broadcast_to(column(parts + part) * r_den, (width, width))

    grad_scr[...] = jnp.zeros_like(grad_scr)
    query_turn[...] = jnp.transpose(
        query_ref[...].astype(jnp.float32) * (den_scr[...] * sharp)
    ).astype(jnp.bfloat16)
    cot_turn[...] = jnp.transpose(cot_ref[...].astype(jnp.float32) * den_scr[...]).astype(
        jnp.bfloat16
    )

    def grads(start, size, part, counts):
        spot = key_spot(start, size)
        below = part * queries // 2
        dv = dot_nn(cot_turn[:, below:], prob_ref[below:, spot])
        turn_scr[spot, width:] = jnp.transpose(dv).astype(jnp.bfloat16)
        for first in range(below, queries, q_rows):
            here = slice(first, first + q_rows)
            dprob = dot_nt(cot_ref[here, :], val_ref[spot, :])
            dscore = prob_ref[here, spot].astype(jnp.float32) * (
                dprob - wide_as(mean_scr[here, :], size)
            )
            dscore = dscore.astype(jnp.bfloat16)
            score_scr[here, 0:size] = dscore
            if counts:
                grad_scr[here, :] += dot_nn(dscore, key_ref[spot, :])
        dk = dot_nn(query_turn[:, below:], score_scr[below:, 0:size])
        turn_scr[spot, 0:width] = jnp.transpose(dk).astype(jnp.bfloat16)

    all_chunks(grads, coarse // 2, shared_ref[0], fine // k_tile)

    own_slot = query_slot(plane)
    scale = coarse_scale_ref[pl.ds(pl.multiple_of(head * 8, 8), 8), :]
    scale = scale * jnp.where(plane == 0, 1.0, 0.0)
    for ref, slot, start, target in (
        (own_ref, own_slot, first_query, od_ref),
        (qc_ref, 1 - own_slot, note_rows, od_send_ref),
    ):
        for run in range(runs):
            spot = pl.ds(place_of(run, slot, block), block)
            pick = ref[2 * run : 2 * run + 2, start : start + rows]
            q_dir, q_inv = unit_rows(pick.reshape(block, width))
            r_den = den_scr[spot, :]
            grad = grad_scr[spot, :] * (r_den * sharp)
            along = jnp.sum(q_dir * grad, axis=-1, keepdims=True)
            scale = scale + fold_rows(query_ref[spot, :].astype(jnp.float32) * grad)
            to = slice(run * block, (run + 1) * block)
            target[to, 0:width] = (num_ref[spot, :] * r_den).astype(jnp.bfloat16)
            target[to, width:] = (q_inv * (grad - q_dir * along)).astype(jnp.bfloat16)

    own_slot = key_slot(plane)
    for slot, target in ((own_slot, dkv_ref), (1 - own_slot, dkv_send_ref)):
        for run in range(runs):
            spot = pl.ds(pl.multiple_of(coarse + place_of(run, slot, block), 64), block)
            target[run * block : (run + 1) * block, :] = turn_scr[spot, :]
    small_ref[0:coarse, :] = turn_scr[0:coarse, :]
    small_ref[coarse:, :] = in_pieces(sum_all(scale), 2 * width)


def run_fine(log_scale, own_rows, kv_rows, qc_rows, key_coarse, val_coarse, coarse_scale, swap):
    members, tall, width = own_rows.shape
    rows = (tall - note_rows) // 4
    coarse = key_coarse.shape[0]
    queries = 2 * members * rows
    total = coarse + queries
    vmem = pl.BlockSpec(memory_space=pltpu.VMEM)
    smem = pl.BlockSpec(memory_space=pltpu.SMEM)

    def low(*shape):
        return jax.ShapeDtypeStruct(shape, jnp.bfloat16)

    def wide(*shape):
        return jax.ShapeDtypeStruct(shape, jnp.float32)

    prob, keys, values, query, cot, num, stat, shared = pl.pallas_call(
        forward_kernel,
        out_shape=(
            low(queries, total),
            low(total, width),
            low(total, width),
            low(queries, width),
            low(queries, width),
            wide(queries, width),
            wide(2 * queries // width, width),
            jax.ShapeDtypeStruct((1,), jnp.int32),
        ),
        in_specs=[smem] + [vmem] * 5,
        out_specs=(vmem,) * 7 + (smem,),
        scratch_shapes=[
            pltpu.VMEM((total, 2 * width), jnp.bfloat16),
            pltpu.VMEM((queries, width), jnp.int32),
            pltpu.VMEM((queries, 2 * width), jnp.float32),
        ],
        compiler_params=params(16),
        cost_estimate=pl.CostEstimate(
            flops=4 * queries * total * width,
            bytes_accessed=4 * queries * total,
            transcendentals=queries * total,
        ),
        name="fine_forward",
    )(log_scale, own_rows, kv_rows, qc_rows, key_coarse, val_coarse)
    other_stat = swap(stat)
    half = low(queries // 2, 2 * width)
    return pl.pallas_call(
        backward_kernel,
        out_shape=(half, half, half, half, low(coarse + note_rows, 2 * width)),
        in_specs=[smem, smem] + [vmem] * 11,
        out_specs=(vmem,) * 5,
        scratch_shapes=[
            pltpu.VMEM((queries, width), jnp.float32),
            pltpu.VMEM((queries, width), jnp.float32),
            pltpu.VMEM((queries, width), jnp.float32),
            pltpu.VMEM((width, queries), jnp.bfloat16),
            pltpu.VMEM((width, queries), jnp.bfloat16),
            pltpu.VMEM((total, 2 * width), jnp.bfloat16),
            pltpu.VMEM((queries, k_tile), jnp.bfloat16),
        ],
        compiler_params=params(16),
        cost_estimate=pl.CostEstimate(
            flops=8 * queries * total * width,
            bytes_accessed=4 * queries * total,
            transcendentals=0,
        ),
        name="fine_backward",
    )(
        log_scale,
        shared,
        own_rows,
        qc_rows,
        stat,
        other_stat,
        prob,
        keys,
        values,
        query,
        cot,
        num,
        coarse_scale,
    )


def coarse_kernel(
    log_ref,
    row_level_ref,
    col_level_ref,
    q_ref,
    k_ref,
    v_ref,
    cot_ref,
    out_ref,
    dq_ref,
    dk_ref,
    dv_ref,
    scale_ref,
    key_low_ref,
    value_ref,
):
    _, own = seq_place()
    count, features = q_ref.shape
    heads = log_ref.shape[0]
    width = features // heads
    visible = col_level_ref[...] <= row_level_ref[...]
    for head in range(heads):
        lanes = slice(head * width, (head + 1) * width)
        sharp = jnp.exp(jnp.full((1, width), log_ref[head], jnp.float32))[:, 0:1]
        slope = sharp * log2_e
        q_dir, q_inv = unit_rows(q_ref[:, lanes])
        q_low = q_dir.astype(jnp.bfloat16)
        key_low = unit_rows(k_ref[:, lanes])[0].astype(jnp.bfloat16)
        values = v_ref[:, lanes]
        cot = cot_ref[:, lanes]
        prob = jnp.exp2(dot_nt(q_low, key_low) * slope - slope)
        prob = jnp.where(visible, prob, 0.0)
        r_den = 1.0 / jnp.sum(prob, axis=-1, keepdims=True)
        norm_prob = prob * r_den
        dprob = dot_nt(cot, values)
        mean = jnp.sum(norm_prob * dprob, axis=-1, keepdims=True)
        dscore = (norm_prob * (dprob - mean)).astype(jnp.bfloat16)
        norm_low = norm_prob.astype(jnp.bfloat16)
        out_ref[:, lanes] = dot_nn(norm_low, values).astype(jnp.bfloat16)
        grad = sharp * dot_nn(dscore, key_low)
        along = jnp.sum(q_dir * grad, axis=-1, keepdims=True)
        dq_ref[:, lanes] = (q_inv * (grad - q_dir * along)).astype(jnp.bfloat16)
        scale_ref[head * 8 : head * 8 + 8, :] = fold_rows(q_low.astype(jnp.float32) * grad)
        q_turned = jnp.transpose(q_dir).astype(jnp.bfloat16)
        cot_turned = jnp.transpose(cot.astype(jnp.float32)).astype(jnp.bfloat16)
        dk_ref[:, lanes] = sharp * jnp.transpose(dot_nn(q_turned, dscore))
        dv_ref[:, lanes] = jnp.transpose(dot_nn(cot_turned, norm_low))

        @pl.when(own == head)
        def _():
            key_low_ref[...] = key_low
            value_ref[...] = values


def run_coarse(log_scale, levels, queries, keys, values, cots):
    count, features = queries.shape
    heads = log_scale.shape[0]
    width = features // heads
    vmem = pl.BlockSpec(memory_space=pltpu.VMEM)
    wide = jax.ShapeDtypeStruct((count, features), jnp.float32)
    low = jax.ShapeDtypeStruct((count, features), jnp.bfloat16)
    return pl.pallas_call(
        coarse_kernel,
        out_shape=(low, low, wide, wide, jax.ShapeDtypeStruct((heads * 8, width), jnp.float32))
        + (jax.ShapeDtypeStruct((count, width), jnp.bfloat16),) * 2,
        in_specs=[pl.BlockSpec(memory_space=pltpu.SMEM)] + [vmem] * 6,
        compiler_params=params(14),
        cost_estimate=pl.CostEstimate(
            flops=12 * count * count * features,
            bytes_accessed=24 * count * features,
            transcendentals=heads * count * count,
        ),
        name="coarse_attention",
    )(log_scale, levels[:, None], levels[None, :], queries, keys, values, cots)


def small_kernel(own_ref, near_ref, sum_ref, scale_ref):
    coarse, both = sum_ref.shape
    some_keys = coarse // 2
    summed = own_ref[...].astype(jnp.float32) + near_ref[...].astype(jnp.float32)
    own_half = query_slot(seq_place()[0])
    for index, half in enumerate((own_half, 1 - own_half)):
        spot = pl.ds(pl.multiple_of(half * some_keys, some_keys), some_keys)
        sum_ref[spot, :] = summed[index * some_keys : (index + 1) * some_keys].astype(jnp.bfloat16)
    scale = jnp.sum(summed[coarse:, : both // 2], axis=0, keepdims=True)
    scale_ref[...] = jnp.broadcast_to(scale, scale_ref.shape)


def run_small(own, near):
    tall, both = own.shape
    return pl.pallas_call(
        small_kernel,
        out_shape=(
            jax.ShapeDtypeStruct((tall - note_rows, both), jnp.bfloat16),
            jax.ShapeDtypeStruct((8, both // 2), jnp.float32),
        ),
        compiler_params=params(2),
        name="sum_coarse_terms",
    )(own, near)


def sum_kernel(
    od_ref, other_od_ref, dkv_ref, other_dkv_ref, own_ref, *scale_and_all
):
    *scale_refs, all_ref = scale_and_all
    members, tall, width = all_ref.shape
    rows = (tall - note_rows) // 4
    fine = members * rows

    def put(place, value):
        all_ref[:, place * rows : (place + 1) * rows] = value.astype(jnp.bfloat16).reshape(
            members, rows, width
        )

    summed = od_ref[...].astype(jnp.float32) + other_od_ref[...].astype(jnp.float32)
    put(0, summed[:, :width])
    put(1, summed[:, width:])
    summed = dkv_ref[...].astype(jnp.float32) + other_dkv_ref[...].astype(jnp.float32)
    put(2, project(own_ref[:, 0:rows].reshape(fine, width), summed[:, :width]))
    put(3, summed[:, width:])
    scale = scale_refs[0][0:1, 0:1]
    for ref in scale_refs[1:]:
        scale = scale + ref[0:1, 0:1]
    note = in_pieces(scale, width)
    for member in range(members):
        all_ref[member, 4 * rows :] = note


def run_sum(od, other_od, dkv, other_dkv, own_rows, scales):
    return pl.pallas_call(
        sum_kernel,
        out_shape=jax.ShapeDtypeStruct(own_rows.shape, jnp.bfloat16),
        compiler_params=params(6),
        name="sum_pairs",
    )(od, other_od, dkv, other_dkv, own_rows, *scales)


def join_kernel(terms_ref, dk_own_ref, dv_own_ref, k_ref, dk_ref, dv_ref, last_ref):
    heads, _, both = terms_ref.shape
    width = both // 2
    for head in range(heads):
        lanes = slice(head * width, (head + 1) * width)
        terms = terms_ref[head].astype(jnp.float32)
        grad = terms[:, :width] + dk_own_ref[:, lanes]
        dk_ref[:, lanes] = project(k_ref[:, lanes], grad).astype(jnp.bfloat16)
        dv_ref[:, lanes] = (terms[:, width:] + dv_own_ref[:, lanes]).astype(jnp.bfloat16)
    last_ref[...] = jnp.zeros_like(last_ref)


def run_join(terms, dk_own, dv_own, keys):
    low = jax.ShapeDtypeStruct(keys.shape, jnp.bfloat16)
    return pl.pallas_call(
        join_kernel,
        out_shape=(low, low, jax.ShapeDtypeStruct((8, 128), jnp.float32)),
        compiler_params=params(8),
        name="join_coarse",
    )(terms, dk_own, dv_own, keys)


def unpack_kernel(factor, all_ref, _, out_ref, dq_ref, dk_ref, dv_ref, scale_ref):
    heads, tall, width = all_ref.shape
    rows = (tall - note_rows) // 4
    for head in range(heads):
        lanes = slice(head * width, (head + 1) * width)
        for place, ref in enumerate((out_ref, dq_ref, dk_ref, dv_ref)):
            ref[:, lanes] = all_ref[head, place * rows : (place + 1) * rows]
        note = all_ref[head, 4 * rows :].astype(jnp.float32)
        scale_ref[head] = jnp.sum(note[:, 0:1]) * factor


def run_unpack(factor, all_back, after):
    heads, tall, width = all_back.shape
    flat = jax.ShapeDtypeStruct(((tall - note_rows) // 4, heads * width), jnp.bfloat16)
    vmem = pl.BlockSpec(memory_space=pltpu.VMEM)
    return pl.pallas_call(
        partial(unpack_kernel, factor),
        out_shape=(flat,) * 4 + (jax.ShapeDtypeStruct((heads,), jnp.float32),),
        in_specs=[vmem, vmem],
        out_specs=(vmem,) * 4 + (pl.BlockSpec(memory_space=pltpu.SMEM),),
        compiler_params=params(3),
        name="unpack_heads",
    )(all_back, after)


def body(
    q_coarse,
    k_coarse,
    v_coarse,
    cot_coarse,
    coarse_ids,
    q_fine,
    k_fine,
    v_fine,
    cot_fine,
    fine_ids,
    log_scale,
):
    heads = log_scale.shape[0]
    coarse = q_coarse.shape[1]
    rows = q_fine.shape[1]
    seq = lax.axis_size("seq")
    images = lax.axis_size("dp")
    groups = [
        [8 * (h // 2) + 2 * plane + h % 2 for h in range(heads)] for plane in range(planes)
    ]

    def exchange(parts):
        return lax.all_to_all(parts, "seq", 0, 0, axis_index_groups=groups, tiled=True)

    def to_plane(array, flip):
        return lax.ppermute(array, "seq", [(i, i ^ (2 * flip)) for i in range(seq)])

    def to_image(array, flip):
        return lax.ppermute(array, "dp", [(i, i ^ flip) for i in range(images)])

    def to_both(array, image_flip, plane_flip):
        there = [
            (i ^ image_flip) * seq + (j ^ (2 * plane_flip))
            for i in range(images)
            for j in range(seq)
        ]
        return lax.ppermute(array, ("dp", "seq"), list(enumerate(there)))

    own_rows = exchange(run_pack(heads, fine_ids, k_fine[0], v_fine[0], q_fine[0], cot_fine[0]))
    kv_rows = to_plane(own_rows[:, : 2 * rows + note_rows], 1)
    qc_rows = to_plane(own_rows[:, 2 * rows :], 3)

    out_c, dq_c, dk_own, dv_own, scale_c, key_c, val_c = run_coarse(
        log_scale, coarse_ids[0], q_coarse[0], k_coarse[0], v_coarse[0], cot_coarse[0]
    )
    od, od_send, dkv, dkv_send, small = run_fine(
        log_scale, own_rows, kv_rows, qc_rows, key_c, val_c, scale_c, lambda stat: to_plane(stat, 3)
    )

    small_sum, scale = run_small(small, to_plane(small, 1))
    of_image = lax.all_gather(small_sum, "seq", axis=0, axis_index_groups=groups)

    other_dkv = to_plane(dkv_send, 1)
    other_od = to_plane(od_send, 3)
    scale = scale + to_image(scale, 1) + to_image(scale, 2) + to_image(scale, 3)
    scales = [scale, to_plane(scale, 3), to_image(scale, 4), to_both(scale, 4, 3)]
    all_parts = run_sum(od, other_od, dkv, other_dkv, own_rows, scales)
    all_back = exchange(all_parts)
    dk_c, dv_c, after = run_join(of_image, dk_own, dv_own, k_coarse[0])
    factor = 1.0 / math.sqrt(images * (coarse + seq * rows))
    fine_out, fine_dq, fine_dk, fine_dv, grad_scale = run_unpack(factor, all_back, after)
    return (
        out_c[None],
        dq_c[None],
        dk_c[None],
        dv_c[None],
        fine_out[None],
        fine_dq[None],
        fine_dk[None],
        fine_dv[None],
        grad_scale,
    )


def solution(mesh):
    whole = P("dp", None, None)
    split = P("dp", "seq", None)
    return jax.shard_map(
        body,
        mesh=mesh,
        in_specs=(whole,) * 4 + (P("dp", None),) + (split,) * 4 + (P("dp", "seq"), P()),
        out_specs=(whole,) * 4 + (split,) * 4 + (P(),),
        check_vma=False,
    )
```

```python
import math
from functools import partial

import jax
import jax.numpy as jnp
from jax import lax
from jax.experimental import pallas as pl
from jax.experimental.pallas import tpu as pltpu
from jax.sharding import PartitionSpec as P

norm_eps = 1e-06
log2_e = 1.4426950408889634
k_tile = 256
note_rows = 16

planes = 4


def dot_nt(left, right):
    return lax.dot_general(
        left, right, (((1,), (1,)), ((), ())), preferred_element_type=jnp.float32
    )


def dot_nn(left, right):
    return jnp.dot(left, right, preferred_element_type=jnp.float32)


def unit_rows(rows):
    wide = rows.astype(jnp.float32)
    inv_norm = lax.rsqrt(jnp.sum(wide * wide, axis=-1, keepdims=True) + norm_eps)
    return wide * inv_norm, inv_norm


def project(key_rows, grad):
    key_dir, key_inv = unit_rows(key_rows)
    along = jnp.sum(key_dir * grad, axis=-1, keepdims=True)
    return key_inv * (grad - key_dir * along)


def fold_rows(terms):
    rows, width = terms.shape
    return jnp.sum(terms.reshape(rows // 8, 8, width), axis=0)


def in_pieces(value, width):
    row = lax.broadcasted_iota(jnp.int32, (note_rows, width), 0)
    note = jnp.zeros((note_rows, width), jnp.float32)
    for part in range(3):
        piece = value.astype(jnp.bfloat16).astype(jnp.float32)
        note = jnp.where(row == part, piece, note)
        value = value - piece
    return note.astype(jnp.bfloat16)


def sum_all(terms):
    return jnp.sum(jnp.sum(terms, axis=0, keepdims=True), axis=-1, keepdims=True)


def seq_place():
    here = lax.axis_index("seq")
    plane = lax.bitwise_and(lax.shift_right_logical(here, 1), 3)
    head = 2 * lax.shift_right_logical(here, 3) + lax.bitwise_and(here, 1)
    return plane, head


def key_slot(plane):
    return lax.bitwise_and(plane, 1)


def query_slot(plane):
    return lax.shift_right_logical(plane, 1)


def params(mebibytes):
    return pltpu.CompilerParams(vmem_limit_bytes=mebibytes * 1024 * 1024)


def pack_kernel(ids_ref, k_ref, v_ref, q_ref, cot_ref, all_ref):
    heads, _, width = all_ref.shape
    rows = k_ref.shape[0]
    ids = ids_ref[...]
    row = lax.broadcasted_iota(jnp.int32, (note_rows, width), 0)
    lane = lax.broadcasted_iota(jnp.int32, (note_rows, width), 1)
    note = jnp.zeros((note_rows, width), jnp.float32)
    for level in range(2):
        count = jnp.sum(jnp.where(ids <= level, 1.0, 0.0), axis=-1, keepdims=True)
        note = jnp.where((row == level) & (lane == 0), count, note)
    note = note.astype(jnp.bfloat16)
    first_query = 2 * rows + note_rows
    for head in range(heads):
        lanes = slice(head * width, (head + 1) * width)
        all_ref[head, 0:rows] = k_ref[:, lanes]
        all_ref[head, rows : 2 * rows] = v_ref[:, lanes]
        all_ref[head, 2 * rows : first_query] = note
        all_ref[head, first_query : first_query + rows] = q_ref[:, lanes]
        all_ref[head, first_query + rows :] = cot_ref[:, lanes]


def run_pack(heads, ids, keys, values, queries, cots):
    rows, features = keys.shape
    shape = (heads, 4 * rows + note_rows, features // heads)
    return pl.pallas_call(
        pack_kernel,
        out_shape=jax.ShapeDtypeStruct(shape, jnp.bfloat16),
        compiler_params=params(56),
        name="pack_heads",
    )(ids, keys, values, queries, cots)


def twice(column):
    return jnp.concatenate([column, column], axis=1)


def wide_as(column, size):
    return column if size == column.shape[1] else twice(column)


def place_of(run, slot, block):
    return pl.multiple_of((2 * run + slot) * block, 64)


def key_spot(first, size):
    return pl.ds(first if isinstance(first, int) else pl.multiple_of(first, 128), size)


def coarse_chunks(work, some_keys):
    work(0, some_keys, 0, True)
    work(some_keys, some_keys, 0, False)


def fine_chunks(work, coarse, shared, chunks):
    def both(chunk, carry):
        work(coarse + chunk * k_tile, k_tile, 0, True)
        return carry

    def upper(chunk, carry):
        work(coarse + chunk * k_tile, k_tile, 1, True)
        return carry

    lax.fori_loop(0, shared, both, 0)
    lax.fori_loop(shared, chunks, upper, 0)


def forward_kernel(
    log_ref,
    own_ref,
    kv_ref,
    qc_ref,
    kc_ref,
    vc_ref,
    prob_ref,
    key_ref,
    val_ref,
    query_ref,
    cot_ref,
    num_ref,
    stat_ref,
    shared_ref,
    wide_scr,
    limit_scr,
    sum_scr,
):
    plane, head = seq_place()
    members, tall, width = own_ref.shape
    rows = (tall - note_rows) // 4
    block = 2 * rows
    runs = members // 2
    queries = query_ref.shape[0]
    coarse = kc_ref.shape[0]
    some_keys = coarse // 2
    fine = key_ref.shape[0] - coarse
    first_query = 2 * rows + note_rows

    def count(notes):
        total = jnp.sum(notes.astype(jnp.float32), axis=0)
        return [jnp.sum(total[level : level + 1]).astype(jnp.int32) for level in range(2)]

    own_counts = count(own_ref[:, 2 * rows : first_query])
    key_counts = [a + b for a, b in zip(own_counts, count(kv_ref[:, 2 * rows :]))]
    query_counts = [a + b for a, b in zip(own_counts, count(qc_ref[:, :note_rows]))]

    def limit_of(place):
        return jnp.where(
            place < query_counts[0],
            key_counts[0],
            jnp.where(place < query_counts[1], key_counts[1], fine),
        )

    own_slot = key_slot(plane)
    for ref, slot in ((own_ref, own_slot), (kv_ref, 1 - own_slot)):
        for run in range(runs):
            pick = slice(2 * run, 2 * run + 2)
            spot = pl.ds(pl.multiple_of(coarse + place_of(run, slot, block), 64), block)
            key_ref[spot, :] = unit_rows(ref[pick, 0:rows].reshape(block, width))[0].astype(
                jnp.bfloat16
            )
            values = ref[pick, rows : 2 * rows].reshape(block, width)
            val_ref[spot, :] = values
            wide_scr[spot, 0:width] = values
    own_half = query_slot(plane)
    for index, half in enumerate((own_half, 1 - own_half)):
        spot = slice(index * some_keys, (index + 1) * some_keys)
        half = pl.ds(pl.multiple_of(half * some_keys, some_keys), some_keys)
        key_ref[spot, :] = kc_ref[half, :]
        val_ref[spot, :] = vc_ref[half, :]
        wide_scr[spot, 0:width] = vc_ref[half, :]
    wide_scr[:, width:] = jnp.ones((coarse + fine, width), jnp.bfloat16)

    own_slot = query_slot(plane)
    for ref, slot, start in ((own_ref, own_slot, first_query), (qc_ref, 1 - own_slot, note_rows)):
        for run in range(runs):
            pick = slice(2 * run, 2 * run + 2)
            spot = pl.ds(place_of(run, slot, block), block)
            query_ref[spot, :] = unit_rows(
                ref[pick, start : start + rows].reshape(block, width)
            )[0].astype(jnp.bfloat16)
            cot_ref[spot, :] = ref[pick, start + rows : start + 2 * rows].reshape(block, width)
    limit_scr[...] = coarse + limit_of(
        lax.broadcasted_iota(jnp.int32, (queries, width), 0)
    )

    sharp = jnp.exp(jnp.full((1, width), log_ref[head], jnp.float32))[:, 0:1]
    slope = sharp * log2_e
    sum_scr[...] = jnp.zeros_like(sum_scr)

    def probs(start, size, part, counts):
        first = part * queries // 2
        spot = key_spot(start, size)
        cosine = dot_nt(query_ref[first:, :], key_ref[spot, :])
        prob = jnp.exp2(cosine * slope - slope)
        place = start + lax.broadcasted_iota(jnp.int32, (1, size), 1)
        seen = place < wide_as(limit_scr[first:, :], size)
        prob = jnp.where(seen, prob, 0.0).astype(jnp.bfloat16)
        prob_ref[first:, spot] = prob
        if counts:
            sum_scr[first:, :] += dot_nn(prob, wide_scr[spot, :])

    shared = (limit_of(queries // 2 - 1) + k_tile - 1) // k_tile
    shared_ref[0] = shared
    coarse_chunks(probs, some_keys)
    fine_chunks(probs, coarse, shared, fine // k_tile)

    num = sum_scr[:, :width]
    num_ref[...] = num
    weighted = jnp.sum(num * cot_ref[...].astype(jnp.float32), axis=-1, keepdims=True)
    row = lax.broadcasted_iota(jnp.int32, (width, width), 0)
    lane = lax.broadcasted_iota(jnp.int32, (width, width), 1)
    parts = queries // width
    for part in range(parts):
        spot = slice(part * width, (part + 1) * width)
        for index, value in ((part, sum_scr[spot, width:]), (parts + part, weighted[spot])):
            stat_ref[index : index + 1, :] = jnp.sum(
                jnp.where(row == lane, value, 0.0), axis=0, keepdims=True
            )


def key_grads(refs, targets, start, size, first, counts):
    prob_ref, key_ref, val_ref, cot_ref, mean_ref, query_turn, cot_turn, grad_ref = refs
    dk_target, dv_target = targets
    spot = key_spot(start, size)
    prob = prob_ref[first:, spot]
    dprob = dot_nt(cot_ref[first:, :], val_ref[spot, :])
    dscore = prob.astype(jnp.float32) * (dprob - wide_as(mean_ref[first:, :], size))
    dscore = dscore.astype(jnp.bfloat16)
    if counts:
        grad_ref[first:, :] += dot_nn(dscore, key_ref[spot, :])
    dk = dot_nn(query_turn[:, first:], dscore)
    dv = dot_nn(cot_turn[:, first:], prob)
    dk_target[...] = jnp.transpose(dk).astype(jnp.bfloat16)
    dv_target[...] = jnp.transpose(dv).astype(jnp.bfloat16)


def coarse_back_kernel(
    log_ref,
    stat_ref,
    other_stat_ref,
    prob_ref,
    key_ref,
    val_ref,
    query_ref,
    cot_ref,
    small_ref,
    den_ref,
    mean_ref,
    grad_ref,
    query_turn,
    cot_turn,
):
    _, head = seq_place()
    queries, width = query_ref.shape
    coarse = small_ref.shape[0]
    sharp = jnp.exp(jnp.full((1, width), log_ref[head], jnp.float32))[:, 0:1]
    row = lax.broadcasted_iota(jnp.int32, (width, width), 0)
    lane = lax.broadcasted_iota(jnp.int32, (width, width), 1)
    parts = queries // width

    def column(index):
        values = stat_ref[index : index + 1, :] + other_stat_ref[index : index + 1, :]
        return jnp.sum(jnp.where(row == lane, values, 0.0), axis=1, keepdims=True)

    for part in range(parts):
        spot = slice(part * width, (part + 1) * width)
        r_den = 1.0 / column(part)
        den_ref[spot, :] = jnp.broadcast_to(r_den, (width, width))
        mean_ref[spot, :] = jnp.broadcast_to(column(parts + part) * r_den, (width, width))

    grad_ref[...] = jnp.zeros_like(grad_ref)
    query_turn[...] = jnp.transpose(
        query_ref[...].astype(jnp.float32) * (den_ref[...] * sharp)
    ).astype(jnp.bfloat16)
    cot_turn[...] = jnp.transpose(cot_ref[...].astype(jnp.float32) * den_ref[...]).astype(
        jnp.bfloat16
    )
    refs = (prob_ref, key_ref, val_ref, cot_ref, mean_ref, query_turn, cot_turn, grad_ref)

    def work(start, size, part, counts):
        spot = slice(start, start + size)
        targets = (small_ref.at[spot, 0:width], small_ref.at[spot, width:])
        key_grads(refs, targets, start, size, 0, counts)

    coarse_chunks(work, coarse // 2)


def fine_back_kernel(
    log_ref,
    shared_ref,
    own_ref,
    qc_ref,
    prob_ref,
    key_ref,
    val_ref,
    query_ref,
    cot_ref,
    num_ref,
    den_ref,
    mean_ref,
    grad_in_ref,
    query_turn,
    cot_turn,
    coarse_scale_ref,
    od_ref,
    od_send_ref,
    dkv_ref,
    dkv_send_ref,
    scale_ref,
    grad_scr,
    turn_scr,
):
    plane, head = seq_place()
    members, tall, width = own_ref.shape
    rows = (tall - note_rows) // 4
    block = 2 * rows
    runs = members // 2
    queries = query_ref.shape[0]
    first_query = 2 * rows + note_rows
    fine = turn_scr.shape[0]
    coarse = key_ref.shape[0] - fine
    sharp = jnp.exp(jnp.full((1, width), log_ref[head], jnp.float32))[:, 0:1]
    grad_scr[...] = grad_in_ref[...]
    refs = (prob_ref, key_ref, val_ref, cot_ref, mean_ref, query_turn, cot_turn, grad_scr)

    def work(start, size, part, counts):
        spot = key_spot(start - coarse, size)
        targets = (turn_scr.at[spot, 0:width], turn_scr.at[spot, width:])
        key_grads(refs, targets, start, size, part * queries // 2, counts)

    fine_chunks(work, coarse, shared_ref[0], fine // k_tile)

    own_slot = query_slot(plane)
    scale = coarse_scale_ref[pl.ds(pl.multiple_of(head * 8, 8), 8), :]
    scale = scale * jnp.where(plane == 0, 1.0, 0.0)
    for ref, slot, start, target in (
        (own_ref, own_slot, first_query, od_ref),
        (qc_ref, 1 - own_slot, note_rows, od_send_ref),
    ):
        for run in range(runs):
            spot = pl.ds(place_of(run, slot, block), block)
            pick = ref[2 * run : 2 * run + 2, start : start + rows]
            q_dir, q_inv = unit_rows(pick.reshape(block, width))
            r_den = den_ref[spot, :]
            grad = grad_scr[spot, :] * (r_den * sharp)
            along = jnp.sum(q_dir * grad, axis=-1, keepdims=True)
            scale = scale + fold_rows(query_ref[spot, :].astype(jnp.float32) * grad)
            to = slice(run * block, (run + 1) * block)
            target[to, 0:width] = (num_ref[spot, :] * r_den).astype(jnp.bfloat16)
            target[to, width:] = (q_inv * (grad - q_dir * along)).astype(jnp.bfloat16)

    own_slot = key_slot(plane)
    for slot, target in ((own_slot, dkv_ref), (1 - own_slot, dkv_send_ref)):
        for run in range(runs):
            spot = pl.ds(place_of(run, slot, block), block)
            target[run * block : (run + 1) * block, :] = turn_scr[spot, :]
    scale_ref[...] = jnp.broadcast_to(sum_all(scale), scale_ref.shape)


def run_fine(log_scale, own_rows, kv_rows, qc_rows, key_coarse, val_coarse, coarse_scale, swap):
    members, tall, width = own_rows.shape
    rows = (tall - note_rows) // 4
    coarse = key_coarse.shape[0]
    queries = 2 * members * rows
    total = coarse + queries
    vmem = pl.BlockSpec(memory_space=pltpu.VMEM)
    smem = pl.BlockSpec(memory_space=pltpu.SMEM)

    def low(*shape):
        return jax.ShapeDtypeStruct(shape, jnp.bfloat16)

    def wide(*shape):
        return jax.ShapeDtypeStruct(shape, jnp.float32)

    prob, keys, values, query, cot, num, stat, shared = pl.pallas_call(
        forward_kernel,
        out_shape=(
            low(queries, total),
            low(total, width),
            low(total, width),
            low(queries, width),
            low(queries, width),
            wide(queries, width),
            wide(2 * queries // width, width),
            jax.ShapeDtypeStruct((1,), jnp.int32),
        ),
        in_specs=[smem] + [vmem] * 5,
        out_specs=(vmem,) * 7 + (smem,),
        scratch_shapes=[
            pltpu.VMEM((total, 2 * width), jnp.bfloat16),
            pltpu.VMEM((queries, width), jnp.int32),
            pltpu.VMEM((queries, 2 * width), jnp.float32),
        ],
        compiler_params=params(16),
        cost_estimate=pl.CostEstimate(
            flops=4 * queries * total * width,
            bytes_accessed=4 * queries * total,
            transcendentals=queries * total,
        ),
        name="fine_forward",
    )(log_scale, own_rows, kv_rows, qc_rows, key_coarse, val_coarse)
    other_stat = swap(stat)
    small, den, mean, grad, query_turned, cot_turned = pl.pallas_call(
        coarse_back_kernel,
        out_shape=(
            low(coarse, 2 * width),
            wide(queries, width),
            wide(queries, width),
            wide(queries, width),
            low(width, queries),
            low(width, queries),
        ),
        in_specs=[smem] + [vmem] * 7,
        out_specs=(vmem,) * 6,
        compiler_params=params(12),
        cost_estimate=pl.CostEstimate(
            flops=8 * queries * coarse * width,
            bytes_accessed=4 * queries * coarse,
            transcendentals=0,
        ),
        name="coarse_key_grads",
    )(log_scale, stat, other_stat, prob, keys, values, query, cot)
    half = low(queries // 2, 2 * width)
    outs = pl.pallas_call(
        fine_back_kernel,
        out_shape=(half, half, half, half, wide(8, width)),
        in_specs=[smem, smem] + [vmem] * 14,
        out_specs=(vmem,) * 5,
        scratch_shapes=[
            pltpu.VMEM((queries, width), jnp.float32),
            pltpu.VMEM((queries, 2 * width), jnp.bfloat16),
        ],
        compiler_params=params(16),
        cost_estimate=pl.CostEstimate(
            flops=8 * queries * queries * width,
            bytes_accessed=4 * queries * queries,
            transcendentals=0,
        ),
        name="fine_backward",
    )(
        log_scale,
        shared,
        own_rows,
        qc_rows,
        prob,
        keys,
        values,
        query,
        cot,
        num,
        den,
        mean,
        grad,
        query_turned,
        cot_turned,
        coarse_scale,
    )
    return small, outs


def coarse_kernel(
    log_ref,
    row_level_ref,
    col_level_ref,
    q_ref,
    k_ref,
    v_ref,
    cot_ref,
    out_ref,
    dq_ref,
    dk_ref,
    dv_ref,
    scale_ref,
    key_low_ref,
    value_ref,
):
    _, own = seq_place()
    count, features = q_ref.shape
    heads = log_ref.shape[0]
    width = features // heads
    visible = col_level_ref[...] <= row_level_ref[...]
    for head in range(heads):
        lanes = slice(head * width, (head + 1) * width)
        sharp = jnp.exp(jnp.full((1, width), log_ref[head], jnp.float32))[:, 0:1]
        slope = sharp * log2_e
        q_dir, q_inv = unit_rows(q_ref[:, lanes])
        q_low = q_dir.astype(jnp.bfloat16)
        key_low = unit_rows(k_ref[:, lanes])[0].astype(jnp.bfloat16)
        values = v_ref[:, lanes]
        cot = cot_ref[:, lanes]
        prob = jnp.exp2(dot_nt(q_low, key_low) * slope - slope)
        prob = jnp.where(visible, prob, 0.0)
        r_den = 1.0 / jnp.sum(prob, axis=-1, keepdims=True)
        norm_prob = prob * r_den
        dprob = dot_nt(cot, values)
        mean = jnp.sum(norm_prob * dprob, axis=-1, keepdims=True)
        dscore = (norm_prob * (dprob - mean)).astype(jnp.bfloat16)
        norm_low = norm_prob.astype(jnp.bfloat16)
        out_ref[:, lanes] = dot_nn(norm_low, values).astype(jnp.bfloat16)
        grad = sharp * dot_nn(dscore, key_low)
        along = jnp.sum(q_dir * grad, axis=-1, keepdims=True)
        dq_ref[:, lanes] = (q_inv * (grad - q_dir * along)).astype(jnp.bfloat16)
        scale_ref[head * 8 : head * 8 + 8, :] = fold_rows(q_low.astype(jnp.float32) * grad)
        q_turned = jnp.transpose(q_dir).astype(jnp.bfloat16)
        cot_turned = jnp.transpose(cot.astype(jnp.float32)).astype(jnp.bfloat16)
        dk_ref[:, lanes] = sharp * jnp.transpose(dot_nn(q_turned, dscore))
        dv_ref[:, lanes] = jnp.transpose(dot_nn(cot_turned, norm_low))

        @pl.when(own == head)
        def _():
            key_low_ref[...] = key_low
            value_ref[...] = values


def run_coarse(log_scale, levels, queries, keys, values, cots):
    count, features = queries.shape
    heads = log_scale.shape[0]
    width = features // heads
    vmem = pl.BlockSpec(memory_space=pltpu.VMEM)
    wide = jax.ShapeDtypeStruct((count, features), jnp.float32)
    low = jax.ShapeDtypeStruct((count, features), jnp.bfloat16)
    return pl.pallas_call(
        coarse_kernel,
        out_shape=(low, low, wide, wide, jax.ShapeDtypeStruct((heads * 8, width), jnp.float32))
        + (jax.ShapeDtypeStruct((count, width), jnp.bfloat16),) * 2,
        in_specs=[pl.BlockSpec(memory_space=pltpu.SMEM)] + [vmem] * 6,
        compiler_params=params(14),
        cost_estimate=pl.CostEstimate(
            flops=12 * count * count * features,
            bytes_accessed=24 * count * features,
            transcendentals=heads * count * count,
        ),
        name="coarse_attention",
    )(log_scale, levels[:, None], levels[None, :], queries, keys, values, cots)


def small_kernel(own_ref, near_ref, _, sum_ref):
    some_keys = sum_ref.shape[0] // 2
    summed = own_ref[...].astype(jnp.float32) + near_ref[...].astype(jnp.float32)
    own_half = query_slot(seq_place()[0])
    for index, half in enumerate((own_half, 1 - own_half)):
        spot = pl.ds(pl.multiple_of(half * some_keys, some_keys), some_keys)
        sum_ref[spot, :] = summed[index * some_keys : (index + 1) * some_keys].astype(jnp.bfloat16)


def run_small(own, near, after):
    return pl.pallas_call(
        small_kernel,
        out_shape=jax.ShapeDtypeStruct(own.shape, jnp.bfloat16),
        compiler_params=params(2),
        name="sum_coarse_terms",
    )(own, near, after)


def sum_kernel(
    od_ref, other_od_ref, dkv_ref, other_dkv_ref, own_ref, *scale_and_all
):
    *scale_refs, all_ref = scale_and_all
    members, tall, width = all_ref.shape
    rows = (tall - note_rows) // 4
    fine = members * rows

    def put(place, value):
        all_ref[:, place * rows : (place + 1) * rows] = value.astype(jnp.bfloat16).reshape(
            members, rows, width
        )

    summed = od_ref[...].astype(jnp.float32) + other_od_ref[...].astype(jnp.float32)
    put(0, summed[:, :width])
    put(1, summed[:, width:])
    summed = dkv_ref[...].astype(jnp.float32) + other_dkv_ref[...].astype(jnp.float32)
    put(2, project(own_ref[:, 0:rows].reshape(fine, width), summed[:, :width]))
    put(3, summed[:, width:])
    scale = scale_refs[0][0:1, 0:1]
    for ref in scale_refs[1:]:
        scale = scale + ref[0:1, 0:1]
    note = in_pieces(scale, width)
    for member in range(members):
        all_ref[member, 4 * rows :] = note


def run_sum(od, other_od, dkv, other_dkv, own_rows, scales):
    return pl.pallas_call(
        sum_kernel,
        out_shape=jax.ShapeDtypeStruct(own_rows.shape, jnp.bfloat16),
        compiler_params=params(6),
        name="sum_pairs",
    )(od, other_od, dkv, other_dkv, own_rows, *scales)


def join_kernel(terms_ref, dk_own_ref, dv_own_ref, k_ref, dk_ref, dv_ref, last_ref):
    heads, _, both = terms_ref.shape
    width = both // 2
    for head in range(heads):
        lanes = slice(head * width, (head + 1) * width)
        terms = terms_ref[head].astype(jnp.float32)
        grad = terms[:, :width] + dk_own_ref[:, lanes]
        dk_ref[:, lanes] = project(k_ref[:, lanes], grad).astype(jnp.bfloat16)
        dv_ref[:, lanes] = (terms[:, width:] + dv_own_ref[:, lanes]).astype(jnp.bfloat16)
    last_ref[...] = jnp.zeros_like(last_ref)


def run_join(terms, dk_own, dv_own, keys):
    low = jax.ShapeDtypeStruct(keys.shape, jnp.bfloat16)
    return pl.pallas_call(
        join_kernel,
        out_shape=(low, low, jax.ShapeDtypeStruct((8, 128), jnp.float32)),
        compiler_params=params(8),
        name="join_coarse",
    )(terms, dk_own, dv_own, keys)


def unpack_kernel(factor, all_ref, _, out_ref, dq_ref, dk_ref, dv_ref, scale_ref):
    heads, tall, width = all_ref.shape
    rows = (tall - note_rows) // 4
    for head in range(heads):
        lanes = slice(head * width, (head + 1) * width)
        for place, ref in enumerate((out_ref, dq_ref, dk_ref, dv_ref)):
            ref[:, lanes] = all_ref[head, place * rows : (place + 1) * rows]
        note = all_ref[head, 4 * rows :].astype(jnp.float32)
        scale_ref[head] = jnp.sum(note[:, 0:1]) * factor


def run_unpack(factor, all_back, after):
    heads, tall, width = all_back.shape
    flat = jax.ShapeDtypeStruct(((tall - note_rows) // 4, heads * width), jnp.bfloat16)
    vmem = pl.BlockSpec(memory_space=pltpu.VMEM)
    return pl.pallas_call(
        partial(unpack_kernel, factor),
        out_shape=(flat,) * 4 + (jax.ShapeDtypeStruct((heads,), jnp.float32),),
        in_specs=[vmem, vmem],
        out_specs=(vmem,) * 4 + (pl.BlockSpec(memory_space=pltpu.SMEM),),
        compiler_params=params(3),
        name="unpack_heads",
    )(all_back, after)


def body(
    q_coarse,
    k_coarse,
    v_coarse,
    cot_coarse,
    coarse_ids,
    q_fine,
    k_fine,
    v_fine,
    cot_fine,
    fine_ids,
    log_scale,
):
    heads = log_scale.shape[0]
    coarse = q_coarse.shape[1]
    rows = q_fine.shape[1]
    seq = lax.axis_size("seq")
    images = lax.axis_size("dp")
    groups = [
        [8 * (h // 2) + 2 * plane + h % 2 for h in range(heads)] for plane in range(planes)
    ]

    def exchange(parts):
        return lax.all_to_all(parts, "seq", 0, 0, axis_index_groups=groups, tiled=True)

    def to_plane(array, flip):
        return lax.ppermute(array, "seq", [(i, i ^ (2 * flip)) for i in range(seq)])

    def to_image(array, flip):
        return lax.ppermute(array, "dp", [(i, i ^ flip) for i in range(images)])

    def to_both(array, image_flip, plane_flip):
        there = [
            (i ^ image_flip) * seq + (j ^ (2 * plane_flip))
            for i in range(images)
            for j in range(seq)
        ]
        return lax.ppermute(array, ("dp", "seq"), list(enumerate(there)))

    own_rows = exchange(run_pack(heads, fine_ids, k_fine[0], v_fine[0], q_fine[0], cot_fine[0]))
    kv_rows = to_plane(own_rows[:, : 2 * rows + note_rows], 1)
    qc_rows = to_plane(own_rows[:, 2 * rows :], 3)

    out_c, dq_c, dk_own, dv_own, scale_c, key_c, val_c = run_coarse(
        log_scale, coarse_ids[0], q_coarse[0], k_coarse[0], v_coarse[0], cot_coarse[0]
    )
    small, (od, od_send, dkv, dkv_send, scale) = run_fine(
        log_scale, own_rows, kv_rows, qc_rows, key_c, val_c, scale_c, lambda stat: to_plane(stat, 3)
    )

    small_sum = run_small(small, to_plane(small, 1), scale)
    of_image = lax.all_gather(small_sum, "seq", axis=0, axis_index_groups=groups)

    other_dkv = to_plane(dkv_send, 1)
    other_od = to_plane(od_send, 3)
    scale = scale + to_image(scale, 1) + to_image(scale, 2) + to_image(scale, 3)
    scales = [scale, to_image(scale, 4)]
    for flip in (1, 2, 3):
        scales += [to_plane(scale, flip), to_both(scale, 4, flip)]
    all_parts = run_sum(od, other_od, dkv, other_dkv, own_rows, scales)
    all_back = exchange(all_parts)
    dk_c, dv_c, after = run_join(of_image, dk_own, dv_own, k_coarse[0])
    factor = 1.0 / math.sqrt(images * (coarse + seq * rows))
    fine_out, fine_dq, fine_dk, fine_dv, grad_scale = run_unpack(factor, all_back, after)
    return (
        out_c[None],
        dq_c[None],
        dk_c[None],
        dv_c[None],
        fine_out[None],
        fine_dq[None],
        fine_dk[None],
        fine_dv[None],
        grad_scale,
    )


def solution(mesh):
    whole = P("dp", None, None)
    split = P("dp", "seq", None)
    return jax.shard_map(
        body,
        mesh=mesh,
        in_specs=(whole,) * 4 + (P("dp", None),) + (split,) * 4 + (P("dp", "seq"), P()),
        out_specs=(whole,) * 4 + (split,) * 4 + (P(),),
        check_vma=False,
    )
```

```python
import math
from functools import partial

import jax
import jax.numpy as jnp
from jax import lax
from jax.experimental import pallas as pl
from jax.experimental.pallas import tpu as pltpu
from jax.sharding import PartitionSpec as P

norm_eps = 1e-06
log2_e = 1.4426950408889634
k_tile = 256
note_rows = 16

planes = 4


def dot_nt(left, right):
    return lax.dot_general(
        left, right, (((1,), (1,)), ((), ())), preferred_element_type=jnp.float32
    )


def dot_nn(left, right):
    return jnp.dot(left, right, preferred_element_type=jnp.float32)


def unit_rows(rows):
    wide = rows.astype(jnp.float32)
    inv_norm = lax.rsqrt(jnp.sum(wide * wide, axis=-1, keepdims=True) + norm_eps)
    return wide * inv_norm, inv_norm


def project(key_rows, grad):
    key_dir, key_inv = unit_rows(key_rows)
    along = jnp.sum(key_dir * grad, axis=-1, keepdims=True)
    return key_inv * (grad - key_dir * along)


def fold_rows(terms):
    rows, width = terms.shape
    return jnp.sum(terms.reshape(rows // 8, 8, width), axis=0)


def in_pieces(value, width):
    row = lax.broadcasted_iota(jnp.int32, (note_rows, width), 0)
    note = jnp.zeros((note_rows, width), jnp.float32)
    for part in range(3):
        piece = value.astype(jnp.bfloat16).astype(jnp.float32)
        note = jnp.where(row == part, piece, note)
        value = value - piece
    return note.astype(jnp.bfloat16)


def sum_all(terms):
    return jnp.sum(jnp.sum(terms, axis=0, keepdims=True), axis=-1, keepdims=True)


def seq_place():
    here = lax.axis_index("seq")
    plane = lax.bitwise_and(lax.shift_right_logical(here, 1), 3)
    head = 2 * lax.shift_right_logical(here, 3) + lax.bitwise_and(here, 1)
    return plane, head


def key_slot(plane):
    return lax.bitwise_and(plane, 1)


def query_slot(plane):
    return lax.shift_right_logical(plane, 1)


def params(mebibytes):
    return pltpu.CompilerParams(vmem_limit_bytes=mebibytes * 1024 * 1024)


def pack_kernel(ids_ref, k_ref, v_ref, q_ref, cot_ref, all_ref):
    heads, _, width = all_ref.shape
    rows = k_ref.shape[0]
    ids = ids_ref[...]
    row = lax.broadcasted_iota(jnp.int32, (note_rows, width), 0)
    lane = lax.broadcasted_iota(jnp.int32, (note_rows, width), 1)
    note = jnp.zeros((note_rows, width), jnp.float32)
    for level in range(2):
        count = jnp.sum(jnp.where(ids <= level, 1.0, 0.0), axis=-1, keepdims=True)
        note = jnp.where((row == level) & (lane == 0), count, note)
    note = note.astype(jnp.bfloat16)
    first_query = 2 * rows + note_rows
    for head in range(heads):
        lanes = slice(head * width, (head + 1) * width)
        all_ref[head, 0:rows] = k_ref[:, lanes]
        all_ref[head, rows : 2 * rows] = v_ref[:, lanes]
        all_ref[head, 2 * rows : first_query] = note
        all_ref[head, first_query : first_query + rows] = q_ref[:, lanes]
        all_ref[head, first_query + rows :] = cot_ref[:, lanes]


def run_pack(heads, ids, keys, values, queries, cots):
    rows, features = keys.shape
    shape = (heads, 4 * rows + note_rows, features // heads)
    return pl.pallas_call(
        pack_kernel,
        out_shape=jax.ShapeDtypeStruct(shape, jnp.bfloat16),
        compiler_params=params(56),
        name="pack_heads",
    )(ids, keys, values, queries, cots)


def twice(column):
    return jnp.concatenate([column, column], axis=1)


def wide_as(column, size):
    return column if size == column.shape[1] else twice(column)


def place_of(run, slot, block):
    return pl.multiple_of((2 * run + slot) * block, 64)


def key_spot(first, size):
    return pl.ds(first if isinstance(first, int) else pl.multiple_of(first, 128), size)


def coarse_chunks(work, some_keys):
    work(0, some_keys, 0, True)
    work(some_keys, some_keys, 0, False)


def fine_chunks(work, coarse, shared, chunks):
    def both(chunk, carry):
        work(coarse + chunk * k_tile, k_tile, 0, True)
        return carry

    def upper(chunk, carry):
        work(coarse + chunk * k_tile, k_tile, 1, True)
        return carry

    lax.fori_loop(0, shared, both, 0)
    lax.fori_loop(shared, chunks, upper, 0)


def forward_kernel(
    log_ref,
    own_ref,
    kv_ref,
    qc_ref,
    kc_ref,
    vc_ref,
    prob_ref,
    key_ref,
    val_ref,
    query_ref,
    cot_ref,
    num_ref,
    stat_ref,
    shared_ref,
    wide_scr,
    limit_scr,
    sum_scr,
):
    plane, head = seq_place()
    members, tall, width = own_ref.shape
    rows = (tall - note_rows) // 4
    block = 2 * rows
    runs = members // 2
    queries = query_ref.shape[0]
    coarse = kc_ref.shape[0]
    some_keys = coarse // 2
    fine = key_ref.shape[0] - coarse
    first_query = 2 * rows + note_rows

    def count(notes):
        total = jnp.sum(notes.astype(jnp.float32), axis=0)
        return [jnp.sum(total[level : level + 1]).astype(jnp.int32) for level in range(2)]

    own_counts = count(own_ref[:, 2 * rows : first_query])
    key_counts = [a + b for a, b in zip(own_counts, count(kv_ref[:, 2 * rows :]))]
    query_counts = [a + b for a, b in zip(own_counts, count(qc_ref[:, :note_rows]))]

    def limit_of(place):
        return jnp.where(
            place < query_counts[0],
            key_counts[0],
            jnp.where(place < query_counts[1], key_counts[1], fine),
        )

    own_slot = key_slot(plane)
    for ref, slot in ((own_ref, own_slot), (kv_ref, 1 - own_slot)):
        for run in range(runs):
            pick = slice(2 * run, 2 * run + 2)
            spot = pl.ds(pl.multiple_of(coarse + place_of(run, slot, block), 64), block)
            key_ref[spot, :] = unit_rows(ref[pick, 0:rows].reshape(block, width))[0].astype(
                jnp.bfloat16
            )
            values = ref[pick, rows : 2 * rows].reshape(block, width)
            val_ref[spot, :] = values
            wide_scr[spot, 0:width] = values
    own_half = query_slot(plane)
    for index, half in enumerate((own_half, 1 - own_half)):
        spot = slice(index * some_keys, (index + 1) * some_keys)
        half = pl.ds(pl.multiple_of(half * some_keys, some_keys), some_keys)
        key_ref[spot, :] = kc_ref[half, :]
        val_ref[spot, :] = vc_ref[half, :]
        wide_scr[spot, 0:width] = vc_ref[half, :]
    wide_scr[:, width:] = jnp.ones((coarse + fine, width), jnp.bfloat16)

    own_slot = query_slot(plane)
    for ref, slot, start in ((own_ref, own_slot, first_query), (qc_ref, 1 - own_slot, note_rows)):
        for run in range(runs):
            pick = slice(2 * run, 2 * run + 2)
            spot = pl.ds(place_of(run, slot, block), block)
            query_ref[spot, :] = unit_rows(
                ref[pick, start : start + rows].reshape(block, width)
            )[0].astype(jnp.bfloat16)
            cot_ref[spot, :] = ref[pick, start + rows : start + 2 * rows].reshape(block, width)
    limit_scr[...] = coarse + limit_of(
        lax.broadcasted_iota(jnp.int32, (queries, width), 0)
    )

    sharp = jnp.exp(jnp.full((1, width), log_ref[head], jnp.float32))[:, 0:1]
    slope = sharp * log2_e
    sum_scr[...] = jnp.zeros_like(sum_scr)

    def probs(start, size, part, counts):
        first = part * queries // 2
        spot = key_spot(start, size)
        cosine = dot_nt(query_ref[first:, :], key_ref[spot, :])
        prob = jnp.exp2(cosine * slope - slope)
        place = start + lax.broadcasted_iota(jnp.int32, (1, size), 1)
        seen = place < wide_as(limit_scr[first:, :], size)
        prob = jnp.where(seen, prob, 0.0).astype(jnp.bfloat16)
        prob_ref[first:, spot] = prob
        if counts:
            sum_scr[first:, :] += dot_nn(prob, wide_scr[spot, :])

    shared = (limit_of(queries // 2 - 1) + k_tile - 1) // k_tile
    shared_ref[0] = shared
    coarse_chunks(probs, some_keys)
    fine_chunks(probs, coarse, shared, fine // k_tile)

    num = sum_scr[:, :width]
    num_ref[...] = num
    weighted = jnp.sum(num * cot_ref[...].astype(jnp.float32), axis=-1, keepdims=True)
    row = lax.broadcasted_iota(jnp.int32, (width, width), 0)
    lane = lax.broadcasted_iota(jnp.int32, (width, width), 1)
    parts = queries // width
    for part in range(parts):
        spot = slice(part * width, (part + 1) * width)
        for index, value in ((part, sum_scr[spot, width:]), (parts + part, weighted[spot])):
            stat_ref[index : index + 1, :] = jnp.sum(
                jnp.where(row == lane, value, 0.0), axis=0, keepdims=True
            )


def key_grads(refs, targets, start, size, first, counts):
    prob_ref, key_ref, val_ref, cot_ref, mean_ref, query_turn, cot_turn, grad_ref = refs
    dk_target, dv_target = targets
    spot = key_spot(start, size)
    prob = prob_ref[first:, spot]
    dprob = dot_nt(cot_ref[first:, :], val_ref[spot, :])
    dscore = prob.astype(jnp.float32) * (dprob - wide_as(mean_ref[first:, :], size))
    dscore = dscore.astype(jnp.bfloat16)
    if counts:
        grad_ref[first:, :] += dot_nn(dscore, key_ref[spot, :])
    dk = dot_nn(query_turn[:, first:], dscore)
    dv = dot_nn(cot_turn[:, first:], prob)
    dk_target[...] = jnp.transpose(dk).astype(jnp.bfloat16)
    dv_target[...] = jnp.transpose(dv).astype(jnp.bfloat16)


def coarse_back_kernel(
    log_ref,
    stat_ref,
    other_stat_ref,
    prob_ref,
    key_ref,
    val_ref,
    query_ref,
    cot_ref,
    small_ref,
    den_ref,
    mean_ref,
    grad_ref,
    query_turn,
    cot_turn,
):
    _, head = seq_place()
    queries, width = query_ref.shape
    coarse = small_ref.shape[0]
    sharp = jnp.exp(jnp.full((1, width), log_ref[head], jnp.float32))[:, 0:1]
    row = lax.broadcasted_iota(jnp.int32, (width, width), 0)
    lane = lax.broadcasted_iota(jnp.int32, (width, width), 1)
    parts = queries // width

    def column(index):
        values = stat_ref[index : index + 1, :] + other_stat_ref[index : index + 1, :]
        return jnp.sum(jnp.where(row == lane, values, 0.0), axis=1, keepdims=True)

    for part in range(parts):
        spot = slice(part * width, (part + 1) * width)
        r_den = 1.0 / column(part)
        den_ref[spot, :] = jnp.broadcast_to(r_den, (width, width))
        mean_ref[spot, :] = jnp.broadcast_to(column(parts + part) * r_den, (width, width))

    grad_ref[...] = jnp.zeros_like(grad_ref)
    query_turn[...] = jnp.transpose(
        query_ref[...].astype(jnp.float32) * (den_ref[...] * sharp)
    ).astype(jnp.bfloat16)
    cot_turn[...] = jnp.transpose(cot_ref[...].astype(jnp.float32) * den_ref[...]).astype(
        jnp.bfloat16
    )
    refs = (prob_ref, key_ref, val_ref, cot_ref, mean_ref, query_turn, cot_turn, grad_ref)

    def work(start, size, part, counts):
        spot = slice(start, start + size)
        targets = (small_ref.at[spot, 0:width], small_ref.at[spot, width:])
        key_grads(refs, targets, start, size, 0, counts)

    coarse_chunks(work, coarse // 2)


def fine_back_kernel(
    log_ref,
    shared_ref,
    own_ref,
    qc_ref,
    prob_ref,
    key_ref,
    val_ref,
    query_ref,
    cot_ref,
    num_ref,
    den_ref,
    mean_ref,
    grad_in_ref,
    query_turn,
    cot_turn,
    coarse_scale_ref,
    od_ref,
    od_send_ref,
    dkv_ref,
    dkv_send_ref,
    scale_ref,
    grad_scr,
    turn_scr,
):
    plane, head = seq_place()
    members, tall, width = own_ref.shape
    rows = (tall - note_rows) // 4
    block = 2 * rows
    runs = members // 2
    queries = query_ref.shape[0]
    first_query = 2 * rows + note_rows
    fine = turn_scr.shape[0]
    coarse = key_ref.shape[0] - fine
    sharp = jnp.exp(jnp.full((1, width), log_ref[head], jnp.float32))[:, 0:1]
    grad_scr[...] = grad_in_ref[...]
    refs = (prob_ref, key_ref, val_ref, cot_ref, mean_ref, query_turn, cot_turn, grad_scr)

    def work(start, size, part, counts):
        spot = key_spot(start - coarse, size)
        targets = (turn_scr.at[spot, 0:width], turn_scr.at[spot, width:])
        key_grads(refs, targets, start, size, part * queries // 2, counts)

    fine_chunks(work, coarse, shared_ref[0], fine // k_tile)

    own_slot = query_slot(plane)
    scale = coarse_scale_ref[pl.ds(pl.multiple_of(head * 8, 8), 8), :]
    scale = scale * jnp.where(plane == 0, 1.0, 0.0)
    for ref, slot, start, target in (
        (own_ref, own_slot, first_query, od_ref),
        (qc_ref, 1 - own_slot, note_rows, od_send_ref),
    ):
        for run in range(runs):
            spot = pl.ds(place_of(run, slot, block), block)
            pick = ref[2 * run : 2 * run + 2, start : start + rows]
            q_dir, q_inv = unit_rows(pick.reshape(block, width))
            r_den = den_ref[spot, :]
            grad = grad_scr[spot, :] * (r_den * sharp)
            along = jnp.sum(q_dir * grad, axis=-1, keepdims=True)
            scale = scale + fold_rows(query_ref[spot, :].astype(jnp.float32) * grad)
            to = slice(run * block, (run + 1) * block)
            target[to, 0:width] = (num_ref[spot, :] * r_den).astype(jnp.bfloat16)
            target[to, width:] = (q_inv * (grad - q_dir * along)).astype(jnp.bfloat16)

    own_slot = key_slot(plane)
    for slot, target in ((own_slot, dkv_ref), (1 - own_slot, dkv_send_ref)):
        for run in range(runs):
            spot = pl.ds(place_of(run, slot, block), block)
            target[run * block : (run + 1) * block, :] = turn_scr[spot, :]
    scale_ref[...] = jnp.broadcast_to(sum_all(scale), scale_ref.shape)


def run_fine(log_scale, own_rows, kv_rows, qc_rows, key_coarse, val_coarse, coarse_scale, swap):
    members, tall, width = own_rows.shape
    rows = (tall - note_rows) // 4
    coarse = key_coarse.shape[0]
    queries = 2 * members * rows
    total = coarse + queries
    vmem = pl.BlockSpec(memory_space=pltpu.VMEM)
    smem = pl.BlockSpec(memory_space=pltpu.SMEM)

    def low(*shape):
        return jax.ShapeDtypeStruct(shape, jnp.bfloat16)

    def wide(*shape):
        return jax.ShapeDtypeStruct(shape, jnp.float32)

    prob, keys, values, query, cot, num, stat, shared = pl.pallas_call(
        forward_kernel,
        out_shape=(
            low(queries, total),
            low(total, width),
            low(total, width),
            low(queries, width),
            low(queries, width),
            wide(queries, width),
            wide(2 * queries // width, width),
            jax.ShapeDtypeStruct((1,), jnp.int32),
        ),
        in_specs=[smem] + [vmem] * 5,
        out_specs=(vmem,) * 7 + (smem,),
        scratch_shapes=[
            pltpu.VMEM((total, 2 * width), jnp.bfloat16),
            pltpu.VMEM((queries, width), jnp.int32),
            pltpu.VMEM((queries, 2 * width), jnp.float32),
        ],
        compiler_params=params(16),
        cost_estimate=pl.CostEstimate(
            flops=4 * queries * total * width,
            bytes_accessed=4 * queries * total,
            transcendentals=queries * total,
        ),
        name="fine_forward",
    )(log_scale, own_rows, kv_rows, qc_rows, key_coarse, val_coarse)
    other_stat = swap(stat)
    small, den, mean, grad, query_turned, cot_turned = pl.pallas_call(
        coarse_back_kernel,
        out_shape=(
            low(coarse, 2 * width),
            wide(queries, width),
            wide(queries, width),
            wide(queries, width),
            low(width, queries),
            low(width, queries),
        ),
        in_specs=[smem] + [vmem] * 7,
        out_specs=(vmem,) * 6,
        compiler_params=params(12),
        cost_estimate=pl.CostEstimate(
            flops=8 * queries * coarse * width,
            bytes_accessed=4 * queries * coarse,
            transcendentals=0,
        ),
        name="coarse_key_grads",
    )(log_scale, stat, other_stat, prob, keys, values, query, cot)
    half = low(queries // 2, 2 * width)
    outs = pl.pallas_call(
        fine_back_kernel,
        out_shape=(half, half, half, half, wide(8, width)),
        in_specs=[smem, smem] + [vmem] * 14,
        out_specs=(vmem,) * 5,
        scratch_shapes=[
            pltpu.VMEM((queries, width), jnp.float32),
            pltpu.VMEM((queries, 2 * width), jnp.bfloat16),
        ],
        compiler_params=params(16),
        cost_estimate=pl.CostEstimate(
            flops=8 * queries * queries * width,
            bytes_accessed=4 * queries * queries,
            transcendentals=0,
        ),
        name="fine_backward",
    )(
        log_scale,
        shared,
        own_rows,
        qc_rows,
        prob,
        keys,
        values,
        query,
        cot,
        num,
        den,
        mean,
        grad,
        query_turned,
        cot_turned,
        coarse_scale,
    )
    return small, outs


def coarse_kernel(
    log_ref,
    row_level_ref,
    col_level_ref,
    q_ref,
    k_ref,
    v_ref,
    cot_ref,
    out_ref,
    dq_ref,
    dk_ref,
    dv_ref,
    scale_ref,
    key_low_ref,
    value_ref,
):
    _, own = seq_place()
    count, features = q_ref.shape
    heads = log_ref.shape[0]
    width = features // heads
    visible = col_level_ref[...] <= row_level_ref[...]
    for head in range(heads):
        lanes = slice(head * width, (head + 1) * width)
        sharp = jnp.exp(jnp.full((1, width), log_ref[head], jnp.float32))[:, 0:1]
        slope = sharp * log2_e
        q_dir, q_inv = unit_rows(q_ref[:, lanes])
        q_low = q_dir.astype(jnp.bfloat16)
        key_low = unit_rows(k_ref[:, lanes])[0].astype(jnp.bfloat16)
        values = v_ref[:, lanes]
        cot = cot_ref[:, lanes]
        prob = jnp.exp2(dot_nt(q_low, key_low) * slope - slope)
        prob = jnp.where(visible, prob, 0.0)
        r_den = 1.0 / jnp.sum(prob, axis=-1, keepdims=True)
        norm_prob = prob * r_den
        dprob = dot_nt(cot, values)
        mean = jnp.sum(norm_prob * dprob, axis=-1, keepdims=True)
        dscore = (norm_prob * (dprob - mean)).astype(jnp.bfloat16)
        norm_low = norm_prob.astype(jnp.bfloat16)
        out_ref[:, lanes] = dot_nn(norm_low, values).astype(jnp.bfloat16)
        grad = sharp * dot_nn(dscore, key_low)
        along = jnp.sum(q_dir * grad, axis=-1, keepdims=True)
        dq_ref[:, lanes] = (q_inv * (grad - q_dir * along)).astype(jnp.bfloat16)
        scale_ref[head * 8 : head * 8 + 8, :] = fold_rows(q_low.astype(jnp.float32) * grad)
        q_turned = jnp.transpose(q_dir).astype(jnp.bfloat16)
        cot_turned = jnp.transpose(cot.astype(jnp.float32)).astype(jnp.bfloat16)
        dk_ref[:, lanes] = sharp * jnp.transpose(dot_nn(q_turned, dscore))
        dv_ref[:, lanes] = jnp.transpose(dot_nn(cot_turned, norm_low))

        @pl.when(own == head)
        def _():
            key_low_ref[...] = key_low
            value_ref[...] = values


def run_coarse(log_scale, levels, queries, keys, values, cots):
    count, features = queries.shape
    heads = log_scale.shape[0]
    width = features // heads
    vmem = pl.BlockSpec(memory_space=pltpu.VMEM)
    wide = jax.ShapeDtypeStruct((count, features), jnp.float32)
    low = jax.ShapeDtypeStruct((count, features), jnp.bfloat16)
    return pl.pallas_call(
        coarse_kernel,
        out_shape=(low, low, wide, wide, jax.ShapeDtypeStruct((heads * 8, width), jnp.float32))
        + (jax.ShapeDtypeStruct((count, width), jnp.bfloat16),) * 2,
        in_specs=[pl.BlockSpec(memory_space=pltpu.SMEM)] + [vmem] * 6,
        compiler_params=params(14),
        cost_estimate=pl.CostEstimate(
            flops=12 * count * count * features,
            bytes_accessed=24 * count * features,
            transcendentals=heads * count * count,
        ),
        name="coarse_attention",
    )(log_scale, levels[:, None], levels[None, :], queries, keys, values, cots)


def small_kernel(own_ref, near_ref, scale_ref, near_scale_ref, sum_ref, pair_ref):
    pair_ref[...] = scale_ref[...] + near_scale_ref[...]
    some_keys = sum_ref.shape[0] // 2
    summed = own_ref[...].astype(jnp.float32) + near_ref[...].astype(jnp.float32)
    own_half = query_slot(seq_place()[0])
    for index, half in enumerate((own_half, 1 - own_half)):
        spot = pl.ds(pl.multiple_of(half * some_keys, some_keys), some_keys)
        sum_ref[spot, :] = summed[index * some_keys : (index + 1) * some_keys].astype(jnp.bfloat16)


def run_small(own, near, scale, near_scale):
    return pl.pallas_call(
        small_kernel,
        out_shape=(
            jax.ShapeDtypeStruct(own.shape, jnp.bfloat16),
            jax.ShapeDtypeStruct(scale.shape, jnp.float32),
        ),
        compiler_params=params(2),
        name="sum_coarse_terms",
    )(own, near, scale, near_scale)


def sum_kernel(
    od_ref, other_od_ref, dkv_ref, other_dkv_ref, own_ref, *scale_and_all
):
    *scale_refs, all_ref = scale_and_all
    members, tall, width = all_ref.shape
    rows = (tall - note_rows) // 4
    fine = members * rows

    def put(place, value):
        all_ref[:, place * rows : (place + 1) * rows] = value.astype(jnp.bfloat16).reshape(
            members, rows, width
        )

    summed = od_ref[...].astype(jnp.float32) + other_od_ref[...].astype(jnp.float32)
    put(0, summed[:, :width])
    put(1, summed[:, width:])
    summed = dkv_ref[...].astype(jnp.float32) + other_dkv_ref[...].astype(jnp.float32)
    put(2, project(own_ref[:, 0:rows].reshape(fine, width), summed[:, :width]))
    put(3, summed[:, width:])
    scale = scale_refs[0][0:1, 0:1]
    for ref in scale_refs[1:]:
        scale = scale + ref[0:1, 0:1]
    note = in_pieces(scale, width)
    for member in range(members):
        all_ref[member, 4 * rows :] = note


def run_sum(od, other_od, dkv, other_dkv, own_rows, scales):
    return pl.pallas_call(
        sum_kernel,
        out_shape=jax.ShapeDtypeStruct(own_rows.shape, jnp.bfloat16),
        compiler_params=params(6),
        name="sum_pairs",
    )(od, other_od, dkv, other_dkv, own_rows, *scales)


def join_kernel(terms_ref, dk_own_ref, dv_own_ref, k_ref, dk_ref, dv_ref, last_ref):
    heads, _, both = terms_ref.shape
    width = both // 2
    for head in range(heads):
        lanes = slice(head * width, (head + 1) * width)
        terms = terms_ref[head].astype(jnp.float32)
        grad = terms[:, :width] + dk_own_ref[:, lanes]
        dk_ref[:, lanes] = project(k_ref[:, lanes], grad).astype(jnp.bfloat16)
        dv_ref[:, lanes] = (terms[:, width:] + dv_own_ref[:, lanes]).astype(jnp.bfloat16)
    last_ref[...] = jnp.zeros_like(last_ref)


def run_join(terms, dk_own, dv_own, keys):
    low = jax.ShapeDtypeStruct(keys.shape, jnp.bfloat16)
    return pl.pallas_call(
        join_kernel,
        out_shape=(low, low, jax.ShapeDtypeStruct((8, 128), jnp.float32)),
        compiler_params=params(8),
        name="join_coarse",
    )(terms, dk_own, dv_own, keys)


def unpack_kernel(factor, all_ref, _, out_ref, dq_ref, dk_ref, dv_ref, scale_ref):
    heads, tall, width = all_ref.shape
    rows = (tall - note_rows) // 4
    for head in range(heads):
        lanes = slice(head * width, (head + 1) * width)
        for place, ref in enumerate((out_ref, dq_ref, dk_ref, dv_ref)):
            ref[:, lanes] = all_ref[head, place * rows : (place + 1) * rows]
        note = all_ref[head, 4 * rows :].astype(jnp.float32)
        scale_ref[head] = jnp.sum(note[:, 0:1]) * factor


def run_unpack(factor, all_back, after):
    heads, tall, width = all_back.shape
    flat = jax.ShapeDtypeStruct(((tall - note_rows) // 4, heads * width), jnp.bfloat16)
    vmem = pl.BlockSpec(memory_space=pltpu.VMEM)
    return pl.pallas_call(
        partial(unpack_kernel, factor),
        out_shape=(flat,) * 4 + (jax.ShapeDtypeStruct((heads,), jnp.float32),),
        in_specs=[vmem, vmem],
        out_specs=(vmem,) * 4 + (pl.BlockSpec(memory_space=pltpu.SMEM),),
        compiler_params=params(3),
        name="unpack_heads",
    )(all_back, after)


def body(
    q_coarse,
    k_coarse,
    v_coarse,
    cot_coarse,
    coarse_ids,
    q_fine,
    k_fine,
    v_fine,
    cot_fine,
    fine_ids,
    log_scale,
):
    heads = log_scale.shape[0]
    coarse = q_coarse.shape[1]
    rows = q_fine.shape[1]
    seq = lax.axis_size("seq")
    images = lax.axis_size("dp")
    groups = [
        [8 * (h // 2) + 2 * plane + h % 2 for h in range(heads)] for plane in range(planes)
    ]

    def exchange(parts):
        return lax.all_to_all(parts, "seq", 0, 0, axis_index_groups=groups, tiled=True)

    def to_plane(array, flip):
        return lax.ppermute(array, "seq", [(i, i ^ (2 * flip)) for i in range(seq)])

    def to_image(array, flip):
        return lax.ppermute(array, "dp", [(i, i ^ flip) for i in range(images)])

    def to_both(array, image_flip, plane_flip):
        there = [
            (i ^ image_flip) * seq + (j ^ (2 * plane_flip))
            for i in range(images)
            for j in range(seq)
        ]
        return lax.ppermute(array, ("dp", "seq"), list(enumerate(there)))

    own_rows = exchange(run_pack(heads, fine_ids, k_fine[0], v_fine[0], q_fine[0], cot_fine[0]))
    kv_rows = to_plane(own_rows[:, : 2 * rows + note_rows], 1)
    qc_rows = to_plane(own_rows[:, 2 * rows :], 3)

    out_c, dq_c, dk_own, dv_own, scale_c, key_c, val_c = run_coarse(
        log_scale, coarse_ids[0], q_coarse[0], k_coarse[0], v_coarse[0], cot_coarse[0]
    )
    small, (od, od_send, dkv, dkv_send, scale) = run_fine(
        log_scale, own_rows, kv_rows, qc_rows, key_c, val_c, scale_c, lambda stat: to_plane(stat, 3)
    )

    small_sum, scale = run_small(small, to_plane(small, 1), scale, to_plane(scale, 1))
    of_image = lax.all_gather(small_sum, "seq", axis=0, axis_index_groups=groups)

    other_dkv = to_plane(dkv_send, 1)
    other_od = to_plane(od_send, 3)
    scale = scale + to_image(scale, 1) + to_image(scale, 2) + to_image(scale, 3)
    scales = [scale, to_plane(scale, 3), to_image(scale, 4), to_both(scale, 4, 3)]
    all_parts = run_sum(od, other_od, dkv, other_dkv, own_rows, scales)
    all_back = exchange(all_parts)
    dk_c, dv_c, after = run_join(of_image, dk_own, dv_own, k_coarse[0])
    factor = 1.0 / math.sqrt(images * (coarse + seq * rows))
    fine_out, fine_dq, fine_dk, fine_dv, grad_scale = run_unpack(factor, all_back, after)
    return (
        out_c[None],
        dq_c[None],
        dk_c[None],
        dv_c[None],
        fine_out[None],
        fine_dq[None],
        fine_dk[None],
        fine_dv[None],
        grad_scale,
    )


def solution(mesh):
    whole = P("dp", None, None)
    split = P("dp", "seq", None)
    return jax.shard_map(
        body,
        mesh=mesh,
        in_specs=(whole,) * 4 + (P("dp", None),) + (split,) * 4 + (P("dp", "seq"), P()),
        out_specs=(whole,) * 4 + (split,) * 4 + (P(),),
        check_vma=False,
    )
```

```python
import math
from functools import partial

import jax
import jax.numpy as jnp
from jax import lax
from jax.experimental import pallas as pl
from jax.experimental.pallas import tpu as pltpu
from jax.sharding import PartitionSpec as P

norm_eps = 1e-06
log2_e = 1.4426950408889634
k_tile = 256
note_rows = 16

planes = 4


def dot_nt(left, right):
    return lax.dot_general(
        left, right, (((1,), (1,)), ((), ())), preferred_element_type=jnp.float32
    )


def dot_nn(left, right):
    return jnp.dot(left, right, preferred_element_type=jnp.float32)


def unit_rows(rows):
    wide = rows.astype(jnp.float32)
    inv_norm = lax.rsqrt(jnp.sum(wide * wide, axis=-1, keepdims=True) + norm_eps)
    return wide * inv_norm, inv_norm


def project(key_rows, grad):
    key_dir, key_inv = unit_rows(key_rows)
    along = jnp.sum(key_dir * grad, axis=-1, keepdims=True)
    return key_inv * (grad - key_dir * along)


def fold_rows(terms):
    rows, width = terms.shape
    return jnp.sum(terms.reshape(rows // 8, 8, width), axis=0)


def in_pieces(value, width):
    row = lax.broadcasted_iota(jnp.int32, (note_rows, width), 0)
    note = jnp.zeros((note_rows, width), jnp.float32)
    for part in range(3):
        piece = value.astype(jnp.bfloat16).astype(jnp.float32)
        note = jnp.where(row == part, piece, note)
        value = value - piece
    return note.astype(jnp.bfloat16)


def sum_all(terms):
    return jnp.sum(jnp.sum(terms, axis=0, keepdims=True), axis=-1, keepdims=True)


def seq_place():
    here = lax.axis_index("seq")
    plane = lax.bitwise_and(lax.shift_right_logical(here, 1), 3)
    head = 2 * lax.shift_right_logical(here, 3) + lax.bitwise_and(here, 1)
    return plane, head


def key_slot(plane):
    return lax.bitwise_and(plane, 1)


def query_slot(plane):
    return lax.shift_right_logical(plane, 1)


def params(mebibytes):
    return pltpu.CompilerParams(vmem_limit_bytes=mebibytes * 1024 * 1024)


def pack_kernel(ids_ref, k_ref, v_ref, q_ref, cot_ref, all_ref):
    heads, _, width = all_ref.shape
    rows = k_ref.shape[0]
    ids = ids_ref[...]
    row = lax.broadcasted_iota(jnp.int32, (note_rows, width), 0)
    lane = lax.broadcasted_iota(jnp.int32, (note_rows, width), 1)
    note = jnp.zeros((note_rows, width), jnp.float32)
    for level in range(2):
        count = jnp.sum(jnp.where(ids <= level, 1.0, 0.0), axis=-1, keepdims=True)
        note = jnp.where((row == level) & (lane == 0), count, note)
    note = note.astype(jnp.bfloat16)
    first_query = 2 * rows + note_rows
    for head in range(heads):
        lanes = slice(head * width, (head + 1) * width)
        all_ref[head, 0:rows] = k_ref[:, lanes]
        all_ref[head, rows : 2 * rows] = v_ref[:, lanes]
        all_ref[head, 2 * rows : first_query] = note
        all_ref[head, first_query : first_query + rows] = q_ref[:, lanes]
        all_ref[head, first_query + rows :] = cot_ref[:, lanes]


def run_pack(heads, ids, keys, values, queries, cots):
    rows, features = keys.shape
    shape = (heads, 4 * rows + note_rows, features // heads)
    return pl.pallas_call(
        pack_kernel,
        out_shape=jax.ShapeDtypeStruct(shape, jnp.bfloat16),
        compiler_params=params(56),
        name="pack_heads",
    )(ids, keys, values, queries, cots)


def twice(column):
    return jnp.concatenate([column, column], axis=1)


def wide_as(column, size):
    return column if size == column.shape[1] else twice(column)


def place_of(run, slot, block):
    return pl.multiple_of((2 * run + slot) * block, 64)


def key_spot(first, size):
    return pl.ds(first if isinstance(first, int) else pl.multiple_of(first, 128), size)


def coarse_chunks(work, some_keys):
    work(0, some_keys, 0, True)
    work(some_keys, some_keys, 0, False)


def fine_chunks(work, coarse, shared, chunks):
    def both(chunk, carry):
        work(coarse + chunk * k_tile, k_tile, 0, True)
        return carry

    def upper(chunk, carry):
        work(coarse + chunk * k_tile, k_tile, 1, True)
        return carry

    lax.fori_loop(0, shared, both, 0)
    lax.fori_loop(shared, chunks, upper, 0)


def forward_kernel(
    log_ref,
    own_ref,
    kv_ref,
    qc_ref,
    kc_ref,
    vc_ref,
    prob_ref,
    key_ref,
    val_ref,
    query_ref,
    cot_ref,
    num_ref,
    stat_ref,
    shared_ref,
    wide_scr,
    limit_scr,
    sum_scr,
):
    plane, head = seq_place()
    members, tall, width = own_ref.shape
    rows = (tall - note_rows) // 4
    block = 2 * rows
    runs = members // 2
    queries = query_ref.shape[0]
    coarse = kc_ref.shape[0]
    some_keys = coarse // 2
    fine = key_ref.shape[0] - coarse
    first_query = 2 * rows + note_rows

    def count(notes):
        total = jnp.sum(notes.astype(jnp.float32), axis=0)
        return [jnp.sum(total[level : level + 1]).astype(jnp.int32) for level in range(2)]

    own_counts = count(own_ref[:, 2 * rows : first_query])
    key_counts = [a + b for a, b in zip(own_counts, count(kv_ref[:, 2 * rows :]))]
    query_counts = [a + b for a, b in zip(own_counts, count(qc_ref[:, :note_rows]))]

    def limit_of(place):
        return jnp.where(
            place < query_counts[0],
            key_counts[0],
            jnp.where(place < query_counts[1], key_counts[1], fine),
        )

    own_slot = key_slot(plane)
    for ref, slot in ((own_ref, own_slot), (kv_ref, 1 - own_slot)):
        for run in range(runs):
            pick = slice(2 * run, 2 * run + 2)
            spot = pl.ds(pl.multiple_of(coarse + place_of(run, slot, block), 64), block)
            key_ref[spot, :] = unit_rows(ref[pick, 0:rows].reshape(block, width))[0].astype(
                jnp.bfloat16
            )
            values = ref[pick, rows : 2 * rows].reshape(block, width)
            val_ref[spot, :] = values
            wide_scr[spot, 0:width] = values
    own_half = query_slot(plane)
    for index, half in enumerate((own_half, 1 - own_half)):
        spot = slice(index * some_keys, (index + 1) * some_keys)
        half = pl.ds(pl.multiple_of(half * some_keys, some_keys), some_keys)
        key_ref[spot, :] = kc_ref[half, :]
        val_ref[spot, :] = vc_ref[half, :]
        wide_scr[spot, 0:width] = vc_ref[half, :]
    wide_scr[:, width:] = jnp.ones((coarse + fine, width), jnp.bfloat16)

    own_slot = query_slot(plane)
    for ref, slot, start in ((own_ref, own_slot, first_query), (qc_ref, 1 - own_slot, note_rows)):
        for run in range(runs):
            pick = slice(2 * run, 2 * run + 2)
            spot = pl.ds(place_of(run, slot, block), block)
            query_ref[spot, :] = unit_rows(
                ref[pick, start : start + rows].reshape(block, width)
            )[0].astype(jnp.bfloat16)
            cot_ref[spot, :] = ref[pick, start + rows : start + 2 * rows].reshape(block, width)
    limit_scr[...] = coarse + limit_of(
        lax.broadcasted_iota(jnp.int32, (queries, width), 0)
    )

    sharp = jnp.exp(jnp.full((1, width), log_ref[head], jnp.float32))[:, 0:1]
    slope = sharp * log2_e
    sum_scr[...] = jnp.zeros_like(sum_scr)

    def probs(start, size, part, counts):
        first = part * queries // 2
        spot = key_spot(start, size)
        cosine = dot_nt(query_ref[first:, :], key_ref[spot, :])
        prob = jnp.exp2(cosine * slope - slope)
        place = start + lax.broadcasted_iota(jnp.int32, (1, size), 1)
        seen = place < wide_as(limit_scr[first:, :], size)
        prob = jnp.where(seen, prob, 0.0).astype(jnp.bfloat16)
        prob_ref[first:, spot] = prob
        if counts:
            sum_scr[first:, :] += dot_nn(prob, wide_scr[spot, :])

    shared = (limit_of(queries // 2 - 1) + k_tile - 1) // k_tile
    shared_ref[0] = shared
    coarse_chunks(probs, some_keys)
    fine_chunks(probs, coarse, shared, fine // k_tile)

    num = sum_scr[:, :width]
    num_ref[...] = num
    weighted = jnp.sum(num * cot_ref[...].astype(jnp.float32), axis=-1, keepdims=True)
    row = lax.broadcasted_iota(jnp.int32, (width, width), 0)
    lane = lax.broadcasted_iota(jnp.int32, (width, width), 1)
    parts = queries // width
    for part in range(parts):
        spot = slice(part * width, (part + 1) * width)
        for index, value in ((part, sum_scr[spot, width:]), (parts + part, weighted[spot])):
            stat_ref[index : index + 1, :] = jnp.sum(
                jnp.where(row == lane, value, 0.0), axis=0, keepdims=True
            )


def key_grads(refs, targets, start, size, first, counts):
    prob_ref, key_ref, val_ref, cot_ref, mean_ref, query_turn, cot_turn, grad_ref = refs
    dk_target, dv_target = targets
    spot = key_spot(start, size)
    prob = prob_ref[first:, spot]
    dprob = dot_nt(cot_ref[first:, :], val_ref[spot, :])
    dscore = prob.astype(jnp.float32) * (dprob - wide_as(mean_ref[first:, :], size))
    dscore = dscore.astype(jnp.bfloat16)
    if counts:
        grad_ref[first:, :] += dot_nn(dscore, key_ref[spot, :])
    dk = dot_nn(query_turn[:, first:], dscore)
    dv = dot_nn(cot_turn[:, first:], prob)
    dk_target[...] = jnp.transpose(dk).astype(jnp.bfloat16)
    dv_target[...] = jnp.transpose(dv).astype(jnp.bfloat16)


def coarse_back_kernel(
    log_ref,
    stat_ref,
    other_stat_ref,
    prob_ref,
    key_ref,
    val_ref,
    query_ref,
    cot_ref,
    small_ref,
    den_ref,
    mean_ref,
    grad_ref,
    query_turn,
    cot_turn,
):
    _, head = seq_place()
    queries, width = query_ref.shape
    coarse = small_ref.shape[0]
    sharp = jnp.exp(jnp.full((1, width), log_ref[head], jnp.float32))[:, 0:1]
    row = lax.broadcasted_iota(jnp.int32, (width, width), 0)
    lane = lax.broadcasted_iota(jnp.int32, (width, width), 1)
    parts = queries // width

    def column(index):
        values = stat_ref[index : index + 1, :] + other_stat_ref[index : index + 1, :]
        return jnp.sum(jnp.where(row == lane, values, 0.0), axis=1, keepdims=True)

    for part in range(parts):
        spot = slice(part * width, (part + 1) * width)
        r_den = 1.0 / column(part)
        den_ref[spot, :] = jnp.broadcast_to(r_den, (width, width))
        mean_ref[spot, :] = jnp.broadcast_to(column(parts + part) * r_den, (width, width))

    grad_ref[...] = jnp.zeros_like(grad_ref)
    query_turn[...] = jnp.transpose(
        query_ref[...].astype(jnp.float32) * (den_ref[...] * sharp)
    ).astype(jnp.bfloat16)
    cot_turn[...] = jnp.transpose(cot_ref[...].astype(jnp.float32) * den_ref[...]).astype(
        jnp.bfloat16
    )
    refs = (prob_ref, key_ref, val_ref, cot_ref, mean_ref, query_turn, cot_turn, grad_ref)

    def work(start, size, part, counts):
        spot = slice(start, start + size)
        targets = (small_ref.at[spot, 0:width], small_ref.at[spot, width:])
        key_grads(refs, targets, start, size, 0, counts)

    coarse_chunks(work, coarse // 2)


def fine_back_kernel(
    log_ref,
    shared_ref,
    own_ref,
    qc_ref,
    prob_ref,
    key_ref,
    val_ref,
    query_ref,
    cot_ref,
    num_ref,
    den_ref,
    mean_ref,
    grad_in_ref,
    query_turn,
    cot_turn,
    coarse_scale_ref,
    od_ref,
    od_send_ref,
    dkv_ref,
    dkv_send_ref,
    scale_ref,
    grad_scr,
    turn_scr,
):
    plane, head = seq_place()
    members, tall, width = own_ref.shape
    rows = (tall - note_rows) // 4
    block = 2 * rows
    runs = members // 2
    queries = query_ref.shape[0]
    first_query = 2 * rows + note_rows
    fine = turn_scr.shape[0]
    coarse = key_ref.shape[0] - fine
    sharp = jnp.exp(jnp.full((1, width), log_ref[head], jnp.float32))[:, 0:1]
    grad_scr[...] = grad_in_ref[...]
    refs = (prob_ref, key_ref, val_ref, cot_ref, mean_ref, query_turn, cot_turn, grad_scr)

    def work(start, size, part, counts):
        spot = key_spot(start - coarse, size)
        targets = (turn_scr.at[spot, 0:width], turn_scr.at[spot, width:])
        key_grads(refs, targets, start, size, part * queries // 2, counts)

    fine_chunks(work, coarse, shared_ref[0], fine // k_tile)

    own_slot = query_slot(plane)
    scale = coarse_scale_ref[pl.ds(pl.multiple_of(head * 8, 8), 8), :]
    scale = scale * jnp.where(plane == 0, 1.0, 0.0)
    for ref, slot, start, target in (
        (own_ref, own_slot, first_query, od_ref),
        (qc_ref, 1 - own_slot, note_rows, od_send_ref),
    ):
        for run in range(runs):
            spot = pl.ds(place_of(run, slot, block), block)
            pick = ref[2 * run : 2 * run + 2, start : start + rows]
            q_dir, q_inv = unit_rows(pick.reshape(block, width))
            r_den = den_ref[spot, :]
            grad = grad_scr[spot, :] * (r_den * sharp)
            along = jnp.sum(q_dir * grad, axis=-1, keepdims=True)
            scale = scale + fold_rows(query_ref[spot, :].astype(jnp.float32) * grad)
            to = slice(run * block, (run + 1) * block)
            target[to, 0:width] = (num_ref[spot, :] * r_den).astype(jnp.bfloat16)
            target[to, width:] = (q_inv * (grad - q_dir * along)).astype(jnp.bfloat16)

    own_slot = key_slot(plane)
    for slot, target in ((own_slot, dkv_ref), (1 - own_slot, dkv_send_ref)):
        for run in range(runs):
            spot = pl.ds(place_of(run, slot, block), block)
            target[run * block : (run + 1) * block, :] = turn_scr[spot, :]
    scale_ref[...] = jnp.broadcast_to(sum_all(scale), scale_ref.shape)


def run_fine(log_scale, own_rows, kv_rows, qc_rows, key_coarse, val_coarse, coarse_scale, swap):
    members, tall, width = own_rows.shape
    rows = (tall - note_rows) // 4
    coarse = key_coarse.shape[0]
    queries = 2 * members * rows
    total = coarse + queries
    vmem = pl.BlockSpec(memory_space=pltpu.VMEM)
    smem = pl.BlockSpec(memory_space=pltpu.SMEM)

    def low(*shape):
        return jax.ShapeDtypeStruct(shape, jnp.bfloat16)

    def wide(*shape):
        return jax.ShapeDtypeStruct(shape, jnp.float32)

    prob, keys, values, query, cot, num, stat, shared = pl.pallas_call(
        forward_kernel,
        out_shape=(
            low(queries, total),
            low(total, width),
            low(total, width),
            low(queries, width),
            low(queries, width),
            wide(queries, width),
            wide(2 * queries // width, width),
            jax.ShapeDtypeStruct((1,), jnp.int32),
        ),
        in_specs=[smem] + [vmem] * 5,
        out_specs=(vmem,) * 7 + (smem,),
        scratch_shapes=[
            pltpu.VMEM((total, 2 * width), jnp.bfloat16),
            pltpu.VMEM((queries, width), jnp.int32),
            pltpu.VMEM((queries, 2 * width), jnp.float32),
        ],
        compiler_params=params(16),
        cost_estimate=pl.CostEstimate(
            flops=4 * queries * total * width,
            bytes_accessed=4 * queries * total,
            transcendentals=queries * total,
        ),
        name="fine_forward",
    )(log_scale, own_rows, kv_rows, qc_rows, key_coarse, val_coarse)
    other_stat = swap(stat)
    small, den, mean, grad, query_turned, cot_turned = pl.pallas_call(
        coarse_back_kernel,
        out_shape=(
            low(coarse, 2 * width),
            wide(queries, width),
            wide(queries, width),
            wide(queries, width),
            low(width, queries),
            low(width, queries),
        ),
        in_specs=[smem] + [vmem] * 7,
        out_specs=(vmem,) * 6,
        compiler_params=params(12),
        cost_estimate=pl.CostEstimate(
            flops=8 * queries * coarse * width,
            bytes_accessed=4 * queries * coarse,
            transcendentals=0,
        ),
        name="coarse_key_grads",
    )(log_scale, stat, other_stat, prob, keys, values, query, cot)
    half = low(queries // 2, 2 * width)
    outs = pl.pallas_call(
        fine_back_kernel,
        out_shape=(half, half, half, half, wide(8, width)),
        in_specs=[smem, smem] + [vmem] * 14,
        out_specs=(vmem,) * 5,
        scratch_shapes=[
            pltpu.VMEM((queries, width), jnp.float32),
            pltpu.VMEM((queries, 2 * width), jnp.bfloat16),
        ],
        compiler_params=params(16),
        cost_estimate=pl.CostEstimate(
            flops=8 * queries * queries * width,
            bytes_accessed=4 * queries * queries,
            transcendentals=0,
        ),
        name="fine_backward",
    )(
        log_scale,
        shared,
        own_rows,
        qc_rows,
        prob,
        keys,
        values,
        query,
        cot,
        num,
        den,
        mean,
        grad,
        query_turned,
        cot_turned,
        coarse_scale,
    )
    return small, outs


def coarse_kernel(
    log_ref,
    row_level_ref,
    col_level_ref,
    q_ref,
    k_ref,
    v_ref,
    cot_ref,
    out_ref,
    dq_ref,
    dk_ref,
    dv_ref,
    scale_ref,
    key_low_ref,
    value_ref,
):
    _, own = seq_place()
    count, features = q_ref.shape
    heads = log_ref.shape[0]
    width = features // heads
    visible = col_level_ref[...] <= row_level_ref[...]
    for head in range(heads):
        lanes = slice(head * width, (head + 1) * width)
        sharp = jnp.exp(jnp.full((1, width), log_ref[head], jnp.float32))[:, 0:1]
        slope = sharp * log2_e
        q_dir, q_inv = unit_rows(q_ref[:, lanes])
        q_low = q_dir.astype(jnp.bfloat16)
        key_low = unit_rows(k_ref[:, lanes])[0].astype(jnp.bfloat16)
        values = v_ref[:, lanes]
        cot = cot_ref[:, lanes]
        prob = jnp.exp2(dot_nt(q_low, key_low) * slope - slope)
        prob = jnp.where(visible, prob, 0.0)
        r_den = 1.0 / jnp.sum(prob, axis=-1, keepdims=True)
        norm_prob = prob * r_den
        dprob = dot_nt(cot, values)
        mean = jnp.sum(norm_prob * dprob, axis=-1, keepdims=True)
        dscore = (norm_prob * (dprob - mean)).astype(jnp.bfloat16)
        norm_low = norm_prob.astype(jnp.bfloat16)
        out_ref[:, lanes] = dot_nn(norm_low, values).astype(jnp.bfloat16)
        grad = sharp * dot_nn(dscore, key_low)
        along = jnp.sum(q_dir * grad, axis=-1, keepdims=True)
        dq_ref[:, lanes] = (q_inv * (grad - q_dir * along)).astype(jnp.bfloat16)
        scale_ref[head * 8 : head * 8 + 8, :] = fold_rows(q_low.astype(jnp.float32) * grad)
        q_turned = jnp.transpose(q_dir).astype(jnp.bfloat16)
        cot_turned = jnp.transpose(cot.astype(jnp.float32)).astype(jnp.bfloat16)
        dk_ref[:, lanes] = sharp * jnp.transpose(dot_nn(q_turned, dscore))
        dv_ref[:, lanes] = jnp.transpose(dot_nn(cot_turned, norm_low))

        @pl.when(own == head)
        def _():
            key_low_ref[...] = key_low
            value_ref[...] = values


def run_coarse(log_scale, levels, queries, keys, values, cots):
    count, features = queries.shape
    heads = log_scale.shape[0]
    width = features // heads
    vmem = pl.BlockSpec(memory_space=pltpu.VMEM)
    wide = jax.ShapeDtypeStruct((count, features), jnp.float32)
    low = jax.ShapeDtypeStruct((count, features), jnp.bfloat16)
    return pl.pallas_call(
        coarse_kernel,
        out_shape=(low, low, wide, wide, jax.ShapeDtypeStruct((heads * 8, width), jnp.float32))
        + (jax.ShapeDtypeStruct((count, width), jnp.bfloat16),) * 2,
        in_specs=[pl.BlockSpec(memory_space=pltpu.SMEM)] + [vmem] * 6,
        compiler_params=params(14),
        cost_estimate=pl.CostEstimate(
            flops=12 * count * count * features,
            bytes_accessed=24 * count * features,
            transcendentals=heads * count * count,
        ),
        name="coarse_attention",
    )(log_scale, levels[:, None], levels[None, :], queries, keys, values, cots)


def small_kernel(own_ref, near_ref, _, sum_ref):
    some_keys = sum_ref.shape[0] // 2
    summed = own_ref[...].astype(jnp.float32) + near_ref[...].astype(jnp.float32)
    own_half = query_slot(seq_place()[0])
    for index, half in enumerate((own_half, 1 - own_half)):
        spot = pl.ds(pl.multiple_of(half * some_keys, some_keys), some_keys)
        sum_ref[spot, :] = summed[index * some_keys : (index + 1) * some_keys].astype(jnp.bfloat16)


def run_small(own, near, after):
    return pl.pallas_call(
        small_kernel,
        out_shape=jax.ShapeDtypeStruct(own.shape, jnp.bfloat16),
        compiler_params=params(2),
        name="sum_coarse_terms",
    )(own, near, after)


def sum_kernel(
    od_ref, other_od_ref, dkv_ref, other_dkv_ref, own_ref, *scale_refs
):
    *scale_refs, all_ref, table_ref = scale_refs
    members, tall, width = all_ref.shape
    rows = tall // 4
    fine = members * rows
    _, head = seq_place()
    for flip, ref in enumerate(scale_refs):
        table_ref[pl.ds(lax.bitwise_xor(head, flip), 1), :] = ref[0:1, :]

    def put(place, value):
        all_ref[:, place * rows : (place + 1) * rows] = value.astype(jnp.bfloat16).reshape(
            members, rows, width
        )

    summed = od_ref[...].astype(jnp.float32) + other_od_ref[...].astype(jnp.float32)
    put(0, summed[:, :width])
    put(1, summed[:, width:])
    summed = dkv_ref[...].astype(jnp.float32) + other_dkv_ref[...].astype(jnp.float32)
    put(2, project(own_ref[:, 0:rows].reshape(fine, width), summed[:, :width]))
    put(3, summed[:, width:])


def run_sum(od, other_od, dkv, other_dkv, own_rows, scales):
    members, tall, width = own_rows.shape
    return pl.pallas_call(
        sum_kernel,
        out_shape=(
            jax.ShapeDtypeStruct((members, tall - note_rows, width), jnp.bfloat16),
            jax.ShapeDtypeStruct((members, width), jnp.float32),
        ),
        compiler_params=params(6),
        name="sum_pairs",
    )(od, other_od, dkv, other_dkv, own_rows, *scales)


def join_kernel(terms_ref, dk_own_ref, dv_own_ref, k_ref, dk_ref, dv_ref, last_ref):
    heads, _, both = terms_ref.shape
    width = both // 2
    for head in range(heads):
        lanes = slice(head * width, (head + 1) * width)
        terms = terms_ref[head].astype(jnp.float32)
        grad = terms[:, :width] + dk_own_ref[:, lanes]
        dk_ref[:, lanes] = project(k_ref[:, lanes], grad).astype(jnp.bfloat16)
        dv_ref[:, lanes] = (terms[:, width:] + dv_own_ref[:, lanes]).astype(jnp.bfloat16)
    last_ref[...] = jnp.zeros_like(last_ref)


def run_join(terms, dk_own, dv_own, keys):
    low = jax.ShapeDtypeStruct(keys.shape, jnp.bfloat16)
    return pl.pallas_call(
        join_kernel,
        out_shape=(low, low, jax.ShapeDtypeStruct((8, 128), jnp.float32)),
        compiler_params=params(8),
        name="join_coarse",
    )(terms, dk_own, dv_own, keys)


def unpack_kernel(factor, all_ref, _, *refs):
    *table_refs, out_ref, dq_ref, dk_ref, dv_ref, scale_ref = refs
    heads, tall, width = all_ref.shape
    rows = tall // 4
    table = table_refs[0][...]
    for ref in table_refs[1:]:
        table = table + ref[...]
    for head in range(heads):
        lanes = slice(head * width, (head + 1) * width)
        for place, ref in enumerate((out_ref, dq_ref, dk_ref, dv_ref)):
            ref[:, lanes] = all_ref[head, place * rows : (place + 1) * rows]
        scale_ref[head] = jnp.sum(table[head : head + 1, 0:1]) * factor


def run_unpack(factor, all_back, after, tables):
    heads, tall, width = all_back.shape
    flat = jax.ShapeDtypeStruct((tall // 4, heads * width), jnp.bfloat16)
    vmem = pl.BlockSpec(memory_space=pltpu.VMEM)
    return pl.pallas_call(
        partial(unpack_kernel, factor),
        out_shape=(flat,) * 4 + (jax.ShapeDtypeStruct((heads,), jnp.float32),),
        in_specs=[vmem] * (2 + len(tables)),
        out_specs=(vmem,) * 4 + (pl.BlockSpec(memory_space=pltpu.SMEM),),
        compiler_params=params(3),
        name="unpack_heads",
    )(all_back, after, *tables)


def body(
    q_coarse,
    k_coarse,
    v_coarse,
    cot_coarse,
    coarse_ids,
    q_fine,
    k_fine,
    v_fine,
    cot_fine,
    fine_ids,
    log_scale,
):
    heads = log_scale.shape[0]
    coarse = q_coarse.shape[1]
    rows = q_fine.shape[1]
    seq = lax.axis_size("seq")
    images = lax.axis_size("dp")
    groups = [
        [8 * (h // 2) + 2 * plane + h % 2 for h in range(heads)] for plane in range(planes)
    ]

    def exchange(parts):
        return lax.all_to_all(parts, "seq", 0, 0, axis_index_groups=groups, tiled=True)

    def to_plane(array, flip):
        return lax.ppermute(array, "seq", [(i, i ^ (2 * flip)) for i in range(seq)])

    def to_head(array, flip):
        other = 8 * (flip // 2) + flip % 2
        return lax.ppermute(array, "seq", [(i, i ^ other) for i in range(seq)])

    def to_image(array, flip):
        return lax.ppermute(array, "dp", [(i, i ^ flip) for i in range(images)])

    def to_both(array, image_flip, plane_flip):
        there = [
            (i ^ image_flip) * seq + (j ^ (2 * plane_flip))
            for i in range(images)
            for j in range(seq)
        ]
        return lax.ppermute(array, ("dp", "seq"), list(enumerate(there)))

    own_rows = exchange(run_pack(heads, fine_ids, k_fine[0], v_fine[0], q_fine[0], cot_fine[0]))
    kv_rows = to_plane(own_rows[:, : 2 * rows + note_rows], 1)
    qc_rows = to_plane(own_rows[:, 2 * rows :], 3)

    out_c, dq_c, dk_own, dv_own, scale_c, key_c, val_c = run_coarse(
        log_scale, coarse_ids[0], q_coarse[0], k_coarse[0], v_coarse[0], cot_coarse[0]
    )
    small, (od, od_send, dkv, dkv_send, scale) = run_fine(
        log_scale, own_rows, kv_rows, qc_rows, key_c, val_c, scale_c, lambda stat: to_plane(stat, 3)
    )

    small_sum = run_small(small, to_plane(small, 1), scale)
    of_image = lax.all_gather(small_sum, "seq", axis=0, axis_index_groups=groups)

    other_dkv = to_plane(dkv_send, 1)
    other_od = to_plane(od_send, 3)
    scale = scale + to_image(scale, 1) + to_image(scale, 2) + to_image(scale, 3)
    scales = [scale] + [to_head(scale, flip) for flip in range(1, heads)]
    all_parts, table = run_sum(od, other_od, dkv, other_dkv, own_rows, scales)
    tables = [table, to_image(table, 4)]
    for flip in (1, 2, 3):
        tables += [to_plane(table, flip), to_both(table, 4, flip)]
    all_back = exchange(all_parts)
    dk_c, dv_c, after = run_join(of_image, dk_own, dv_own, k_coarse[0])
    factor = 1.0 / math.sqrt(images * (coarse + seq * rows))
    fine_out, fine_dq, fine_dk, fine_dv, grad_scale = run_unpack(factor, all_back, after, tables)
    return (
        out_c[None],
        dq_c[None],
        dk_c[None],
        dv_c[None],
        fine_out[None],
        fine_dq[None],
        fine_dk[None],
        fine_dv[None],
        grad_scale,
    )


def solution(mesh):
    whole = P("dp", None, None)
    split = P("dp", "seq", None)
    return jax.shard_map(
        body,
        mesh=mesh,
        in_specs=(whole,) * 4 + (P("dp", None),) + (split,) * 4 + (P("dp", "seq"), P()),
        out_specs=(whole,) * 4 + (split,) * 4 + (P(),),
        check_vma=False,
    )
```

```python
import math
from functools import partial

import jax
import jax.numpy as jnp
from jax import lax
from jax.experimental import pallas as pl
from jax.experimental.pallas import tpu as pltpu
from jax.sharding import PartitionSpec as P

norm_eps = 1e-06
log2_e = 1.4426950408889634
k_tile = 256
note_rows = 16

planes = 4


def dot_nt(left, right):
    return lax.dot_general(
        left, right, (((1,), (1,)), ((), ())), preferred_element_type=jnp.float32
    )


def dot_nn(left, right):
    return jnp.dot(left, right, preferred_element_type=jnp.float32)


def unit_rows(rows):
    wide = rows.astype(jnp.float32)
    inv_norm = lax.rsqrt(jnp.sum(wide * wide, axis=-1, keepdims=True) + norm_eps)
    return wide * inv_norm, inv_norm


def project(key_rows, grad):
    key_dir, key_inv = unit_rows(key_rows)
    along = jnp.sum(key_dir * grad, axis=-1, keepdims=True)
    return key_inv * (grad - key_dir * along)


def fold_rows(terms):
    rows, width = terms.shape
    return jnp.sum(terms.reshape(rows // 8, 8, width), axis=0)


def in_pieces(value, width):
    row = lax.broadcasted_iota(jnp.int32, (note_rows, width), 0)
    note = jnp.zeros((note_rows, width), jnp.float32)
    for part in range(3):
        piece = value.astype(jnp.bfloat16).astype(jnp.float32)
        note = jnp.where(row == part, piece, note)
        value = value - piece
    return note.astype(jnp.bfloat16)


def sum_all(terms):
    return jnp.sum(jnp.sum(terms, axis=0, keepdims=True), axis=-1, keepdims=True)


def seq_place():
    here = lax.axis_index("seq")
    plane = lax.bitwise_and(lax.shift_right_logical(here, 1), 3)
    head = 2 * lax.shift_right_logical(here, 3) + lax.bitwise_and(here, 1)
    return plane, head


def key_slot(plane):
    return lax.bitwise_and(plane, 1)


def query_slot(plane):
    return lax.shift_right_logical(plane, 1)


def params(mebibytes):
    return pltpu.CompilerParams(vmem_limit_bytes=mebibytes * 1024 * 1024)


def pack_kernel(ids_ref, k_ref, v_ref, q_ref, cot_ref, all_ref):
    heads, _, width = all_ref.shape
    rows = k_ref.shape[0]
    ids = ids_ref[...]
    row = lax.broadcasted_iota(jnp.int32, (note_rows, width), 0)
    lane = lax.broadcasted_iota(jnp.int32, (note_rows, width), 1)
    note = jnp.zeros((note_rows, width), jnp.float32)
    for level in range(2):
        count = jnp.sum(jnp.where(ids <= level, 1.0, 0.0), axis=-1, keepdims=True)
        note = jnp.where((row == level) & (lane == 0), count, note)
    note = note.astype(jnp.bfloat16)
    first_query = 2 * rows + note_rows
    for head in range(heads):
        lanes = slice(head * width, (head + 1) * width)
        all_ref[head, 0:rows] = k_ref[:, lanes]
        all_ref[head, rows : 2 * rows] = v_ref[:, lanes]
        all_ref[head, 2 * rows : first_query] = note
        all_ref[head, first_query : first_query + rows] = q_ref[:, lanes]
        all_ref[head, first_query + rows :] = cot_ref[:, lanes]


def run_pack(heads, ids, keys, values, queries, cots):
    rows, features = keys.shape
    shape = (heads, 4 * rows + note_rows, features // heads)
    return pl.pallas_call(
        pack_kernel,
        out_shape=jax.ShapeDtypeStruct(shape, jnp.bfloat16),
        compiler_params=params(56),
        name="pack_heads",
    )(ids, keys, values, queries, cots)


def twice(column):
    return jnp.concatenate([column, column], axis=1)


def wide_as(column, size):
    return column if size == column.shape[1] else twice(column)


def place_of(run, slot, block):
    return pl.multiple_of((2 * run + slot) * block, 64)


def key_spot(first, size):
    return pl.ds(first if isinstance(first, int) else pl.multiple_of(first, 128), size)


def coarse_chunks(work, some_keys):
    work(0, some_keys, 0, True)
    work(some_keys, some_keys, 0, False)


def fine_chunks(work, coarse, shared, chunks):
    def both(chunk, carry):
        work(coarse + chunk * k_tile, k_tile, 0, True)
        return carry

    def upper(chunk, carry):
        work(coarse + chunk * k_tile, k_tile, 1, True)
        return carry

    lax.fori_loop(0, shared, both, 0)
    lax.fori_loop(shared, chunks, upper, 0)


def forward_kernel(
    log_ref,
    own_ref,
    kv_ref,
    qc_ref,
    kc_ref,
    vc_ref,
    prob_ref,
    key_ref,
    val_ref,
    query_ref,
    cot_ref,
    num_ref,
    stat_ref,
    shared_ref,
    wide_scr,
    limit_scr,
    sum_scr,
):
    plane, head = seq_place()
    members, tall, width = own_ref.shape
    rows = (tall - note_rows) // 4
    block = 2 * rows
    runs = members // 2
    queries = query_ref.shape[0]
    coarse = kc_ref.shape[0]
    some_keys = coarse // 2
    fine = key_ref.shape[0] - coarse
    first_query = 2 * rows + note_rows

    def count(notes):
        total = jnp.sum(notes.astype(jnp.float32), axis=0)
        return [jnp.sum(total[level : level + 1]).astype(jnp.int32) for level in range(2)]

    own_counts = count(own_ref[:, 2 * rows : first_query])
    key_counts = [a + b for a, b in zip(own_counts, count(kv_ref[:, 2 * rows :]))]
    query_counts = [a + b for a, b in zip(own_counts, count(qc_ref[:, :note_rows]))]

    def limit_of(place):
        return jnp.where(
            place < query_counts[0],
            key_counts[0],
            jnp.where(place < query_counts[1], key_counts[1], fine),
        )

    own_slot = key_slot(plane)
    for ref, slot in ((own_ref, own_slot), (kv_ref, 1 - own_slot)):
        for run in range(runs):
            pick = slice(2 * run, 2 * run + 2)
            spot = pl.ds(pl.multiple_of(coarse + place_of(run, slot, block), 64), block)
            key_ref[spot, :] = unit_rows(ref[pick, 0:rows].reshape(block, width))[0].astype(
                jnp.bfloat16
            )
            values = ref[pick, rows : 2 * rows].reshape(block, width)
            val_ref[spot, :] = values
            wide_scr[spot, 0:width] = values
    own_half = query_slot(plane)
    for index, half in enumerate((own_half, 1 - own_half)):
        spot = slice(index * some_keys, (index + 1) * some_keys)
        half = pl.ds(pl.multiple_of(half * some_keys, some_keys), some_keys)
        key_ref[spot, :] = kc_ref[half, :]
        val_ref[spot, :] = vc_ref[half, :]
        wide_scr[spot, 0:width] = vc_ref[half, :]
    wide_scr[:, width:] = jnp.ones((coarse + fine, width), jnp.bfloat16)

    own_slot = query_slot(plane)
    for ref, slot, start in ((own_ref, own_slot, first_query), (qc_ref, 1 - own_slot, note_rows)):
        for run in range(runs):
            pick = slice(2 * run, 2 * run + 2)
            spot = pl.ds(place_of(run, slot, block), block)
            query_ref[spot, :] = unit_rows(
                ref[pick, start : start + rows].reshape(block, width)
            )[0].astype(jnp.bfloat16)
            cot_ref[spot, :] = ref[pick, start + rows : start + 2 * rows].reshape(block, width)
    limit_scr[...] = coarse + limit_of(
        lax.broadcasted_iota(jnp.int32, (queries, width), 0)
    )

    sharp = jnp.exp(jnp.full((1, width), log_ref[head], jnp.float32))[:, 0:1]
    slope = sharp * log2_e
    sum_scr[...] = jnp.zeros_like(sum_scr)

    def probs(start, size, part, counts):
        first = part * queries // 2
        spot = key_spot(start, size)
        cosine = dot_nt(query_ref[first:, :], key_ref[spot, :])
        prob = jnp.exp2(cosine * slope - slope)
        place = start + lax.broadcasted_iota(jnp.int32, (1, size), 1)
        seen = place < wide_as(limit_scr[first:, :], size)
        prob = jnp.where(seen, prob, 0.0).astype(jnp.bfloat16)
        prob_ref[first:, spot] = prob
        if counts:
            sum_scr[first:, :] += dot_nn(prob, wide_scr[spot, :])

    shared = (limit_of(queries // 2 - 1) + k_tile - 1) // k_tile
    shared_ref[0] = shared
    coarse_chunks(probs, some_keys)
    fine_chunks(probs, coarse, shared, fine // k_tile)

    num = sum_scr[:, :width]
    num_ref[...] = num
    weighted = jnp.sum(num * cot_ref[...].astype(jnp.float32), axis=-1, keepdims=True)
    row = lax.broadcasted_iota(jnp.int32, (width, width), 0)
    lane = lax.broadcasted_iota(jnp.int32, (width, width), 1)
    parts = queries // width
    for part in range(parts):
        spot = slice(part * width, (part + 1) * width)
        for index, value in ((part, sum_scr[spot, width:]), (parts + part, weighted[spot])):
            stat_ref[index : index + 1, :] = jnp.sum(
                jnp.where(row == lane, value, 0.0), axis=0, keepdims=True
            )


def key_grads(refs, targets, start, size, first, counts):
    prob_ref, key_ref, val_ref, cot_ref, mean_ref, query_turn, cot_turn, grad_ref = refs
    dk_target, dv_target = targets
    spot = key_spot(start, size)
    prob = prob_ref[first:, spot]
    dprob = dot_nt(cot_ref[first:, :], val_ref[spot, :])
    dscore = prob.astype(jnp.float32) * (dprob - wide_as(mean_ref[first:, :], size))
    dscore = dscore.astype(jnp.bfloat16)
    if counts:
        grad_ref[first:, :] += dot_nn(dscore, key_ref[spot, :])
    dk = dot_nn(query_turn[:, first:], dscore)
    dv = dot_nn(cot_turn[:, first:], prob)
    dk_target[...] = jnp.transpose(dk).astype(jnp.bfloat16)
    dv_target[...] = jnp.transpose(dv).astype(jnp.bfloat16)


def coarse_back_kernel(
    log_ref,
    stat_ref,
    other_stat_ref,
    prob_ref,
    key_ref,
    val_ref,
    query_ref,
    cot_ref,
    small_ref,
    den_ref,
    mean_ref,
    grad_ref,
    query_turn,
    cot_turn,
):
    _, head = seq_place()
    queries, width = query_ref.shape
    coarse = small_ref.shape[0]
    sharp = jnp.exp(jnp.full((1, width), log_ref[head], jnp.float32))[:, 0:1]
    row = lax.broadcasted_iota(jnp.int32, (width, width), 0)
    lane = lax.broadcasted_iota(jnp.int32, (width, width), 1)
    parts = queries // width

    def column(index):
        values = stat_ref[index : index + 1, :] + other_stat_ref[index : index + 1, :]
        return jnp.sum(jnp.where(row == lane, values, 0.0), axis=1, keepdims=True)

    for part in range(parts):
        spot = slice(part * width, (part + 1) * width)
        r_den = 1.0 / column(part)
        den_ref[spot, :] = jnp.broadcast_to(r_den, (width, width))
        mean_ref[spot, :] = jnp.broadcast_to(column(parts + part) * r_den, (width, width))

    grad_ref[...] = jnp.zeros_like(grad_ref)
    query_turn[...] = jnp.transpose(
        query_ref[...].astype(jnp.float32) * (den_ref[...] * sharp)
    ).astype(jnp.bfloat16)
    cot_turn[...] = jnp.transpose(cot_ref[...].astype(jnp.float32) * den_ref[...]).astype(
        jnp.bfloat16
    )
    refs = (prob_ref, key_ref, val_ref, cot_ref, mean_ref, query_turn, cot_turn, grad_ref)

    def work(start, size, part, counts):
        spot = slice(start, start + size)
        targets = (small_ref.at[spot, 0:width], small_ref.at[spot, width:])
        key_grads(refs, targets, start, size, 0, counts)

    coarse_chunks(work, coarse // 2)


def fine_back_kernel(
    log_ref,
    shared_ref,
    own_ref,
    qc_ref,
    prob_ref,
    key_ref,
    val_ref,
    query_ref,
    cot_ref,
    num_ref,
    den_ref,
    mean_ref,
    grad_in_ref,
    query_turn,
    cot_turn,
    coarse_scale_ref,
    od_ref,
    od_send_ref,
    dkv_ref,
    dkv_send_ref,
    scale_ref,
    grad_scr,
    turn_scr,
):
    plane, head = seq_place()
    members, tall, width = own_ref.shape
    rows = (tall - note_rows) // 4
    block = 2 * rows
    runs = members // 2
    queries = query_ref.shape[0]
    first_query = 2 * rows + note_rows
    fine = turn_scr.shape[0]
    coarse = key_ref.shape[0] - fine
    sharp = jnp.exp(jnp.full((1, width), log_ref[head], jnp.float32))[:, 0:1]
    grad_scr[...] = grad_in_ref[...]
    refs = (prob_ref, key_ref, val_ref, cot_ref, mean_ref, query_turn, cot_turn, grad_scr)

    def work(start, size, part, counts):
        spot = key_spot(start - coarse, size)
        targets = (turn_scr.at[spot, 0:width], turn_scr.at[spot, width:])
        key_grads(refs, targets, start, size, part * queries // 2, counts)

    fine_chunks(work, coarse, shared_ref[0], fine // k_tile)

    own_slot = query_slot(plane)
    scale = coarse_scale_ref[pl.ds(pl.multiple_of(head * 8, 8), 8), :]
    scale = scale * jnp.where(plane == 0, 1.0, 0.0)
    for ref, slot, start, target in (
        (own_ref, own_slot, first_query, od_ref),
        (qc_ref, 1 - own_slot, note_rows, od_send_ref),
    ):
        for run in range(runs):
            spot = pl.ds(place_of(run, slot, block), block)
            pick = ref[2 * run : 2 * run + 2, start : start + rows]
            q_dir, q_inv = unit_rows(pick.reshape(block, width))
            r_den = den_ref[spot, :]
            grad = grad_scr[spot, :] * (r_den * sharp)
            along = jnp.sum(q_dir * grad, axis=-1, keepdims=True)
            scale = scale + fold_rows(query_ref[spot, :].astype(jnp.float32) * grad)
            to = slice(run * block, (run + 1) * block)
            target[to, 0:width] = (num_ref[spot, :] * r_den).astype(jnp.bfloat16)
            target[to, width:] = (q_inv * (grad - q_dir * along)).astype(jnp.bfloat16)

    own_slot = key_slot(plane)
    for slot, target in ((own_slot, dkv_ref), (1 - own_slot, dkv_send_ref)):
        for run in range(runs):
            spot = pl.ds(place_of(run, slot, block), block)
            target[run * block : (run + 1) * block, :] = turn_scr[spot, :]
    scale_ref[...] = jnp.broadcast_to(sum_all(scale), scale_ref.shape)


def run_fine(log_scale, own_rows, kv_rows, qc_rows, key_coarse, val_coarse, coarse_scale, swap):
    members, tall, width = own_rows.shape
    rows = (tall - note_rows) // 4
    coarse = key_coarse.shape[0]
    queries = 2 * members * rows
    total = coarse + queries
    vmem = pl.BlockSpec(memory_space=pltpu.VMEM)
    smem = pl.BlockSpec(memory_space=pltpu.SMEM)

    def low(*shape):
        return jax.ShapeDtypeStruct(shape, jnp.bfloat16)

    def wide(*shape):
        return jax.ShapeDtypeStruct(shape, jnp.float32)

    prob, keys, values, query, cot, num, stat, shared = pl.pallas_call(
        forward_kernel,
        out_shape=(
            low(queries, total),
            low(total, width),
            low(total, width),
            low(queries, width),
            low(queries, width),
            wide(queries, width),
            wide(2 * queries // width, width),
            jax.ShapeDtypeStruct((1,), jnp.int32),
        ),
        in_specs=[smem] + [vmem] * 5,
        out_specs=(vmem,) * 7 + (smem,),
        scratch_shapes=[
            pltpu.VMEM((total, 2 * width), jnp.bfloat16),
            pltpu.VMEM((queries, width), jnp.int32),
            pltpu.VMEM((queries, 2 * width), jnp.float32),
        ],
        compiler_params=params(16),
        cost_estimate=pl.CostEstimate(
            flops=4 * queries * total * width,
            bytes_accessed=4 * queries * total,
            transcendentals=queries * total,
        ),
        name="fine_forward",
    )(log_scale, own_rows, kv_rows, qc_rows, key_coarse, val_coarse)
    other_stat = swap(stat)
    small, den, mean, grad, query_turned, cot_turned = pl.pallas_call(
        coarse_back_kernel,
        out_shape=(
            low(coarse, 2 * width),
            wide(queries, width),
            wide(queries, width),
            wide(queries, width),
            low(width, queries),
            low(width, queries),
        ),
        in_specs=[smem] + [vmem] * 7,
        out_specs=(vmem,) * 6,
        compiler_params=params(12),
        cost_estimate=pl.CostEstimate(
            flops=8 * queries * coarse * width,
            bytes_accessed=4 * queries * coarse,
            transcendentals=0,
        ),
        name="coarse_key_grads",
    )(log_scale, stat, other_stat, prob, keys, values, query, cot)
    half = low(queries // 2, 2 * width)
    outs = pl.pallas_call(
        fine_back_kernel,
        out_shape=(half, half, half, half, wide(8, width)),
        in_specs=[smem, smem] + [vmem] * 14,
        out_specs=(vmem,) * 5,
        scratch_shapes=[
            pltpu.VMEM((queries, width), jnp.float32),
            pltpu.VMEM((queries, 2 * width), jnp.bfloat16),
        ],
        compiler_params=params(16),
        cost_estimate=pl.CostEstimate(
            flops=8 * queries * queries * width,
            bytes_accessed=4 * queries * queries,
            transcendentals=0,
        ),
        name="fine_backward",
    )(
        log_scale,
        shared,
        own_rows,
        qc_rows,
        prob,
        keys,
        values,
        query,
        cot,
        num,
        den,
        mean,
        grad,
        query_turned,
        cot_turned,
        coarse_scale,
    )
    return small, outs


def coarse_kernel(
    log_ref,
    row_level_ref,
    col_level_ref,
    q_ref,
    k_ref,
    v_ref,
    cot_ref,
    out_ref,
    dq_ref,
    dk_ref,
    dv_ref,
    scale_ref,
    key_low_ref,
    value_ref,
):
    _, own = seq_place()
    count, features = q_ref.shape
    heads = log_ref.shape[0]
    width = features // heads
    visible = col_level_ref[...] <= row_level_ref[...]
    for head in range(heads):
        lanes = slice(head * width, (head + 1) * width)
        sharp = jnp.exp(jnp.full((1, width), log_ref[head], jnp.float32))[:, 0:1]
        slope = sharp * log2_e
        q_dir, q_inv = unit_rows(q_ref[:, lanes])
        q_low = q_dir.astype(jnp.bfloat16)
        key_low = unit_rows(k_ref[:, lanes])[0].astype(jnp.bfloat16)
        values = v_ref[:, lanes]
        cot = cot_ref[:, lanes]
        prob = jnp.exp2(dot_nt(q_low, key_low) * slope - slope)
        prob = jnp.where(visible, prob, 0.0)
        r_den = 1.0 / jnp.sum(prob, axis=-1, keepdims=True)
        norm_prob = prob * r_den
        dprob = dot_nt(cot, values)
        mean = jnp.sum(norm_prob * dprob, axis=-1, keepdims=True)
        dscore = (norm_prob * (dprob - mean)).astype(jnp.bfloat16)
        norm_low = norm_prob.astype(jnp.bfloat16)
        out_ref[:, lanes] = dot_nn(norm_low, values).astype(jnp.bfloat16)
        grad = sharp * dot_nn(dscore, key_low)
        along = jnp.sum(q_dir * grad, axis=-1, keepdims=True)
        dq_ref[:, lanes] = (q_inv * (grad - q_dir * along)).astype(jnp.bfloat16)
        scale_ref[head * 8 : head * 8 + 8, :] = fold_rows(q_low.astype(jnp.float32) * grad)
        q_turned = jnp.transpose(q_dir).astype(jnp.bfloat16)
        cot_turned = jnp.transpose(cot.astype(jnp.float32)).astype(jnp.bfloat16)
        dk_ref[:, lanes] = sharp * jnp.transpose(dot_nn(q_turned, dscore))
        dv_ref[:, lanes] = jnp.transpose(dot_nn(cot_turned, norm_low))

        @pl.when(own == head)
        def _():
            key_low_ref[...] = key_low
            value_ref[...] = values


def run_coarse(log_scale, levels, queries, keys, values, cots):
    count, features = queries.shape
    heads = log_scale.shape[0]
    width = features // heads
    vmem = pl.BlockSpec(memory_space=pltpu.VMEM)
    wide = jax.ShapeDtypeStruct((count, features), jnp.float32)
    low = jax.ShapeDtypeStruct((count, features), jnp.bfloat16)
    return pl.pallas_call(
        coarse_kernel,
        out_shape=(low, low, wide, wide, jax.ShapeDtypeStruct((heads * 8, width), jnp.float32))
        + (jax.ShapeDtypeStruct((count, width), jnp.bfloat16),) * 2,
        in_specs=[pl.BlockSpec(memory_space=pltpu.SMEM)] + [vmem] * 6,
        compiler_params=params(14),
        cost_estimate=pl.CostEstimate(
            flops=12 * count * count * features,
            bytes_accessed=24 * count * features,
            transcendentals=heads * count * count,
        ),
        name="coarse_attention",
    )(log_scale, levels[:, None], levels[None, :], queries, keys, values, cots)


def small_kernel(own_ref, near_ref, _, sum_ref):
    some_keys = sum_ref.shape[0] // 2
    summed = own_ref[...].astype(jnp.float32) + near_ref[...].astype(jnp.float32)
    own_half = query_slot(seq_place()[0])
    for index, half in enumerate((own_half, 1 - own_half)):
        spot = pl.ds(pl.multiple_of(half * some_keys, some_keys), some_keys)
        sum_ref[spot, :] = summed[index * some_keys : (index + 1) * some_keys].astype(jnp.bfloat16)


def run_small(own, near, after):
    return pl.pallas_call(
        small_kernel,
        out_shape=jax.ShapeDtypeStruct(own.shape, jnp.bfloat16),
        compiler_params=params(2),
        name="sum_coarse_terms",
    )(own, near, after)


def sum_kernel(
    od_ref, other_od_ref, dkv_ref, other_dkv_ref, own_ref, *scale_refs
):
    *scale_refs, all_ref, table_ref = scale_refs
    members, tall, width = all_ref.shape
    rows = tall // 4
    fine = members * rows
    _, head = seq_place()
    for flip, ref in enumerate(scale_refs):
        table_ref[pl.ds(lax.bitwise_xor(head, flip), 1), :] = ref[0:1, :]

    def put(place, value):
        all_ref[:, place * rows : (place + 1) * rows] = value.astype(jnp.bfloat16).reshape(
            members, rows, width
        )

    summed = od_ref[...].astype(jnp.float32) + other_od_ref[...].astype(jnp.float32)
    put(0, summed[:, :width])
    put(1, summed[:, width:])
    summed = dkv_ref[...].astype(jnp.float32) + other_dkv_ref[...].astype(jnp.float32)
    put(2, project(own_ref[:, 0:rows].reshape(fine, width), summed[:, :width]))
    put(3, summed[:, width:])


def run_sum(od, other_od, dkv, other_dkv, own_rows, scales):
    members, tall, width = own_rows.shape
    return pl.pallas_call(
        sum_kernel,
        out_shape=(
            jax.ShapeDtypeStruct((members, tall - note_rows, width), jnp.bfloat16),
            jax.ShapeDtypeStruct((members, width), jnp.float32),
        ),
        compiler_params=params(6),
        name="sum_pairs",
    )(od, other_od, dkv, other_dkv, own_rows, *scales)


def join_kernel(terms_ref, dk_own_ref, dv_own_ref, k_ref, dk_ref, dv_ref, last_ref):
    heads, _, both = terms_ref.shape
    width = both // 2
    for head in range(heads):
        lanes = slice(head * width, (head + 1) * width)
        terms = terms_ref[head].astype(jnp.float32)
        grad = terms[:, :width] + dk_own_ref[:, lanes]
        dk_ref[:, lanes] = project(k_ref[:, lanes], grad).astype(jnp.bfloat16)
        dv_ref[:, lanes] = (terms[:, width:] + dv_own_ref[:, lanes]).astype(jnp.bfloat16)
    last_ref[...] = jnp.zeros_like(last_ref)


def run_join(terms, dk_own, dv_own, keys):
    low = jax.ShapeDtypeStruct(keys.shape, jnp.bfloat16)
    return pl.pallas_call(
        join_kernel,
        out_shape=(low, low, jax.ShapeDtypeStruct((8, 128), jnp.float32)),
        compiler_params=params(8),
        name="join_coarse",
    )(terms, dk_own, dv_own, keys)


def unpack_kernel(factor, all_ref, _, *refs):
    *table_refs, out_ref, dq_ref, dk_ref, dv_ref, scale_ref = refs
    heads, tall, width = all_ref.shape
    rows = tall // 4
    table = table_refs[0][...]
    for ref in table_refs[1:]:
        table = table + ref[...]
    for head in range(heads):
        lanes = slice(head * width, (head + 1) * width)
        for place, ref in enumerate((out_ref, dq_ref, dk_ref, dv_ref)):
            ref[:, lanes] = all_ref[head, place * rows : (place + 1) * rows]
        scale_ref[head] = jnp.sum(table[head : head + 1, 0:1]) * factor


def run_unpack(factor, all_back, after, tables):
    heads, tall, width = all_back.shape
    flat = jax.ShapeDtypeStruct((tall // 4, heads * width), jnp.bfloat16)
    vmem = pl.BlockSpec(memory_space=pltpu.VMEM)
    return pl.pallas_call(
        partial(unpack_kernel, factor),
        out_shape=(flat,) * 4 + (jax.ShapeDtypeStruct((heads,), jnp.float32),),
        in_specs=[vmem] * (2 + len(tables)),
        out_specs=(vmem,) * 4 + (pl.BlockSpec(memory_space=pltpu.SMEM),),
        compiler_params=params(3),
        name="unpack_heads",
    )(all_back, after, *tables)


def body(
    q_coarse,
    k_coarse,
    v_coarse,
    cot_coarse,
    coarse_ids,
    q_fine,
    k_fine,
    v_fine,
    cot_fine,
    fine_ids,
    log_scale,
):
    heads = log_scale.shape[0]
    coarse = q_coarse.shape[1]
    rows = q_fine.shape[1]
    seq = lax.axis_size("seq")
    images = lax.axis_size("dp")
    groups = [
        [8 * (h // 2) + 2 * plane + h % 2 for h in range(heads)] for plane in range(planes)
    ]

    def exchange(parts):
        return lax.all_to_all(parts, "seq", 0, 0, axis_index_groups=groups, tiled=True)

    def to_plane(array, flip):
        return lax.ppermute(array, "seq", [(i, i ^ (2 * flip)) for i in range(seq)])

    def to_head(array, flip):
        other = 8 * (flip // 2) + flip % 2
        return lax.ppermute(array, "seq", [(i, i ^ other) for i in range(seq)])

    def to_image(array, flip):
        return lax.ppermute(array, "dp", [(i, i ^ flip) for i in range(images)])

    own_rows = exchange(run_pack(heads, fine_ids, k_fine[0], v_fine[0], q_fine[0], cot_fine[0]))
    kv_rows = to_plane(own_rows[:, : 2 * rows + note_rows], 1)
    qc_rows = to_plane(own_rows[:, 2 * rows :], 3)

    out_c, dq_c, dk_own, dv_own, scale_c, key_c, val_c = run_coarse(
        log_scale, coarse_ids[0], q_coarse[0], k_coarse[0], v_coarse[0], cot_coarse[0]
    )
    small, (od, od_send, dkv, dkv_send, scale) = run_fine(
        log_scale, own_rows, kv_rows, qc_rows, key_c, val_c, scale_c, lambda stat: to_plane(stat, 3)
    )

    small_sum = run_small(small, to_plane(small, 1), scale)
    of_image = lax.all_gather(small_sum, "seq", axis=0, axis_index_groups=groups)

    other_dkv = to_plane(dkv_send, 1)
    other_od = to_plane(od_send, 3)
    scale = scale + to_image(scale, 1) + to_image(scale, 2) + to_image(scale, 3)
    scales = [scale] + [to_head(scale, flip) for flip in range(1, heads)]
    all_parts, table = run_sum(od, other_od, dkv, other_dkv, own_rows, scales)
    table = table + to_plane(table, 1) + to_plane(table, 2) + to_plane(table, 3)
    tables = [table, to_image(table, 4)]
    all_back = exchange(all_parts)
    dk_c, dv_c, after = run_join(of_image, dk_own, dv_own, k_coarse[0])
    factor = 1.0 / math.sqrt(images * (coarse + seq * rows))
    fine_out, fine_dq, fine_dk, fine_dv, grad_scale = run_unpack(factor, all_back, after, tables)
    return (
        out_c[None],
        dq_c[None],
        dk_c[None],
        dv_c[None],
        fine_out[None],
        fine_dq[None],
        fine_dk[None],
        fine_dv[None],
        grad_scale,
    )


def solution(mesh):
    whole = P("dp", None, None)
    split = P("dp", "seq", None)
    return jax.shard_map(
        body,
        mesh=mesh,
        in_specs=(whole,) * 4 + (P("dp", None),) + (split,) * 4 + (P("dp", "seq"), P()),
        out_specs=(whole,) * 4 + (split,) * 4 + (P(),),
        check_vma=False,
    )
```
